256 devices in a mesh: space: 32 (over x, z_hi, core), sparse: 8 (over y, z_lo).
Axes of the slice: x: 4, y: 4, z: 8 (z_hi: 4, z_lo: 2; z = z_hi * 2 + z_lo), core: 2. Of those that a mesh axis runs over, the one named last changes fastest.
Arguments:
- positions: float32 [3, 8192], P(None, 'space'), may hold values from -4 to 4
- species: int32 [8192], P('space'), may hold values from 0 to 3
- live_count: int32 [32], P('space'), may hold values from 1 to 256, as said below
- neighbors: int32 [64, 8192], P(None, 'space'), may hold values from 0 to 511, as said below
- neighbor_mask: int32 [64, 8192], P(None, 'space'), may hold values from 0 to 1, as said below
- send_lo: int32 [4096], P('space'), may hold values from 0 to 255, as said below
- send_hi: int32 [4096], P('space'), may hold values from 0 to 255, as said below
- sparse_desc: bfloat16 [20480, 768], P('sparse'), may hold values from -6 to 6
- alpha: float32 [20480], P('sparse'), may hold values from -15 to 15
- var_factor: bfloat16 [20480, 128], P('sparse'), may hold values from -1.796875 to 1.796875
Outputs:
- forces: float32 [3, 8192], P(None, ('space', 'sparse'))
- energies: float32 [8192], P(('space', 'sparse'))
- variances: float32 [8192], P(('space', 'sparse'))
- virials: float32 [6, 8192], P(None, ('space', 'sparse'))
The draws below stay inside these ranges and needn't reach their ends.
Inputs may be any that keep to these rules, and one draw needn't show every extreme that they name: The atoms present in brick b are its first live_count[b] slots; some brick holds 256. `neighbors`: indices into the brick's extended list: 256 own slots, then 128 ghosts from the brick below, then 128 from the brick above; an unmasked slot of a present atom names a present own atom or a ghost that exists. `neighbor_mask`: slot 0 of every present atom is used; atoms beyond the live count use no slot. `send_lo`: entries name present atoms of the sending brick, local to it. `send_hi`: entries name present atoms of the sending brick, local to it.
All inputs are finite; a program needn't handle non-finite values.
Results may differ from the reference program's by a relative error of at most 0.025.
Values may be sent and summed in bfloat16 or wider, within the bound.
A program may use at most 128 MiB of HBM per device.

```python
import jax
import jax.numpy as jnp
from jax import lax

SPECIES = 4
RADIAL = 4
D = 768
NB = 64
A_DEV = 256
SP_DEV = 2560
R = 128
GHOST = 128
BRICKS = 32
ATOMS = 8192
SPARSE = 20480
N_SPARSE = 8


def brick_counts(key):
    key = jax.random.fold_in(key, 101)
    key_heavy, key_light, key_full = jax.random.split(key, 3)
    brick_index = jnp.arange(BRICKS, dtype=jnp.int32)
    inner_brick = (brick_index >= BRICKS // 4) & (brick_index < BRICKS - BRICKS // 4)
    heavy_count = jax.random.randint(key_heavy, (BRICKS,), A_DEV // 2, A_DEV + 1)
    light_count = jax.random.randint(key_light, (BRICKS,), 1, A_DEV // 8 + 1)
    full_brick = jax.random.randint(key_full, (), BRICKS // 4, BRICKS - BRICKS // 4)
    counts = jnp.where(inner_brick, heavy_count, light_count)
    return jnp.where(brick_index == full_brick, A_DEV, counts).astype(jnp.int32)


def draw_positions(key, part):
    key = jax.random.fold_in(key, 11)
    key_base, key_scale = jax.random.split(key)
    base = jax.random.normal(key_base, (3, ATOMS), jnp.float32)
    spread = jnp.exp(jax.random.uniform(key_scale, (ATOMS,), jnp.float32, -2.5, 0.8))
    return jnp.clip(base * spread[None, :], -4.0, 4.0).astype(jnp.float32)


def draw_live_count(key, part):
    return brick_counts(key)


def draw_neighbors(key, part):
    counts = brick_counts(key)
    key = jax.random.fold_in(key, 7)
    key_own, key_ghost, key_kind = jax.random.split(key, 3)
    brick_of = jnp.arange(ATOMS, dtype=jnp.int32) // A_DEV
    per_atom = counts[brick_of]
    own_pick = jax.random.randint(key_own, (NB, ATOMS), 0, per_atom[None, :])
    ghost_pick = jax.random.randint(key_ghost, (NB, ATOMS), 0, GHOST)
    slot_kind = jax.random.randint(key_kind, (NB, ATOMS), 0, 5)
    take_lower = (slot_kind == 3) & (brick_of > 0)[None, :]
    take_upper = (slot_kind == 4) & (brick_of < BRICKS - 1)[None, :]
    picked = jnp.where(take_lower, A_DEV + ghost_pick, jnp.where(take_upper, A_DEV + GHOST + ghost_pick, own_pick))
    return picked.astype(jnp.int32)


def draw_neighbor_mask(key, part):
    counts = brick_counts(key)
    key = jax.random.fold_in(key, 8)
    key_density, key_slots = jax.random.split(key)
    atom_index = jnp.arange(ATOMS, dtype=jnp.int32)
    present = atom_index % A_DEV < counts[atom_index // A_DEV]
    density = jax.random.randint(key_density, (ATOMS,), 1, 11)
    chosen = jax.random.randint(key_slots, (NB, ATOMS), 0, 10) < density[None, :]
    slot_zero = (jnp.arange(NB, dtype=jnp.int32) == 0)[:, None]
    return ((chosen | slot_zero) & present[None, :]).astype(jnp.int32)


def draw_send_lo(key, part):
    counts = brick_counts(key)
    key = jax.random.fold_in(key, 9)
    sender = counts[jnp.arange(BRICKS * GHOST, dtype=jnp.int32) // GHOST]
    return jax.random.randint(key, (BRICKS * GHOST,), 0, sender).astype(jnp.int32)


def draw_send_hi(key, part):
    counts = brick_counts(key)
    key = jax.random.fold_in(key, 10)
    sender = counts[jnp.arange(BRICKS * GHOST, dtype=jnp.int32) // GHOST]
    return jax.random.randint(key, (BRICKS * GHOST,), 0, sender).astype(jnp.int32)


def set_ends(entries, own_key, least, top_value):
    longest = entries.shape.index(max(entries.shape))
    spots = []
    for shift in (0, 1):
        where = [jax.random.randint(jax.random.fold_in(own_key, axis), (), 0, length) for axis, length in enumerate(entries.shape)]
        where[longest] = (where[longest] + shift) % entries.shape[longest]
        spots.append(tuple(where))
    return entries.at[spots[0]].set(least).at[spots[1]].set(top_value)


def levels(key, extent, shards, low, high):
    def one(dim, shards_of):
        steps = jax.random.uniform(jax.random.fold_in(jax.random.fold_in(key, 6), dim), (shards_of,), jnp.float32, low / len(shards), high / len(shards))
        return jnp.repeat(jnp.exp(steps), extent[dim] // shards_of).reshape((-1,) + (1,) * (len(extent) - dim - 1))

    factor_of = one(*shards[0])
    for cut in shards[1:]:
        factor_of = factor_of * one(*cut)
    return factor_of


def centred(stream_key, dims, deviation, bound, cuts=(), kind=jnp.bfloat16):
    level = levels(stream_key, dims, cuts, -0.22, 0.18) if cuts else 1.0
    values = jax.random.normal(stream_key, dims, jnp.float32) * deviation * level
    return jnp.minimum(jnp.maximum(values, -bound), bound).astype(kind)


def setup_inputs(seed: int = 0) -> dict:
    key_of = jax.random.split(jax.random.key(seed), 11)
    return {
        "positions": draw_positions(jax.random.fold_in(key_of[10], 71), 0),
        "species": set_ends(jax.random.randint(key_of[1], (ATOMS,), 0, SPECIES), jax.random.fold_in(key_of[1], 1), 0, SPECIES - 1).astype(jnp.int32),
        "live_count": draw_live_count(jax.random.fold_in(key_of[10], 71), 0),
        "neighbors": draw_neighbors(jax.random.fold_in(key_of[10], 71), 0),
        "neighbor_mask": draw_neighbor_mask(jax.random.fold_in(key_of[10], 71), 0),
        "send_lo": draw_send_lo(jax.random.fold_in(key_of[10], 71), 0),
        "send_hi": draw_send_hi(jax.random.fold_in(key_of[10], 71), 0),
        "sparse_desc": centred(key_of[7], (SPARSE, D), 1.0, 6.0, ((0, 8),)),
        "alpha": centred(key_of[8], (SPARSE,), 3.0, 15.0, ((0, 8),), jnp.float32),
        "var_factor": centred(key_of[9], (SPARSE, R), 0.3, 1.796875, ((0, 8),)),
    }


epsilon = 1e-06
VIRIAL_PAIRS = ((0, 0), (1, 1), (2, 2), (0, 1), (0, 2), (1, 2))

def rounded(values):
    return lax.optimization_barrier(values.astype(jnp.bfloat16)).astype(jnp.float32)

def channel_weights(ext_species, neighbor_rows, mask_rows, row_index, live_total, own_slots):
    species_grid = jnp.arange(SPECIES, dtype=jnp.float32)
    species_hit = (ext_species[neighbor_rows][None] == species_grid[:, None, None]).astype(jnp.float32)
    alive_other = jnp.where(neighbor_rows < own_slots, neighbor_rows < live_total, True)
    alive_self = row_index < live_total
    slot_weight = mask_rows.astype(jnp.float32) * alive_other.astype(jnp.float32) * alive_self[None, :].astype(jnp.float32)
    return species_hit * slot_weight[None]

def descriptor(offsets, weights):
    square_len = lax.optimization_barrier(jnp.sum(offsets * offsets, axis=0))
    unit_row = jnp.ones_like(square_len)[None]
    products = jnp.stack([offsets[a] * offsets[b] for a in range(3) for b in range(3)])
    angular = jnp.concatenate([unit_row, offsets, products], axis=0)
    moment_list = []
    for rate_scale in (0.1, 0.15):
        rate_list = rate_scale * 2.0 ** jnp.arange(RADIAL, dtype=jnp.float32)
        radial_part = jnp.exp(-rate_list[:, None, None] * square_len[None])
        channels = (weights[:, None] * radial_part[None]).reshape(SPECIES * RADIAL, square_len.shape[0], square_len.shape[1])
        moment_list.append(jnp.einsum('knj,anj->kaj', channels, angular))
    moment_a, moment_b = moment_list
    invariant_list = [jnp.einsum('kaj,maj->kmj', moment_a[:, start_comp:stop_comp], moment_b[:, start_comp:stop_comp]) for start_comp, stop_comp in ((0, 1), (1, 4), (4, 13))]
    raw_values = jnp.stack(invariant_list).reshape(-1, square_len.shape[1])
    return raw_values * lax.rsqrt(lax.optimization_barrier(jnp.sum(raw_values * raw_values, axis=0, keepdims=True)) + epsilon)

def kernel_block(row_block, sparse_unit, alpha, var_factor):
    projection = lax.dot_general(row_block, sparse_unit, (((1,), (1,)), ((), ())), preferred_element_type=jnp.float32)
    kernel = projection * projection
    energy_part = lax.optimization_barrier(jnp.sum(kernel * alpha[None, :], axis=1))
    coefficient = (2.0 * alpha[None, :] * projection).astype(jnp.bfloat16)
    grad_part = jnp.dot(coefficient, sparse_unit, preferred_element_type=jnp.float32)
    vector_part = jnp.dot(kernel.astype(jnp.bfloat16), var_factor, preferred_element_type=jnp.float32)
    return (grad_part, vector_part, energy_part)

def pair_sums(pair_grad, offsets, neighbor_rows, width, row_start):
    virial = -jnp.stack([offsets[a] * pair_grad[b] for a, b in VIRIAL_PAIRS])
    own_terms = jnp.concatenate([lax.optimization_barrier(jnp.sum(pair_grad, axis=1)), 0.5 * lax.optimization_barrier(jnp.sum(virial, axis=1))], axis=0)
    other_terms = jnp.concatenate([-pair_grad, 0.5 * virial], axis=0)
    total = jnp.zeros((9, width), jnp.float32)
    total = lax.dynamic_update_slice(total, own_terms, (0, row_start))
    return total.at[:, neighbor_rows.reshape(-1)].add(other_terms.reshape(9, -1))

def reference(positions, species, live_count, neighbors, neighbor_mask, send_lo, send_hi, sparse_desc, alpha, var_factor):
    own_pack = jnp.concatenate([positions, species.astype(jnp.float32)[None, :]], axis=0)
    by_brick = own_pack.reshape(4, BRICKS, A_DEV).transpose(1, 0, 2)
    send_down = send_lo.reshape(BRICKS, GHOST)
    send_up = send_hi.reshape(BRICKS, GHOST)
    picked_down = jax.vmap(lambda packed, row_list: packed[:, row_list])(by_brick, send_down)
    picked_up = jax.vmap(lambda packed, row_list: packed[:, row_list])(by_brick, send_up)
    empty_face = jnp.zeros((1, 4, GHOST), jnp.float32)
    from_below = jnp.concatenate([empty_face, picked_up[:-1]], axis=0)
    from_above = jnp.concatenate([picked_down[1:], empty_face], axis=0)
    extended = jnp.concatenate([by_brick, from_below, from_above], axis=2)
    neighbor_brick = neighbors.reshape(NB, BRICKS, A_DEV).transpose(1, 0, 2)
    mask_brick = neighbor_mask.reshape(NB, BRICKS, A_DEV).transpose(1, 0, 2)
    sparse_wide = sparse_desc.astype(jnp.float32)
    sparse_unit = (sparse_wide * lax.rsqrt(lax.optimization_barrier(jnp.sum(sparse_wide * sparse_wide, axis=1, keepdims=True)) + epsilon)).astype(jnp.bfloat16)
    unit_slices = sparse_unit.reshape(N_SPARSE, SP_DEV, D)
    alpha_slices = alpha.reshape(N_SPARSE, SP_DEV)
    factor_slices = var_factor.reshape(N_SPARSE, SP_DEV, R)

    def brick_terms(brick_items):
        extended_one, neighbor_one, mask_one, live_total = brick_items
        offsets = extended_one[:3][:, neighbor_one] - extended_one[:3, None, :A_DEV]
        weights = channel_weights(extended_one[3], neighbor_one, mask_one, jnp.arange(A_DEV, dtype=jnp.int32), live_total, A_DEV)
        unit_desc, pull_back = jax.vjp(lambda moved: descriptor(moved, weights), offsets)
        desc_rows = unit_desc.T.astype(jnp.bfloat16)

        def add_slice(carry, pieces):
            grad_part, vector_part, energy_part = kernel_block(desc_rows, pieces[0], pieces[1], pieces[2])
            return ((carry[0] + rounded(grad_part), carry[1] + rounded(vector_part), carry[2] + rounded(energy_part)), None)
        initial = (jnp.zeros((A_DEV, D), jnp.float32), jnp.zeros((A_DEV, R), jnp.float32), jnp.zeros((A_DEV,), jnp.float32))
        sums_out, _ = lax.scan(add_slice, initial, (unit_slices, alpha_slices, factor_slices))
        grad_sum, vector_sum, energy_sum = sums_out
        variance = lax.optimization_barrier(jnp.sum(vector_sum * vector_sum, axis=1))
        pair_grad = pull_back(grad_sum.T)[0]
        totals = pair_sums(pair_grad, offsets, neighbor_one, A_DEV + 2 * GHOST, 0)
        return (totals, energy_sum, variance)
    totals, energies, variances = lax.map(brick_terms, (extended, neighbor_brick, mask_brick, live_count))
    owned = totals[:, :, :A_DEV]
    lower_part = totals[:, :, A_DEV:A_DEV + GHOST]
    upper_part = totals[:, :, A_DEV + GHOST:]
    zero_face = jnp.zeros((1, 9, GHOST), jnp.float32)
    into_high = jnp.concatenate([lower_part[1:], zero_face], axis=0)
    into_low = jnp.concatenate([zero_face, upper_part[:-1]], axis=0)
    add_at = jax.vmap(lambda base_rows, row_list, extra_rows: base_rows.at[:, row_list].add(extra_rows))
    owned = add_at(owned, send_up, into_high)
    owned = add_at(owned, send_down, into_low)
    flat_rows = owned.transpose(1, 0, 2).reshape(9, ATOMS)
    return (flat_rows[:3], energies.reshape(ATOMS), variances.reshape(ATOMS), flat_rows[3:])
```

```python
import jax
import jax.numpy as jnp
from jax import lax
from jax.experimental import pallas as pl
from jax.experimental.pallas import tpu as pltpu
from jax.sharding import PartitionSpec as P

EPS = 1e-6
F32, BF16 = jnp.float32, jnp.bfloat16
SPECIES, RADIAL = 4, 4
K = SPECIES * RADIAL
LANES = 128
RATES = tuple(scale * 2.0**r for scale in (0.1, 0.15) for r in range(RADIAL))
ORDERS = ((0, 1), (1, 4), (4, 10))
FOLD = (1.0,) * 7 + (2.0,) * 3
PAIRS = ((0, 0), (1, 1), (2, 2), (0, 1), (0, 2), (1, 2))
NT = (((1,), (1,)), ((), ()))


def angular(radial, o):
    first = [radial * o[p] for p in range(3)]
    return [radial] + first + [first[a] * o[b] for a, b in PAIRS]


def along(start, size):
    return pl.ds(pl.multiple_of(start, size), size)


def norms(sparse_ref, alpha_ref, scale_ref, chunk=512):
    count, depth = sparse_ref.shape
    ones = jnp.ones((8, depth), BF16)

    def step(t, _):
        raw = sparse_ref[along(t * chunk, chunk), :]
        squares = lax.dot_general(ones, raw * raw, NT, preferred_element_type=F32)
        inverse = 1.0 / (squares + EPS)
        alpha = alpha_ref[:, along(t * chunk, chunk)]
        row = lax.broadcasted_iota(jnp.int32, inverse.shape, 0)
        scale_ref[:, along(t * chunk, chunk)] = inverse * jnp.where(row == 0, 1.0, 2.0 * alpha)
        return 0

    lax.fori_loop(0, count // chunk, step, 0)


def pair_setup(table_ref, pos_ref, nb_ref, mask_ref, live, off_ref, w_ref, sp_ref, r_ref):
    own = pos_ref.shape[1]
    tables = table_ref.shape[1] // LANES
    blocks = nb_ref.shape[0] // 8
    lane = lax.broadcasted_iota(jnp.int32, (8, LANES), 1)

    def step(i, _):
        h, b = i // blocks, i % blocks
        rows, cols = along(b * 8, 8), along(h * LANES, LANES)
        index = nb_ref[rows, cols]
        low, high = index & (LANES - 1), index // LANES
        picked = []
        for c in range(4):
            value = None
            for t in range(tables):
                source = jnp.broadcast_to(table_ref[c : c + 1, t * LANES : (t + 1) * LANES], (8, LANES))
                part = jnp.take_along_axis(source, low, axis=1, mode="promise_in_bounds")
                value = part if value is None else jnp.where(high == t, part, value)
            picked.append(value)
        o = [picked[p] - pos_ref[p : p + 1, cols] for p in range(3)]
        alive = ((index >= own) | (index < live)) & (h * LANES + lane < live)
        valid = jnp.where(alive, mask_ref[rows, cols].astype(F32), 0.0)
        for p in range(3):
            off_ref[h, p, rows, :] = o[p]
        for s in range(SPECIES):
            w_ref[h, s, rows, :] = jnp.where(picked[3] == s, valid, 0.0)
        sp_ref[h, 0, rows, :] = picked[3]
        sp_ref[h, 1, rows, :] = valid
        square = o[0] * o[0] + o[1] * o[1] + o[2] * o[2]
        for e in range(2):
            radial = jnp.exp(square * (-RATES[e * RADIAL]))
            for r in range(RADIAL):
                if r:
                    radial = radial * radial
                r_ref[h, e * RADIAL + r, rows, :] = radial
        return 0

    lax.fori_loop(0, own // LANES * blocks, step, 0)


def moments(off_ref, w_ref, r_ref, acc_ref, m_ref, mc_ref):
    halves, _, count, _ = off_ref.shape
    rates = len(RATES)

    def step(i, _):
        h, er = i // rates, i % rates
        total = [[None] * 10 for _ in range(SPECIES)]
        for b in range(count // 8):
            rows = slice(b * 8, b * 8 + 8)
            v = angular(r_ref[h, er, rows, :], [off_ref[h, p, rows, :] for p in range(3)])
            for s in range(SPECIES):
                weight = w_ref[h, s, rows, :]
                for m in range(10):
                    term = weight * v[m]
                    total[s][m] = term if b == 0 else total[s][m] + term
        e, r = er // RADIAL, er % RADIAL
        for s in range(SPECIES):
            for m in range(10):
                acc_ref[(h * 2 + e) * 10 + m, along((s * RADIAL + r) * 8, 8), :] = total[s][m]
        return 0

    lax.fori_loop(0, halves * rates, step, 0)

    def fold(i, _):
        value = acc_ref[i, pl.ds(0, K, stride=8), :]
        for j in range(1, 8):
            value = value + acc_ref[i, pl.ds(j, K, stride=8), :]
        m_ref[i] = value
        mc_ref[i] = value * jnp.where(i % 10 >= 7, 2.0, 1.0)
        return 0

    lax.fori_loop(0, halves * 20, fold, 0)


def descriptors(m_ref, mc_ref, d_ref, rinv_ref, desc_ref, eye_ref):
    halves = d_ref.shape[0]
    for h in range(halves):
        base = h * 20

        def step(k, squares):
            for l, (start, stop) in enumerate(ORDERS):
                value = None
                for m in range(start, stop):
                    term = m_ref[base + m, pl.ds(k, 1), :] * mc_ref[base + 10 + m]
                    value = term if value is None else value + term
                d_ref[h, along(l * K * K + k * K, K), :] = value
                squares = squares + value * value
            return squares

        squares = lax.fori_loop(0, K, step, jnp.zeros((K, LANES), F32), unroll=2)
        rinv = lax.rsqrt(jnp.sum(squares, axis=0, keepdims=True) + EPS)
        rinv_ref[h] = jnp.broadcast_to(rinv, (8, LANES))
        unit = (d_ref[h] * rinv).astype(BF16)
        desc_ref[h * LANES : (h + 1) * LANES, :] = lax.dot_general(
            eye_ref[:LANES, :LANES], unit, NT, preferred_element_type=F32
        ).astype(BF16)


def kernel_sums(desc_ref, sparse_ref, scale_ref, factor_ref, grad_ref, vec_ref, energy_ref, chunk=512):
    count = sparse_ref.shape[0]
    for t in range(count // chunk):
        rows = slice(t * chunk, (t + 1) * chunk)
        raw = sparse_ref[rows, :]
        projection = lax.dot_general(desc_ref[...], raw, NT, preferred_element_type=F32)
        coefficient = projection * scale_ref[1:2, rows]
        kernel = projection * projection * scale_ref[0:1, rows]
        energy_terms = coefficient * projection
        energy = energy_terms[:, :LANES]
        for j in range(1, chunk // LANES):
            energy = energy + energy_terms[:, j * LANES : (j + 1) * LANES]
        grad = jnp.dot(coefficient.astype(BF16), raw, preferred_element_type=F32)
        vec = jnp.dot(kernel.astype(BF16), factor_ref[rows, :], preferred_element_type=F32)
        if t == 0:
            grad_ref[...] = grad
            vec_ref[...] = vec
            energy_ref[...] = energy
        else:
            grad_ref[...] += grad
            vec_ref[...] += vec
            energy_ref[...] += energy


def moment_grads(grad_ref, desc_ref, eye_ref, gd_ref, gt_ref, mc_ref, rinv_ref, g_ref):
    halves = gt_ref.shape[0]
    unit = desc_ref[...].astype(F32)
    grad = grad_ref[...]
    along_unit = jnp.sum(grad * unit, axis=1, keepdims=True)
    gd_ref[...] = (grad - unit * along_unit).astype(BF16)
    for h in range(halves):
        for l in range(3):
            gt_ref[h, l] = lax.dot_general(
                eye_ref[...],
                gd_ref[h * LANES : (h + 1) * LANES, l * K * K : (l + 1) * K * K],
                NT,
                preferred_element_type=F32,
            )

    def step(i, _):
        h, e = i // 2, i % 2
        rinv = rinv_ref[h, 0:1, :]
        for l, (start, stop) in enumerate(ORDERS):
            total = [None] * 10
            for j in range(K):
                block = gt_ref[h, l, along((1 - e) * K * K + j * K, K), :]
                for m in range(start, stop):
                    term = block * mc_ref[h * 20 + (1 - e) * 10 + m, j : j + 1, :]
                    total[m] = term if j == 0 else total[m] + term
            for m in range(start, stop):
                g_ref[i * 10 + m] = total[m] * rinv
        return 0

    lax.fori_loop(0, halves * 2, step, 0)


def pair_terms(off_ref, sp_ref, r_ref, g_ref, t_ref, own_ref, group=2):
    halves, _, count, _ = off_ref.shape
    blocks = count // 8 // group
    own_ref[...] = jnp.zeros(own_ref.shape, F32)
    for h in range(halves):
        t_ref[h, 9 * count :, :] = jnp.zeros((7 * count, LANES), F32)

    def step(i, _):
        h, b = i // blocks, i % blocks
        rows = [along((b * group + q) * 8, 8) for q in range(group)]
        o = [[off_ref[h, p, rows[q], :] for p in range(3)] for q in range(group)]
        ang = [[None] + o[q] + [o[q][x] * o[q][y] for x, y in PAIRS] for q in range(group)]
        kind = [sp_ref[h, 0, rows[q], :] for q in range(group)]
        hit = [[kind[q] == s for s in range(3)] for q in range(group)]
        top = [[None] * 10 for _ in range(group)]
        slope = [None] * group
        for er, rate in enumerate(RATES):
            e, r = er // RADIAL, er % RADIAL
            radial = [r_ref[h, er, rows[q], :] for q in range(group)]
            inner = [None] * group
            for m in range(10):
                g = [g_ref[(h * 2 + e) * 10 + m, s * RADIAL + r : s * RADIAL + r + 1, :] for s in range(SPECIES)]
                for q in range(group):
                    pick = jnp.where(hit[q][0], g[0], jnp.where(hit[q][1], g[1], jnp.where(hit[q][2], g[2], g[3])))
                    if m == 0:
                        inner[q] = pick
                    else:
                        inner[q] = inner[q] + pick * ang[q][m]
                        term = radial[q] * pick
                        top[q][m] = term if er == 0 else top[q][m] + term
            for q in range(group):
                term = (radial[q] * (-rate)) * inner[q]
                slope[q] = term if er == 0 else slope[q] + term
        sums = [None] * 9
        for q in range(group):
            x, y, z = o[q]
            t = top[q]
            valid = sp_ref[h, 1, rows[q], :]
            gx = valid * (t[1] + 2.0 * x * (t[4] + slope[q]) + t[7] * y + t[8] * z)
            gy = valid * (t[2] + 2.0 * y * (t[5] + slope[q]) + t[7] * x + t[9] * z)
            gz = valid * (t[3] + 2.0 * z * (t[6] + slope[q]) + t[8] * x + t[9] * y)
            g = [gx, gy, gz]
            terms = [-v for v in g] + [-0.5 * o[q][a] * g[c] for a, c in PAIRS]
            for c in range(9):
                t_ref[h, along(c * count + (b * group + q) * 8, 8), :] = terms[c]
                sums[c] = terms[c] if q == 0 else sums[c] + terms[c]
        for c in range(9):
            own_ref[h, c * 8 : c * 8 + 8, :] += -sums[c] if c < 3 else sums[c]
        return 0

    lax.fori_loop(0, halves * blocks, step, 0)


def scatter(nb_ref, t_ref, own_ref, energy_ref, tot_ref, unroll=4):
    count, own = nb_ref.shape
    halves = own // LANES
    tables = tot_ref.shape[0] // 16
    slot = lax.broadcasted_iota(jnp.int32, (LANES, own), 0)

    def step(i, total):
        left, right = [], []
        for u in range(unroll):
            n = i * unroll + u
            index = nb_ref[pl.ds(n, 1), :]
            low, high = index & (LANES - 1), index // LANES
            terms = jnp.concatenate([t_ref[h, pl.ds(n, 16, stride=count), :] for h in range(halves)], axis=1)
            left.append(
                jnp.concatenate([jnp.where(high == t, terms, 0.0) for t in range(tables)], axis=0).astype(BF16)
            )
            right.append(jnp.where(slot == low, 1.0, 0.0).astype(BF16))
        return total + lax.dot_general(
            jnp.concatenate(left, axis=1), jnp.concatenate(right, axis=1), NT, preferred_element_type=F32
        )

    total = lax.fori_loop(0, count // unroll, step, jnp.zeros(tot_ref.shape, F32))
    energies = 0.5 * lax.dot_general(
        jnp.ones((16, LANES), F32), energy_ref[...], NT, precision=lax.Precision.HIGHEST, preferred_element_type=F32
    )
    row = lax.broadcasted_iota(jnp.int32, (16, LANES), 0)
    for h in range(halves):
        mine = own_ref[h, pl.ds(0, 16, stride=8), :]
        for j in range(1, 8):
            mine = mine + own_ref[h, pl.ds(j, 16, stride=8), :]
        mine = jnp.where(row == 9, energies[:, h * LANES : (h + 1) * LANES], mine)
        tot_ref[h * 16 : (h + 1) * 16, :] = total[h * 16 : (h + 1) * 16, :] + mine
    for t in range(halves, tables):
        tot_ref[t * 16 : (t + 1) * 16, :] = total[t * 16 : (t + 1) * 16, :]


def identities(eye_ref):
    size = K * K
    row = lax.broadcasted_iota(jnp.int32, (size, size), 0)
    col = lax.broadcasted_iota(jnp.int32, (size, size), 1)
    eye_ref[:size, :] = jnp.where(row == col, 1.0, 0.0).astype(BF16)
    eye_ref[size:, :] = jnp.where((row % K) * K + row // K == col, 1.0, 0.0).astype(BF16)


def scratch_shapes(own, count, width, sparse, depth, rank):
    halves = own // LANES
    return dict(
        off=pltpu.VMEM((halves, 3, count, LANES), F32),
        w=pltpu.VMEM((halves, SPECIES, count, LANES), F32),
        sp=pltpu.VMEM((halves, 2, count, LANES), F32),
        r=pltpu.VMEM((halves, len(RATES), count, LANES), F32),
        acc=pltpu.VMEM((halves * 20, K * 8, LANES), F32),
        m=pltpu.VMEM((halves * 20, K, LANES), F32),
        mc=pltpu.VMEM((halves * 20, K, LANES), F32),
        d=pltpu.VMEM((halves, depth, LANES), F32),
        rinv=pltpu.VMEM((halves, 8, LANES), F32),
        desc=pltpu.VMEM((own, depth), BF16),
        eye=pltpu.VMEM((2 * K * K, K * K), BF16),
        scale=pltpu.VMEM((8, sparse), F32),
        grad=pltpu.VMEM((own, depth), F32),
        energy=pltpu.VMEM((own, LANES), F32),
        gd=pltpu.VMEM((own, depth), BF16),
        gt=pltpu.VMEM((halves, 3, 2 * K * K, LANES), F32),
        g=pltpu.VMEM((halves * 20, K, LANES), F32),
        t=pltpu.VMEM((halves, 16 * count, LANES), F32),
        own=pltpu.VMEM((halves, 16 * 8, LANES), F32),
    )


MESH = pl.DeviceIdType.MESH


def here():
    return lax.axis_index("space"), lax.axis_index("sparse"), lax.axis_size("space"), lax.axis_size("sparse")


def sides():
    brick, part, bricks, _ = here()
    return lax.rem(brick + bricks - 1, bricks), lax.rem(brick + 1, bricks)


def meet(peers):
    barrier = pltpu.get_barrier_semaphore()
    for peer in peers:
        pl.semaphore_signal(barrier, inc=1, device_id=peer, device_id_type=MESH)
    pl.semaphore_wait(barrier, len(peers))


def halo_peers():
    below, above = sides()
    part = lax.axis_index("sparse")
    return [(below, part), (above, part)]


def all_peers():
    brick, part, _, parts = here()
    below, above = sides()
    others = [lax.rem(part + j, parts) for j in range(parts)]
    return [(brick, o) for o in others[1:]] + [(side, o) for side in (below, above) for o in others]


def halo_pick(pos_ref, species_ref, send_refs, table_ref, face_ref):
    own = pos_ref.shape[1]
    table_ref[0:3, :own] = pos_ref[...]
    table_ref[3:4, :own] = species_ref[...].astype(F32)
    table_ref[4:8, :own] = jnp.zeros((4, own), F32)
    for f, send_ref in enumerate(send_refs):
        index = jnp.broadcast_to(send_ref[...], (8, LANES))
        low, high = index & (LANES - 1), index // LANES
        value = None
        for t in range(own // LANES):
            part = jnp.take_along_axis(
                table_ref[:, t * LANES : (t + 1) * LANES], low, axis=1, mode="promise_in_bounds"
            )
            value = part if value is None else jnp.where(high == t, part, value)
        face_ref[f] = value


def halo_copies(face_ref, rim_ref, send_sem, recv_sem):
    return [
        pltpu.make_async_remote_copy(
            src_ref=face_ref.at[f],
            dst_ref=rim_ref.at[1 - f],
            send_sem=send_sem.at[f],
            recv_sem=recv_sem.at[1 - f],
            device_id=peer,
            device_id_type=MESH,
        )
        for f, peer in enumerate(halo_peers())
    ]


def halo_place(rim_ref, table_ref, own):
    brick, _, bricks, _ = here()
    exists = (brick > 0, brick < bricks - 1)
    for f in range(2):
        table_ref[:, own + f * LANES : own + (f + 1) * LANES] = rim_ref[f] * jnp.where(exists[f], 1.0, 0.0)


def pack_messages(tot_ref, vec_ref, msg_ref, ghost_ref):
    own = vec_ref.shape[0]
    parts = msg_ref.shape[0]
    share = own // parts
    halves = own // LANES
    for p in range(parts):
        h = p * share // LANES
        msg_ref[p, :16, :] = tot_ref[h * 16 : (h + 1) * 16, :].astype(BF16)
        msg_ref[p, 16:, :] = vec_ref[p * share : (p + 1) * share, :].astype(BF16)
    for f in range(2):
        ghost_ref[f] = tot_ref[(halves + f) * 16 : (halves + f + 1) * 16, :].astype(BF16)


def message_copies(msg_ref, ghost_ref, msg_in, ghost_in, msg_sems, ghost_sems):
    brick, part, _, parts = here()
    copies = []
    for j in range(1, parts):
        other = lax.rem(part + j, parts)
        copies.append(
            pltpu.make_async_remote_copy(
                src_ref=msg_ref.at[other],
                dst_ref=msg_in.at[j],
                send_sem=msg_sems.at[0, j],
                recv_sem=msg_sems.at[1, j],
                device_id=(brick, other),
                device_id_type=MESH,
            )
        )
    for j in range(parts):
        other = lax.rem(part + j, parts)
        for f, side in enumerate(sides()):
            copies.append(
                pltpu.make_async_remote_copy(
                    src_ref=ghost_ref.at[f],
                    dst_ref=ghost_in.at[f, j],
                    send_sem=ghost_sems.at[0, f, j],
                    recv_sem=ghost_sems.at[1, f, j],
                    device_id=(side, other),
                    device_id_type=MESH,
                )
            )
    return copies


def finish(msg_ref, msg_in, ghost_in, send_refs, force_ref, energy_out, variance_ref, virial_ref):
    brick, part, bricks, parts = here()
    share = msg_ref.shape[1] - 16
    total = msg_ref[part].astype(F32)
    for j in range(1, parts):
        total = total + msg_in[j].astype(F32)
    mine, vec = total[:16], total[16:]
    half = part * share // LANES
    slot = half * LANES + lax.broadcasted_iota(jnp.int32, (LANES, LANES), 0)
    exists = (brick < bricks - 1, brick > 0)
    for f in range(2):
        ghosts = ghost_in[f, 0].astype(F32)
        for j in range(1, parts):
            ghosts = ghosts + ghost_in[f, j].astype(F32)
        ghosts = jnp.where(exists[f], ghosts, 0.0)
        hits = jnp.where(slot == send_refs[1 - f][...], 1.0, 0.0)
        high = ghosts.astype(BF16)
        low = (ghosts - high.astype(F32)).astype(BF16)
        both = lax.dot_general(
            jnp.concatenate([high, low], axis=0), hits.astype(BF16), NT, preferred_element_type=F32
        )
        row = lax.broadcasted_iota(jnp.int32, (16, LANES), 0)
        mine = mine + jnp.where(row < 9, both[:16] + both[16:], 0.0)
    shift = lax.rem(LANES - lax.rem(part * share, LANES), LANES)
    mine = pltpu.roll(mine, shift, 1)[:, :share]
    force_ref[...] = mine[0:3]
    virial_ref[...] = mine[3:9]
    energy_out[...] = mine[9:10]
    squares = lax.dot_general(
        jnp.ones((8, vec.shape[1]), F32), vec * vec, NT, precision=lax.Precision.HIGHEST, preferred_element_type=F32
    )
    variance_ref[...] = squares[0:1]

VM = pl.BlockSpec(memory_space=pltpu.VMEM)


def halo(pos, species, send_lo, send_hi):
    own = pos.shape[1]

    def kernel(pos_ref, species_ref, lo_ref, hi_ref, table_ref, face_ref, rim_ref, send_sem, recv_sem):
        halo_pick(pos_ref, species_ref, (lo_ref, hi_ref), table_ref, face_ref)
        meet(halo_peers())
        copies = halo_copies(face_ref, rim_ref, send_sem, recv_sem)
        for copy in copies:
            copy.start()
        for copy in copies:
            copy.wait()
        halo_place(rim_ref, table_ref, own)

    return pl.pallas_call(
        kernel,
        out_shape=jax.ShapeDtypeStruct((8, own + 2 * LANES), F32),
        in_specs=[VM] * 4,
        out_specs=VM,
        scratch_shapes=[
            pltpu.VMEM((2, 8, LANES), F32),
            pltpu.VMEM((2, 8, LANES), F32),
            pltpu.SemaphoreType.DMA((2,)),
            pltpu.SemaphoreType.DMA((2,)),
        ],
        compiler_params=pltpu.CompilerParams(collective_id=0, has_side_effects=True),
        name="halo",
    )(pos, species, send_lo, send_hi)


def brick(pos, nb, mask, live, table, sparse, alpha, factor):
    own, count, width = pos.shape[1], nb.shape[0], table.shape[1]
    names = scratch_shapes(own, count, width, sparse.shape[0], sparse.shape[1], factor.shape[1])
    keys = list(names)

    def kernel(
        live_ref, pos_ref, nb_ref, mask_ref, table_ref, sparse_ref, alpha_ref, factor_ref, tot_ref, vec_ref, *scratch
    ):
        s = dict(zip(keys, scratch))
        identities(s["eye"])
        norms(sparse_ref, alpha_ref, s["scale"])
        pair_setup(table_ref, pos_ref, nb_ref, mask_ref, live_ref[0], s["off"], s["w"], s["sp"], s["r"])
        moments(s["off"], s["w"], s["r"], s["acc"], s["m"], s["mc"])
        descriptors(s["m"], s["mc"], s["d"], s["rinv"], s["desc"], s["eye"])
        kernel_sums(s["desc"], sparse_ref, s["scale"], factor_ref, s["grad"], vec_ref, s["energy"])
        moment_grads(s["grad"], s["desc"], s["eye"], s["gd"], s["gt"], s["mc"], s["rinv"], s["g"])
        pair_terms(s["off"], s["sp"], s["r"], s["g"], s["t"], s["own"])
        scatter(nb_ref, s["t"], s["own"], s["energy"], tot_ref)

    return pl.pallas_call(
        kernel,
        out_shape=(
            jax.ShapeDtypeStruct((width // LANES * 16, LANES), F32),
            jax.ShapeDtypeStruct((own, factor.shape[1]), F32),
        ),
        in_specs=[pl.BlockSpec(memory_space=pltpu.SMEM)] + [VM] * 7,
        out_specs=(VM, VM),
        scratch_shapes=list(names.values()),
        compiler_params=pltpu.CompilerParams(vmem_limit_bytes=60 * 1024 * 1024),
        name="brick",
    )(live, pos, nb, mask, table, sparse, alpha, factor)


def exchange(tot, vec, send_lo, send_hi, parts):
    own, rank = vec.shape
    share = own // parts
    slots = lambda *lead: pltpu.VMEM((*lead, 16 + share, rank), BF16)
    faces = lambda *lead: pltpu.VMEM((*lead, 16, LANES), BF16)

    def kernel(
        tot_ref, vec_ref, lo_ref, hi_ref, force_ref, energy_ref, variance_ref, virial_ref, msg, ghost, msg_in, ghost_in, msg_sems, ghost_sems
    ):
        pack_messages(tot_ref, vec_ref, msg, ghost)
        meet(all_peers())
        copies = message_copies(msg, ghost, msg_in, ghost_in, msg_sems, ghost_sems)
        for copy in copies:
            copy.start()
        for copy in copies:
            copy.wait()
        finish(msg, msg_in, ghost_in, (lo_ref, hi_ref), force_ref, energy_ref, variance_ref, virial_ref)

    return pl.pallas_call(
        kernel,
        out_shape=tuple(jax.ShapeDtypeStruct((n, share), F32) for n in (3, 1, 1, 6)),
        in_specs=[VM] * 4,
        out_specs=(VM,) * 4,
        scratch_shapes=[
            slots(parts),
            faces(2),
            slots(parts),
            faces(2, parts),
            pltpu.SemaphoreType.DMA((2, parts)),
            pltpu.SemaphoreType.DMA((2, 2, parts)),
        ],
        compiler_params=pltpu.CompilerParams(collective_id=1, has_side_effects=True),
        name="exchange",
    )(tot, vec, send_lo, send_hi)


def shards(
    positions, species, live_count, neighbors, neighbor_mask, send_lo, send_hi, sparse_desc, alpha, var_factor
):
    lo, hi = send_lo[None], send_hi[None]
    table = halo(positions, species[None], lo, hi)
    tot, vec = brick(positions, neighbors, neighbor_mask, live_count, table, sparse_desc, alpha[None], var_factor)
    forces, energies, variances, virials = exchange(tot, vec, lo, hi, lax.axis_size("sparse"))
    return forces, energies[0], variances[0], virials


def solution(mesh):
    return jax.shard_map(
        shards,
        mesh=mesh,
        in_specs=(
            P(None, "space"),
            P("space"),
            P("space"),
            P(None, "space"),
            P(None, "space"),
            P("space"),
            P("space"),
            P("sparse", None),
            P("sparse"),
            P("sparse", None),
        ),
        out_specs=(
            P(None, ("space", "sparse")),
            P(("space", "sparse")),
            P(("space", "sparse")),
            P(None, ("space", "sparse")),
        ),
        check_vma=False,
    )
```

```python
import jax
import jax.numpy as jnp
from jax import lax
from jax.experimental import pallas as pl
from jax.experimental.pallas import tpu as pltpu
from jax.sharding import PartitionSpec as P

EPS = 1e-6
F32, BF16 = jnp.float32, jnp.bfloat16
SPECIES, RADIAL = 4, 4
K = SPECIES * RADIAL
LANES = 128
RATES = tuple(scale * 2.0**r for scale in (0.1, 0.15) for r in range(RADIAL))
ORDERS = ((0, 1), (1, 4), (4, 10))
FOLD = (1.0,) * 7 + (2.0,) * 3
PAIRS = ((0, 0), (1, 1), (2, 2), (0, 1), (0, 2), (1, 2))
NT = (((1,), (1,)), ((), ()))


def angular(radial, o):
    first = [radial * o[p] for p in range(3)]
    return [radial] + first + [first[a] * o[b] for a, b in PAIRS]


def along(start, size):
    return pl.ds(pl.multiple_of(start, size), size)


def norms(sparse_ref, alpha_ref, scale_ref, first, last, chunk=512):
    depth = sparse_ref.shape[1]
    ones = jnp.ones((8, depth), BF16)
    row = lax.broadcasted_iota(jnp.int32, (8, chunk), 0)
    for t in range(first, last):
        raw = sparse_ref[t * chunk : (t + 1) * chunk, :]
        squares = lax.dot_general(ones, raw * raw, NT, preferred_element_type=F32)
        inverse = 1.0 / (squares + EPS)
        per = chunk // LANES
        alpha = jnp.concatenate([alpha_ref[t * per + j : t * per + j + 1, :] for j in range(per)], axis=1)
        scale_ref[:, t * chunk : (t + 1) * chunk] = inverse * jnp.where(row == 0, 1.0, 2.0 * alpha)


def pair_setup(table_ref, pos_ref, nb_ref, mask_ref, live, off_ref, w_ref, sp_ref, r_ref):
    own = pos_ref.shape[1]
    tables = table_ref.shape[1] // LANES
    blocks = nb_ref.shape[0] // 8
    lane = lax.broadcasted_iota(jnp.int32, (8, LANES), 1)

    def step(i, _):
        h, b = i // blocks, i % blocks
        rows, cols = along(b * 8, 8), along(h * LANES, LANES)
        index = nb_ref[rows, cols]
        low, high = index & (LANES - 1), index // LANES
        picked = []
        for c in range(4):
            value = None
            for t in range(tables):
                source = jnp.broadcast_to(table_ref[c : c + 1, t * LANES : (t + 1) * LANES], (8, LANES))
                part = jnp.take_along_axis(source, low, axis=1, mode="promise_in_bounds")
                value = part if value is None else jnp.where(high == t, part, value)
            picked.append(value)
        o = [picked[p] - pos_ref[p : p + 1, cols] for p in range(3)]
        alive = ((index >= own) | (index < live)) & (h * LANES + lane < live)
        valid = jnp.where(alive, mask_ref[rows, cols].astype(F32), 0.0)
        for p in range(3):
            off_ref[h, p, rows, :] = o[p]
        for s in range(SPECIES):
            w_ref[h, s, rows, :] = jnp.where(picked[3] == s, valid, 0.0)
        sp_ref[h, 0, rows, :] = picked[3]
        sp_ref[h, 1, rows, :] = valid
        square = o[0] * o[0] + o[1] * o[1] + o[2] * o[2]
        for e in range(2):
            radial = jnp.exp(square * (-RATES[e * RADIAL]))
            for r in range(RADIAL):
                if r:
                    radial = radial * radial
                r_ref[h, e * RADIAL + r, rows, :] = radial
        return 0

    lax.fori_loop(0, own // LANES * blocks, step, 0)


def moments(off_ref, w_ref, r_ref, acc_ref, m_ref, mc_ref):
    halves, _, count, _ = off_ref.shape
    rates = len(RATES)

    def step(i, _):
        h, er = i // rates, i % rates
        total = [[None] * 10 for _ in range(SPECIES)]
        for b in range(count // 8):
            rows = slice(b * 8, b * 8 + 8)
            v = angular(r_ref[h, er, rows, :], [off_ref[h, p, rows, :] for p in range(3)])
            for s in range(SPECIES):
                weight = w_ref[h, s, rows, :]
                for m in range(10):
                    term = weight * v[m]
                    total[s][m] = term if b == 0 else total[s][m] + term
        e, r = er // RADIAL, er % RADIAL
        for s in range(SPECIES):
            for m in range(10):
                acc_ref[(h * 2 + e) * 10 + m, along((s * RADIAL + r) * 8, 8), :] = total[s][m]
        return 0

    lax.fori_loop(0, halves * rates, step, 0)

    def fold(i, _):
        value = acc_ref[i, pl.ds(0, K, stride=8), :]
        for j in range(1, 8):
            value = value + acc_ref[i, pl.ds(j, K, stride=8), :]
        m_ref[i] = value
        mc_ref[i] = value * jnp.where(i % 10 >= 7, 2.0, 1.0)
        return 0

    lax.fori_loop(0, halves * 20, fold, 0)


def descriptors(m_ref, mc_ref, d_ref, rinv_ref, desc_ref, eye_ref):
    halves = d_ref.shape[0]
    for h in range(halves):
        base = h * 20

        def step(k, squares):
            for l, (start, stop) in enumerate(ORDERS):
                value = None
                for m in range(start, stop):
                    term = m_ref[base + m, pl.ds(k, 1), :] * mc_ref[base + 10 + m]
                    value = term if value is None else value + term
                d_ref[h, along(l * K * K + k * K, K), :] = value
                squares = squares + value * value
            return squares

        squares = lax.fori_loop(0, K, step, jnp.zeros((K, LANES), F32), unroll=2)
        rinv = lax.rsqrt(jnp.sum(squares, axis=0, keepdims=True) + EPS)
        rinv_ref[h] = jnp.broadcast_to(rinv, (8, LANES))
        unit = (d_ref[h] * rinv).astype(BF16)
        desc_ref[h * LANES : (h + 1) * LANES, :] = lax.dot_general(
            eye_ref[:LANES, :LANES], unit, NT, preferred_element_type=F32
        ).astype(BF16)


def kernel_sums(desc_ref, sparse_ref, scale_ref, factor_ref, grad_ref, vec_ref, energy_ref, chunk=512):
    count = sparse_ref.shape[0]
    for t in range(count // chunk):
        rows = slice(t * chunk, (t + 1) * chunk)
        raw = sparse_ref[rows, :]
        projection = lax.dot_general(desc_ref[...], raw, NT, preferred_element_type=F32)
        coefficient = projection * scale_ref[1:2, rows]
        kernel = projection * projection * scale_ref[0:1, rows]
        energy_terms = coefficient * projection
        energy = energy_terms[:, :LANES]
        for j in range(1, chunk // LANES):
            energy = energy + energy_terms[:, j * LANES : (j + 1) * LANES]
        grad = jnp.dot(coefficient.astype(BF16), raw, preferred_element_type=F32)
        vec = jnp.dot(kernel.astype(BF16), factor_ref[rows, :], preferred_element_type=F32)
        if t == 0:
            grad_ref[...] = grad
            vec_ref[...] = vec
            energy_ref[...] = energy
        else:
            grad_ref[...] += grad
            vec_ref[...] += vec
            energy_ref[...] += energy


def moment_grads(grad_ref, desc_ref, eye_ref, gd_ref, gt_ref, mc_ref, rinv_ref, g_ref):
    halves = gt_ref.shape[0]
    unit = desc_ref[...].astype(F32)
    grad = grad_ref[...]
    along_unit = jnp.sum(grad * unit, axis=1, keepdims=True)
    gd_ref[...] = (grad - unit * along_unit).astype(BF16)
    for h in range(halves):
        for l in range(3):
            gt_ref[h, l] = lax.dot_general(
                eye_ref[...],
                gd_ref[h * LANES : (h + 1) * LANES, l * K * K : (l + 1) * K * K],
                NT,
                preferred_element_type=F32,
            )

    def step(i, _):
        h, e = i // 2, i % 2
        rinv = rinv_ref[h, 0:1, :]
        for l, (start, stop) in enumerate(ORDERS):
            total = [None] * 10
            for j in range(K):
                block = gt_ref[h, l, along((1 - e) * K * K + j * K, K), :]
                for m in range(start, stop):
                    term = block * mc_ref[h * 20 + (1 - e) * 10 + m, j : j + 1, :]
                    total[m] = term if j == 0 else total[m] + term
            for m in range(start, stop):
                g_ref[i * 10 + m] = total[m] * rinv
        return 0

    lax.fori_loop(0, halves * 2, step, 0)


def pair_terms(off_ref, sp_ref, r_ref, g_ref, t_ref, own_ref, group=2):
    halves, _, count, _ = off_ref.shape
    blocks = count // 8 // group
    own_ref[...] = jnp.zeros(own_ref.shape, F32)
    for h in range(halves):
        t_ref[h, 9 * count :, :] = jnp.zeros((7 * count, LANES), F32)

    def step(i, _):
        h, b = i // blocks, i % blocks
        rows = [along((b * group + q) * 8, 8) for q in range(group)]
        o = [[off_ref[h, p, rows[q], :] for p in range(3)] for q in range(group)]
        ang = [[None] + o[q] + [o[q][x] * o[q][y] for x, y in PAIRS] for q in range(group)]
        kind = [sp_ref[h, 0, rows[q], :] for q in range(group)]
        hit = [[kind[q] == s for s in range(3)] for q in range(group)]
        top = [[None] * 10 for _ in range(group)]
        slope = [None] * group
        for er, rate in enumerate(RATES):
            e, r = er // RADIAL, er % RADIAL
            radial = [r_ref[h, er, rows[q], :] for q in range(group)]
            inner = [None] * group
            for m in range(10):
                g = [g_ref[(h * 2 + e) * 10 + m, s * RADIAL + r : s * RADIAL + r + 1, :] for s in range(SPECIES)]
                for q in range(group):
                    pick = jnp.where(hit[q][0], g[0], jnp.where(hit[q][1], g[1], jnp.where(hit[q][2], g[2], g[3])))
                    if m == 0:
                        inner[q] = pick
                    else:
                        inner[q] = inner[q] + pick * ang[q][m]
                        term = radial[q] * pick
                        top[q][m] = term if er == 0 else top[q][m] + term
            for q in range(group):
                term = (radial[q] * (-rate)) * inner[q]
                slope[q] = term if er == 0 else slope[q] + term
        sums = [None] * 9
        for q in range(group):
            x, y, z = o[q]
            t = top[q]
            valid = sp_ref[h, 1, rows[q], :]
            gx = valid * (t[1] + 2.0 * x * (t[4] + slope[q]) + t[7] * y + t[8] * z)
            gy = valid * (t[2] + 2.0 * y * (t[5] + slope[q]) + t[7] * x + t[9] * z)
            gz = valid * (t[3] + 2.0 * z * (t[6] + slope[q]) + t[8] * x + t[9] * y)
            g = [gx, gy, gz]
            terms = [-v for v in g] + [-0.5 * o[q][a] * g[c] for a, c in PAIRS]
            for c in range(9):
                t_ref[h, along(c * count + (b * group + q) * 8, 8), :] = terms[c]
                sums[c] = terms[c] if q == 0 else sums[c] + terms[c]
        for c in range(9):
            own_ref[h, c * 8 : c * 8 + 8, :] += -sums[c] if c < 3 else sums[c]
        return 0

    lax.fori_loop(0, halves * blocks, step, 0)


def scatter(nb_ref, t_ref, own_ref, energy_ref, tot_ref, unroll=4):
    count, own = nb_ref.shape
    halves = own // LANES
    tables = tot_ref.shape[0] // 16
    slot = lax.broadcasted_iota(jnp.int32, (LANES, own), 0)

    def step(i, total):
        left, right = [], []
        for u in range(unroll):
            n = i * unroll + u
            index = nb_ref[pl.ds(n, 1), :]
            low, high = index & (LANES - 1), index // LANES
            terms = jnp.concatenate([t_ref[h, pl.ds(n, 16, stride=count), :] for h in range(halves)], axis=1)
            left.append(
                jnp.concatenate([jnp.where(high == t, terms, 0.0) for t in range(tables)], axis=0).astype(BF16)
            )
            right.append(jnp.where(slot == low, 1.0, 0.0).astype(BF16))
        return total + lax.dot_general(
            jnp.concatenate(left, axis=1), jnp.concatenate(right, axis=1), NT, preferred_element_type=F32
        )

    total = lax.fori_loop(0, count // unroll, step, jnp.zeros(tot_ref.shape, F32))
    energies = 0.5 * lax.dot_general(
        jnp.ones((16, LANES), F32), energy_ref[...], NT, precision=lax.Precision.HIGHEST, preferred_element_type=F32
    )
    row = lax.broadcasted_iota(jnp.int32, (16, LANES), 0)
    for h in range(halves):
        mine = own_ref[h, pl.ds(0, 16, stride=8), :]
        for j in range(1, 8):
            mine = mine + own_ref[h, pl.ds(j, 16, stride=8), :]
        mine = jnp.where(row == 9, energies[:, h * LANES : (h + 1) * LANES], mine)
        tot_ref[h * 16 : (h + 1) * 16, :] = total[h * 16 : (h + 1) * 16, :] + mine
    for t in range(halves, tables):
        tot_ref[t * 16 : (t + 1) * 16, :] = total[t * 16 : (t + 1) * 16, :]


def identities(eye_ref):
    size = K * K
    row = lax.broadcasted_iota(jnp.int32, (size, size), 0)
    col = lax.broadcasted_iota(jnp.int32, (size, size), 1)
    eye_ref[:size, :] = jnp.where(row == col, 1.0, 0.0).astype(BF16)
    eye_ref[size:, :] = jnp.where((row % K) * K + row // K == col, 1.0, 0.0).astype(BF16)


def scratch_shapes(own, count, width, sparse, depth, rank):
    halves = own // LANES
    return dict(
        off=pltpu.VMEM((halves, 3, count, LANES), F32),
        w=pltpu.VMEM((halves, SPECIES, count, LANES), F32),
        sp=pltpu.VMEM((halves, 2, count, LANES), F32),
        r=pltpu.VMEM((halves, len(RATES), count, LANES), F32),
        acc=pltpu.VMEM((halves * 20, K * 8, LANES), F32),
        m=pltpu.VMEM((halves * 20, K, LANES), F32),
        mc=pltpu.VMEM((halves * 20, K, LANES), F32),
        d=pltpu.VMEM((halves, depth, LANES), F32),
        rinv=pltpu.VMEM((halves, 8, LANES), F32),
        desc=pltpu.VMEM((own, depth), BF16),
        eye=pltpu.VMEM((2 * K * K, K * K), BF16),
        scale=pltpu.VMEM((8, sparse), F32),
        grad=pltpu.VMEM((own, depth), F32),
        energy=pltpu.VMEM((own, LANES), F32),
        gd=pltpu.VMEM((own, depth), BF16),
        gt=pltpu.VMEM((halves, 3, 2 * K * K, LANES), F32),
        g=pltpu.VMEM((halves * 20, K, LANES), F32),
        t=pltpu.VMEM((halves, 16 * count, LANES), F32),
        own=pltpu.VMEM((halves, 16 * 8, LANES), F32),
    )


MESH = pl.DeviceIdType.MESH


def here():
    return lax.axis_index("space"), lax.axis_index("sparse"), lax.axis_size("space"), lax.axis_size("sparse")


def sides():
    brick, part, bricks, _ = here()
    return lax.rem(brick + bricks - 1, bricks), lax.rem(brick + 1, bricks)


def halo_peers():
    below, above = sides()
    part = lax.axis_index("sparse")
    return [(below, part), (above, part)]


def all_peers():
    brick, part, _, parts = here()
    below, above = sides()
    others = [lax.rem(part + j, parts) for j in range(parts)]
    return [(brick, o) for o in others[1:]] + [(side, o) for side in (below, above) for o in others]


def halo_pick(pos_ref, species_ref, send_refs, table_ref, face_ref):
    own = pos_ref.shape[1]
    table_ref[0:3, :own] = pos_ref[...]
    table_ref[3:4, :own] = species_ref[...].astype(F32)
    table_ref[4:8, :own] = jnp.zeros((4, own), F32)
    for f, send_ref in enumerate(send_refs):
        index = jnp.broadcast_to(send_ref[...], (8, LANES))
        low, high = index & (LANES - 1), index // LANES
        value = None
        for t in range(own // LANES):
            part = jnp.take_along_axis(
                table_ref[:, t * LANES : (t + 1) * LANES], low, axis=1, mode="promise_in_bounds"
            )
            value = part if value is None else jnp.where(high == t, part, value)
        face_ref[f] = value


def halo_copies(face_ref, rim_ref, send_sem, recv_sem):
    return [
        pltpu.make_async_remote_copy(
            src_ref=face_ref.at[f],
            dst_ref=rim_ref.at[1 - f],
            send_sem=send_sem.at[f],
            recv_sem=recv_sem.at[1 - f],
            device_id=peer,
            device_id_type=MESH,
        )
        for f, peer in enumerate(halo_peers())
    ]


def halo_place(rim_ref, table_ref, own):
    brick, _, bricks, _ = here()
    exists = (brick > 0, brick < bricks - 1)
    for f in range(2):
        table_ref[:, own + f * LANES : own + (f + 1) * LANES] = rim_ref[f] * jnp.where(exists[f], 1.0, 0.0)


def pack_messages(tot_ref, vec_ref, msg_ref, ghost_ref):
    own = vec_ref.shape[0]
    parts = msg_ref.shape[0]
    share = own // parts
    halves = own // LANES
    for p in range(parts):
        h = p * share // LANES
        msg_ref[p, :16, :] = tot_ref[h * 16 : (h + 1) * 16, :].astype(BF16)
        msg_ref[p, 16:, :] = vec_ref[p * share : (p + 1) * share, :].astype(BF16)
    for f in range(2):
        ghost_ref[f] = tot_ref[(halves + f) * 16 : (halves + f + 1) * 16, :].astype(BF16)


def message_copies(msg_ref, ghost_ref, msg_in, ghost_in, msg_sems, ghost_sems):
    brick, part, _, parts = here()
    copies = []
    for j in range(1, parts):
        other = lax.rem(part + j, parts)
        copies.append(
            pltpu.make_async_remote_copy(
                src_ref=msg_ref.at[other],
                dst_ref=msg_in.at[j],
                send_sem=msg_sems.at[0, j],
                recv_sem=msg_sems.at[1, j],
                device_id=(brick, other),
                device_id_type=MESH,
            )
        )
    for j in range(parts):
        other = lax.rem(part + j, parts)
        for f, side in enumerate(sides()):
            copies.append(
                pltpu.make_async_remote_copy(
                    src_ref=ghost_ref.at[f],
                    dst_ref=ghost_in.at[f, j],
                    send_sem=ghost_sems.at[0, f, j],
                    recv_sem=ghost_sems.at[1, f, j],
                    device_id=(side, other),
                    device_id_type=MESH,
                )
            )
    return copies


def finish(msg_ref, msg_in, ghost_in, send_refs, out_ref):
    brick, part, bricks, parts = here()
    share = msg_ref.shape[1] - 16
    total = msg_ref[part].astype(F32)
    for j in range(1, parts):
        total = total + msg_in[j].astype(F32)
    mine, vec = total[:16], total[16:]
    half = part * share // LANES
    slot = half * LANES + lax.broadcasted_iota(jnp.int32, (LANES, LANES), 0)
    exists = (brick < bricks - 1, brick > 0)
    for f in range(2):
        ghosts = ghost_in[f, 0].astype(F32)
        for j in range(1, parts):
            ghosts = ghosts + ghost_in[f, j].astype(F32)
        ghosts = jnp.where(exists[f], ghosts, 0.0)
        hits = jnp.where(slot == send_refs[1 - f][...], 1.0, 0.0)
        high = ghosts.astype(BF16)
        low = (ghosts - high.astype(F32)).astype(BF16)
        both = lax.dot_general(
            jnp.concatenate([high, low], axis=0), hits.astype(BF16), NT, preferred_element_type=F32
        )
        row = lax.broadcasted_iota(jnp.int32, (16, LANES), 0)
        mine = mine + jnp.where(row < 9, both[:16] + both[16:], 0.0)
    shift = lax.rem(LANES - lax.rem(part * share, LANES), LANES)
    mine = pltpu.roll(mine, shift, 1)
    squares = lax.dot_general(
        jnp.ones((16, vec.shape[1]), F32), vec * vec, NT, precision=lax.Precision.HIGHEST, preferred_element_type=F32
    )
    out_ref[...] = mine
    out_ref[10:11, :share] = squares[10:11]

VM = pl.BlockSpec(memory_space=pltpu.VMEM)
HBM = pl.BlockSpec(memory_space=pl.ANY)


def brick(pos, species, live, nb, mask, send_lo, send_hi, sparse, alpha, factor, parts):
    own, count = pos.shape[1], nb.shape[0]
    depth, rank = sparse.shape[1], factor.shape[1]
    tables = own // LANES + 2
    share = own // parts
    names = scratch_shapes(own, count, tables * LANES, sparse.shape[0], depth, rank)
    names.update(
        table=pltpu.VMEM((8, tables * LANES), F32),
        face=pltpu.VMEM((2, 8, LANES), F32),
        rim=pltpu.VMEM((2, 8, LANES), F32),
        sparse=pltpu.VMEM(sparse.shape, BF16),
        factor=pltpu.VMEM(factor.shape, BF16),
        vec=pltpu.VMEM((own, rank), F32),
        tot=pltpu.VMEM((tables * 16, LANES), F32),
        msg=pltpu.VMEM((parts, 16 + share, rank), BF16),
        msg_in=pltpu.VMEM((parts, 16 + share, rank), BF16),
        ghost=pltpu.VMEM((2, 16, LANES), BF16),
        ghost_in=pltpu.VMEM((2, parts, 16, LANES), BF16),
        halo_send=pltpu.SemaphoreType.DMA((2,)),
        halo_recv=pltpu.SemaphoreType.DMA((2,)),
        msg_sems=pltpu.SemaphoreType.DMA((2, parts)),
        ghost_sems=pltpu.SemaphoreType.DMA((2, 2, parts)),
        load_sems=pltpu.SemaphoreType.DMA((2,)),
    )
    keys = list(names)

    def kernel(
        live_ref, pos_ref, species_ref, nb_ref, mask_ref, lo_ref, hi_ref, alpha_ref, sparse_hbm, factor_hbm, out_ref, *scratch
    ):
        s = dict(zip(keys, scratch))
        peers = all_peers()
        barrier = pltpu.get_barrier_semaphore()
        for peer in peers:
            pl.semaphore_signal(barrier, inc=1, device_id=peer, device_id_type=MESH)
        loads = [
            pltpu.make_async_copy(sparse_hbm, s["sparse"], s["load_sems"].at[0]),
            pltpu.make_async_copy(factor_hbm, s["factor"], s["load_sems"].at[1]),
        ]
        for load in loads:
            load.start()
        halo_pick(pos_ref, species_ref, (lo_ref, hi_ref), s["table"], s["face"])
        identities(s["eye"])
        for load in loads:
            load.wait()
        norms(s["sparse"], alpha_ref, s["scale"], 0, 2)
        pl.semaphore_wait(barrier, len(peers))
        halos = halo_copies(s["face"], s["rim"], s["halo_send"], s["halo_recv"])
        for copy in halos:
            copy.start()
        norms(s["sparse"], alpha_ref, s["scale"], 2, sparse.shape[0] // 512)
        for copy in halos:
            copy.wait()
        halo_place(s["rim"], s["table"], own)
        pair_setup(s["table"], pos_ref, nb_ref, mask_ref, live_ref[0], s["off"], s["w"], s["sp"], s["r"])
        moments(s["off"], s["w"], s["r"], s["acc"], s["m"], s["mc"])
        descriptors(s["m"], s["mc"], s["d"], s["rinv"], s["desc"], s["eye"])
        kernel_sums(s["desc"], s["sparse"], s["scale"], s["factor"], s["grad"], s["vec"], s["energy"])
        moment_grads(s["grad"], s["desc"], s["eye"], s["gd"], s["gt"], s["mc"], s["rinv"], s["g"])
        pair_terms(s["off"], s["sp"], s["r"], s["g"], s["t"], s["own"])
        scatter(nb_ref, s["t"], s["own"], s["energy"], s["tot"])
        pack_messages(s["tot"], s["vec"], s["msg"], s["ghost"])
        copies = message_copies(s["msg"], s["ghost"], s["msg_in"], s["ghost_in"], s["msg_sems"], s["ghost_sems"])
        for copy in copies:
            copy.start()
        for copy in copies:
            copy.wait()
        finish(s["msg"], s["msg_in"], s["ghost_in"], (lo_ref, hi_ref), out_ref)

    return pl.pallas_call(
        kernel,
        out_shape=jax.ShapeDtypeStruct((16, LANES), F32),
        in_specs=[pl.BlockSpec(memory_space=pltpu.SMEM)] + [VM] * 7 + [HBM] * 2,
        out_specs=VM,
        scratch_shapes=list(names.values()),
        compiler_params=pltpu.CompilerParams(
            vmem_limit_bytes=60 * 1024 * 1024, collective_id=0, has_side_effects=True
        ),
        name="brick",
    )(live, pos, species, nb, mask, send_lo, send_hi, alpha, sparse, factor)


def split(result, share):
    def kernel(result_ref, force_ref, energy_ref, variance_ref, virial_ref):
        force_ref[...] = result_ref[0:3, :share]
        virial_ref[...] = result_ref[3:9, :share]
        energy_ref[...] = result_ref[9:10, :share]
        variance_ref[...] = result_ref[10:11, :share]

    return pl.pallas_call(
        kernel,
        out_shape=tuple(jax.ShapeDtypeStruct((n, share), F32) for n in (3, 1, 1, 6)),
        in_specs=[VM],
        out_specs=(VM,) * 4,
        name="split",
    )(result)


def shards(
    positions, species, live_count, neighbors, neighbor_mask, send_lo, send_hi, sparse_desc, alpha, var_factor
):
    parts = lax.axis_size("sparse")
    result = brick(
        positions,
        species[None],
        live_count,
        neighbors,
        neighbor_mask,
        send_lo[None],
        send_hi[None],
        sparse_desc,
        alpha.reshape(-1, LANES),
        var_factor,
        parts,
    )
    forces, energies, variances, virials = split(result, positions.shape[1] // parts)
    return forces, energies[0], variances[0], virials


def solution(mesh):
    return jax.shard_map(
        shards,
        mesh=mesh,
        in_specs=(
            P(None, "space"),
            P("space"),
            P("space"),
            P(None, "space"),
            P(None, "space"),
            P("space"),
            P("space"),
            P("sparse", None),
            P("sparse"),
            P("sparse", None),
        ),
        out_specs=(
            P(None, ("space", "sparse")),
            P(("space", "sparse")),
            P(("space", "sparse")),
            P(None, ("space", "sparse")),
        ),
        check_vma=False,
    )
```

```python
import jax
import jax.numpy as jnp
from jax import lax
from jax.experimental import pallas as pl
from jax.experimental.pallas import tpu as pltpu
from jax.sharding import PartitionSpec as P

EPS = 1e-6
F32, BF16 = jnp.float32, jnp.bfloat16
SPECIES, RADIAL = 4, 4
K = SPECIES * RADIAL
LANES = 128
RATES = tuple(scale * 2.0**r for scale in (0.1, 0.15) for r in range(RADIAL))
ORDERS = ((0, 1), (1, 4), (4, 10))
FOLD = (1.0,) * 7 + (2.0,) * 3
PAIRS = ((0, 0), (1, 1), (2, 2), (0, 1), (0, 2), (1, 2))
NT = (((1,), (1,)), ((), ()))


def angular(radial, o):
    first = [radial * o[p] for p in range(3)]
    return [radial] + first + [first[a] * o[b] for a, b in PAIRS]


def along(start, size):
    return pl.ds(pl.multiple_of(start, size), size)


def norms(sparse_ref, alpha_ref, scale_ref, first, last, chunk=512):
    depth = sparse_ref.shape[1]
    ones = jnp.ones((8, LANES), BF16)
    row = lax.broadcasted_iota(jnp.int32, (8, chunk), 0)
    per = chunk // LANES
    for t in range(first, last):
        raw = sparse_ref[t * chunk : (t + 1) * chunk, :]
        parts = [raw[:, j * LANES : (j + 1) * LANES] for j in range(depth // LANES)]
        parts = [part * part for part in parts]
        while len(parts) > 1:
            parts = [x + y for x, y in zip(parts[::2], parts[1::2])] + parts[len(parts) // 2 * 2 :]
        squares = lax.dot_general(ones, parts[0], NT, preferred_element_type=F32)
        inverse = 1.0 / (squares + EPS)
        alpha = jnp.concatenate([alpha_ref[t * per + j : t * per + j + 1, :] for j in range(per)], axis=1)
        scale_ref[:, t * chunk : (t + 1) * chunk] = inverse * jnp.where(row == 0, 1.0, 2.0 * alpha)


def pair_setup(table_ref, pos_ref, nb_ref, mask_ref, live, off_ref, w_ref, sp_ref, r_ref):
    own = pos_ref.shape[1]
    tables = table_ref.shape[1] // LANES
    blocks = nb_ref.shape[0] // 8
    lane = lax.broadcasted_iota(jnp.int32, (8, LANES), 1)

    def step(i, _):
        h, b = i // blocks, i % blocks
        rows, cols = along(b * 8, 8), along(h * LANES, LANES)
        index = nb_ref[rows, cols]
        low, high = index & (LANES - 1), index // LANES
        picked = []
        for c in range(4):
            value = None
            for t in range(tables):
                source = jnp.broadcast_to(table_ref[c : c + 1, t * LANES : (t + 1) * LANES], (8, LANES))
                part = jnp.take_along_axis(source, low, axis=1, mode="promise_in_bounds")
                value = part if value is None else jnp.where(high == t, part, value)
            picked.append(value)
        o = [picked[p] - pos_ref[p : p + 1, cols] for p in range(3)]
        alive = ((index >= own) | (index < live)) & (h * LANES + lane < live)
        valid = jnp.where(alive, mask_ref[rows, cols].astype(F32), 0.0)
        for p in range(3):
            off_ref[h, p, rows, :] = o[p]
        for s in range(SPECIES):
            w_ref[h, s, rows, :] = jnp.where(picked[3] == s, valid, 0.0)
        sp_ref[h, 0, rows, :] = picked[3]
        sp_ref[h, 1, rows, :] = valid
        square = o[0] * o[0] + o[1] * o[1] + o[2] * o[2]
        for e in range(2):
            radial = jnp.exp(square * (-RATES[e * RADIAL]))
            for r in range(RADIAL):
                if r:
                    radial = radial * radial
                r_ref[h, e * RADIAL + r, rows, :] = radial
        return 0

    lax.fori_loop(0, own // LANES * blocks, step, 0, unroll=8)


def moments(off_ref, w_ref, r_ref, acc_ref, m_ref, mc_ref):
    halves, _, count, _ = off_ref.shape
    rates = len(RATES)

    def step(i, _):
        h, er = i // rates, i % rates
        total = [[None] * 10 for _ in range(SPECIES)]
        for b in range(count // 8):
            rows = slice(b * 8, b * 8 + 8)
            v = angular(r_ref[h, er, rows, :], [off_ref[h, p, rows, :] for p in range(3)])
            for s in range(SPECIES):
                weight = w_ref[h, s, rows, :]
                for m in range(10):
                    term = weight * v[m]
                    total[s][m] = term if b == 0 else total[s][m] + term
        e, r = er // RADIAL, er % RADIAL
        for s in range(SPECIES):
            for m in range(10):
                acc_ref[(h * 2 + e) * 10 + m, along((s * RADIAL + r) * 8, 8), :] = total[s][m]
        return 0

    lax.fori_loop(0, halves * rates, step, 0)

    def fold(i, _):
        value = acc_ref[i, pl.ds(0, K, stride=8), :]
        for j in range(1, 8):
            value = value + acc_ref[i, pl.ds(j, K, stride=8), :]
        m_ref[i] = value
        mc_ref[i] = value * jnp.where(i % 10 >= 7, 2.0, 1.0)
        return 0

    lax.fori_loop(0, halves * 20, fold, 0, unroll=8)


def descriptors(m_ref, mc_ref, d_ref, rinv_ref, desc_ref, eye_ref):
    halves = d_ref.shape[0]
    for h in range(halves):
        base = h * 20

        def step(k, squares):
            for l, (start, stop) in enumerate(ORDERS):
                value = None
                for m in range(start, stop):
                    term = m_ref[base + m, pl.ds(k, 1), :] * mc_ref[base + 10 + m]
                    value = term if value is None else value + term
                d_ref[h, along(l * K * K + k * K, K), :] = value
                squares = squares + value * value
            return squares

        squares = lax.fori_loop(0, K, step, jnp.zeros((K, LANES), F32), unroll=2)
        rinv = lax.rsqrt(jnp.sum(squares, axis=0, keepdims=True) + EPS)
        rinv_ref[h] = jnp.broadcast_to(rinv, (8, LANES))
        unit = (d_ref[h] * rinv).astype(BF16)
        desc_ref[h * LANES : (h + 1) * LANES, :] = lax.dot_general(
            eye_ref[:LANES, :LANES], unit, NT, preferred_element_type=F32
        ).astype(BF16)


def kernel_sums(desc_ref, sparse_ref, scale_ref, factor_ref, grad_ref, vec_ref, energy_ref, chunk=512):
    count = sparse_ref.shape[0]
    for t in range(count // chunk):
        rows = slice(t * chunk, (t + 1) * chunk)
        raw = sparse_ref[rows, :]
        projection = lax.dot_general(desc_ref[...], raw, NT, preferred_element_type=F32)
        coefficient = projection * scale_ref[1:2, rows]
        kernel = projection * projection * scale_ref[0:1, rows]
        energy_terms = coefficient * projection
        energy = energy_terms[:, :LANES]
        for j in range(1, chunk // LANES):
            energy = energy + energy_terms[:, j * LANES : (j + 1) * LANES]
        grad = jnp.dot(coefficient.astype(BF16), raw, preferred_element_type=F32)
        vec = jnp.dot(kernel.astype(BF16), factor_ref[rows, :], preferred_element_type=F32)
        if t == 0:
            grad_ref[...] = grad
            vec_ref[...] = vec
            energy_ref[...] = energy
        else:
            grad_ref[...] += grad
            vec_ref[...] += vec
            energy_ref[...] += energy


def moment_grads(grad_ref, desc_ref, eye_ref, gd_ref, gt_ref, mc_ref, rinv_ref, g_ref):
    halves = gt_ref.shape[0]
    unit = desc_ref[...].astype(F32)
    grad = grad_ref[...]
    along_unit = jnp.sum(grad * unit, axis=1, keepdims=True)
    gd_ref[...] = (grad - unit * along_unit).astype(BF16)
    for h in range(halves):
        for l in range(3):
            gt_ref[h, l] = lax.dot_general(
                eye_ref[...],
                gd_ref[h * LANES : (h + 1) * LANES, l * K * K : (l + 1) * K * K],
                NT,
                preferred_element_type=F32,
            )

    def step(i, _):
        h, e = i // 2, i % 2
        rinv = rinv_ref[h, 0:1, :]
        for l, (start, stop) in enumerate(ORDERS):
            total = [None] * 10
            for j in range(K):
                block = gt_ref[h, l, along((1 - e) * K * K + j * K, K), :]
                for m in range(start, stop):
                    term = block * mc_ref[h * 20 + (1 - e) * 10 + m, j : j + 1, :]
                    total[m] = term if j == 0 else total[m] + term
            for m in range(start, stop):
                g_ref[i * 10 + m] = total[m] * rinv
        return 0

    lax.fori_loop(0, halves * 2, step, 0)


def pair_terms(off_ref, sp_ref, r_ref, g_ref, t_ref, own_ref, group=2):
    halves, _, count, _ = off_ref.shape
    blocks = count // 8 // group
    own_ref[...] = jnp.zeros(own_ref.shape, F32)
    for h in range(halves):
        t_ref[h, 9 * count :, :] = jnp.zeros((7 * count, LANES), F32)

    def step(i, _):
        h, b = i // blocks, i % blocks
        rows = [along((b * group + q) * 8, 8) for q in range(group)]
        o = [[off_ref[h, p, rows[q], :] for p in range(3)] for q in range(group)]
        ang = [[None] + o[q] + [o[q][x] * o[q][y] for x, y in PAIRS] for q in range(group)]
        kind = [sp_ref[h, 0, rows[q], :] for q in range(group)]
        hit = [[kind[q] == s for s in range(3)] for q in range(group)]
        top = [[None] * 10 for _ in range(group)]
        slope = [None] * group
        for er, rate in enumerate(RATES):
            e, r = er // RADIAL, er % RADIAL
            radial = [r_ref[h, er, rows[q], :] for q in range(group)]
            inner = [None] * group
            for m in range(10):
                g = [g_ref[(h * 2 + e) * 10 + m, s * RADIAL + r : s * RADIAL + r + 1, :] for s in range(SPECIES)]
                for q in range(group):
                    pick = jnp.where(hit[q][0], g[0], jnp.where(hit[q][1], g[1], jnp.where(hit[q][2], g[2], g[3])))
                    if m == 0:
                        inner[q] = pick
                    else:
                        inner[q] = inner[q] + pick * ang[q][m]
                        term = radial[q] * pick
                        top[q][m] = term if er == 0 else top[q][m] + term
            for q in range(group):
                term = (radial[q] * (-rate)) * inner[q]
                slope[q] = term if er == 0 else slope[q] + term
        sums = [None] * 9
        for q in range(group):
            x, y, z = o[q]
            t = top[q]
            valid = sp_ref[h, 1, rows[q], :]
            gx = valid * (t[1] + 2.0 * x * (t[4] + slope[q]) + t[7] * y + t[8] * z)
            gy = valid * (t[2] + 2.0 * y * (t[5] + slope[q]) + t[7] * x + t[9] * z)
            gz = valid * (t[3] + 2.0 * z * (t[6] + slope[q]) + t[8] * x + t[9] * y)
            g = [gx, gy, gz]
            terms = [-v for v in g] + [-0.5 * o[q][a] * g[c] for a, c in PAIRS]
            for c in range(9):
                t_ref[h, along(c * count + (b * group + q) * 8, 8), :] = terms[c]
                sums[c] = terms[c] if q == 0 else sums[c] + terms[c]
        for c in range(9):
            own_ref[h, c * 8 : c * 8 + 8, :] += -sums[c] if c < 3 else sums[c]
        return 0

    lax.fori_loop(0, halves * blocks, step, 0)


def scatter(nb_ref, t_ref, own_ref, energy_ref, tot_ref, unroll=32):
    count, own = nb_ref.shape
    halves = own // LANES
    tables = tot_ref.shape[0] // 16
    slot = lax.broadcasted_iota(jnp.int32, (LANES, own), 0).astype(F32).astype(BF16)

    def step(i, total):
        left, right = [], []
        for u in range(unroll):
            n = i * unroll + u
            index = jnp.broadcast_to(nb_ref[pl.ds(n, 1), :], (16, own))
            low = (index & (LANES - 1)).astype(F32).astype(BF16)
            high = (index // LANES).astype(F32).astype(BF16)
            terms = jnp.concatenate(
                [t_ref[h, pl.ds(n, 16, stride=count), :] for h in range(halves)], axis=1
            ).astype(BF16)
            zero, one = jnp.zeros_like(terms), jnp.ones_like(terms)
            left.append(jnp.concatenate([jnp.where(high == t, terms, zero) for t in range(tables)], axis=0))
            right.append(
                jnp.concatenate(
                    [jnp.where(slot[j : j + 16] == low, one, zero) for j in range(0, LANES, 16)], axis=0
                )
            )
        return total + lax.dot_general(
            jnp.concatenate(left, axis=1), jnp.concatenate(right, axis=1), NT, preferred_element_type=F32
        )

    total = lax.fori_loop(0, count // unroll, step, jnp.zeros(tot_ref.shape, F32))
    energies = 0.5 * lax.dot_general(
        jnp.ones((16, LANES), F32), energy_ref[...], NT, precision=lax.Precision.HIGHEST, preferred_element_type=F32
    )
    row = lax.broadcasted_iota(jnp.int32, (16, LANES), 0)
    for h in range(halves):
        mine = own_ref[h, pl.ds(0, 16, stride=8), :]
        for j in range(1, 8):
            mine = mine + own_ref[h, pl.ds(j, 16, stride=8), :]
        mine = jnp.where(row == 9, energies[:, h * LANES : (h + 1) * LANES], mine)
        tot_ref[h * 16 : (h + 1) * 16, :] = total[h * 16 : (h + 1) * 16, :] + mine
    for t in range(halves, tables):
        tot_ref[t * 16 : (t + 1) * 16, :] = total[t * 16 : (t + 1) * 16, :]


def identities(eye_ref):
    size = K * K
    row = lax.broadcasted_iota(jnp.int32, (size, size), 0)
    col = lax.broadcasted_iota(jnp.int32, (size, size), 1)
    eye_ref[:size, :] = jnp.where(row == col, 1.0, 0.0).astype(BF16)
    eye_ref[size:, :] = jnp.where((row % K) * K + row // K == col, 1.0, 0.0).astype(BF16)


def scratch_shapes(own, count, width, sparse, depth, rank):
    halves = own // LANES
    return dict(
        off=pltpu.VMEM((halves, 3, count, LANES), F32),
        w=pltpu.VMEM((halves, SPECIES, count, LANES), F32),
        sp=pltpu.VMEM((halves, 2, count, LANES), F32),
        r=pltpu.VMEM((halves, len(RATES), count, LANES), F32),
        acc=pltpu.VMEM((halves * 20, K * 8, LANES), F32),
        m=pltpu.VMEM((halves * 20, K, LANES), F32),
        mc=pltpu.VMEM((halves * 20, K, LANES), F32),
        d=pltpu.VMEM((halves, depth, LANES), F32),
        rinv=pltpu.VMEM((halves, 8, LANES), F32),
        desc=pltpu.VMEM((own, depth), BF16),
        eye=pltpu.VMEM((2 * K * K, K * K), BF16),
        scale=pltpu.VMEM((8, sparse), F32),
        grad=pltpu.VMEM((own, depth), F32),
        energy=pltpu.VMEM((own, LANES), F32),
        gd=pltpu.VMEM((own, depth), BF16),
        gt=pltpu.VMEM((halves, 3, 2 * K * K, LANES), F32),
        g=pltpu.VMEM((halves * 20, K, LANES), F32),
        t=pltpu.VMEM((halves, 16 * count, LANES), F32),
        own=pltpu.VMEM((halves, 16 * 8, LANES), F32),
    )


MESH = pl.DeviceIdType.MESH


def remote(source, target, sems, slot, device):
    return pltpu.make_async_remote_copy(
        src_ref=source,
        dst_ref=target,
        send_sem=sems.at[(0, *slot)],
        recv_sem=sems.at[(1, *slot)],
        device_id=device,
        device_id_type=MESH,
    )


class Place:
    def __init__(self):
        self.brick, self.part = lax.axis_index("space"), lax.axis_index("sparse")
        bricks, self.parts = lax.axis_size("space"), lax.axis_size("sparse")
        self.odd = lax.rem(self.brick, 2)
        self.mate = self.brick + 1 - 2 * self.odd
        self.exists = (self.brick > 0) & (self.brick < bricks - 1)
        self.cross = jnp.where(self.exists, self.brick - 1 + 2 * self.odd, self.mate)
        self.others = [lax.rem(self.part + j, self.parts) for j in range(self.parts)]

    def greet(self):
        barrier = pltpu.get_barrier_semaphore()

        def signal(device):
            pl.semaphore_signal(barrier, inc=1, device_id=device, device_id_type=MESH)

        signal((self.mate, self.part))

        @pl.when(self.exists)
        def _():
            for other in self.others:
                signal((self.cross, other))

        for other in self.others[1:]:
            signal((self.brick, other))

    def met(self):
        barrier = pltpu.get_barrier_semaphore()
        pl.semaphore_wait(barrier, jnp.where(self.exists, 2 * self.parts, self.parts))


def halo_pick(pos_ref, species_ref, send_refs, table_ref, face_ref):
    own = pos_ref.shape[1]
    table_ref[0:3, :own] = pos_ref[...]
    table_ref[3:4, :own] = species_ref[...].astype(F32)
    table_ref[4:8, :own] = jnp.zeros((4, own), F32)
    for f, send_ref in enumerate(send_refs):
        index = jnp.broadcast_to(send_ref[...], (8, LANES))
        low, high = index & (LANES - 1), index // LANES
        value = None
        for t in range(own // LANES):
            part = jnp.take_along_axis(
                table_ref[:, t * LANES : (t + 1) * LANES], low, axis=1, mode="promise_in_bounds"
            )
            value = part if value is None else jnp.where(high == t, part, value)
        face_ref[f] = value


def halo_place(rim_ref, table_ref, own, odd):
    mate, cross = rim_ref[0], rim_ref[1]
    table_ref[:, own : own + LANES] = jnp.where(odd == 1, mate, cross)
    table_ref[:, own + LANES : own + 2 * LANES] = jnp.where(odd == 1, cross, mate)


def deliver(ghosts, slots):
    high = ghosts.astype(BF16)
    low = (ghosts - high.astype(F32)).astype(BF16)
    both = lax.dot_general(jnp.concatenate([high, low], axis=0), slots, NT, preferred_element_type=F32)
    row = lax.broadcasted_iota(jnp.int32, (16, both.shape[1]), 0)
    return jnp.where(row < 9, both[:16] + both[16:], 0.0)


def slots_of(send, first, count):
    slot = first + lax.broadcasted_iota(jnp.int32, (count, LANES), 0)
    return jnp.where(slot == send, 1.0, 0.0).astype(BF16)


def brick(pos, species, live, nb, mask, send_lo, send_hi, sparse, alpha, factor, parts):
    own, count = pos.shape[1], nb.shape[0]
    depth, rank = sparse.shape[1], factor.shape[1]
    halves = own // LANES
    tables = halves + 2
    share = own // parts
    names = scratch_shapes(own, count, tables * LANES, sparse.shape[0], depth, rank)
    inputs = (pos, species, send_lo, send_hi, nb, mask, alpha, sparse, factor)
    names.update(
        table=pltpu.VMEM((8, tables * LANES), F32),
        face=pltpu.VMEM((2, 8, LANES), F32),
        rim=pltpu.VMEM((2, 8, LANES), F32),
        vec=pltpu.VMEM((own, rank), F32),
        tot=pltpu.VMEM((tables * 16, LANES), F32),
        vec_out=pltpu.VMEM((own, rank), BF16),
        vec_in=pltpu.VMEM((parts, share, rank), BF16),
        tot_out=pltpu.VMEM((halves, 16, LANES), BF16),
        tot_in=pltpu.VMEM((parts, 16, LANES), BF16),
        relay_out=pltpu.VMEM((16, LANES), F32),
        relay_in=pltpu.VMEM((16, LANES), F32),
        cross_out=pltpu.VMEM((16, LANES), BF16),
        cross_in=pltpu.VMEM((parts, 16, LANES), BF16),
        halo_sems=pltpu.SemaphoreType.DMA((2, 2)),
        relay_sems=pltpu.SemaphoreType.DMA((2, 1)),
        vec_sems=pltpu.SemaphoreType.DMA((2, parts)),
        tot_sems=pltpu.SemaphoreType.DMA((2, parts)),
        cross_sems=pltpu.SemaphoreType.DMA((2, parts)),
        load_sems=pltpu.SemaphoreType.DMA((len(inputs) + 1,)),
        live=pltpu.SMEM((1,), jnp.int32),
    )
    keys = list(names)
    local = [pltpu.VMEM(x.shape, x.dtype) for x in inputs]

    def kernel(*refs):
        sources, live_hbm, out_ref = refs[: len(inputs)], refs[len(inputs)], refs[len(inputs) + 1]
        held = refs[len(inputs) + 2 : 2 * len(inputs) + 2]
        s = dict(zip(keys, refs[2 * len(inputs) + 2 :]))
        pos_ref, species_ref, lo_ref, hi_ref, nb_ref, mask_ref, alpha_ref, sparse_ref, factor_ref = held
        place = Place()
        place.greet()
        loads = [
            pltpu.make_async_copy(x, y, s["load_sems"].at[k])
            for k, (x, y) in enumerate(zip((*sources, live_hbm), (*held, s["live"])))
        ]
        for load in loads:
            load.start()
        for load in loads[:4]:
            load.wait()
        halo_pick(pos_ref, species_ref, (lo_ref, hi_ref), s["table"], s["face"])
        place.met()
        near = remote(s["face"].at[1 - place.odd], s["rim"].at[0], s["halo_sems"], (0,), (place.mate, place.part))
        far = remote(s["face"].at[place.odd], s["rim"].at[1], s["halo_sems"], (1,), (place.cross, place.part))
        near.start()

        @pl.when(place.exists)
        def _():
            far.start()

        @pl.when(jnp.logical_not(place.exists))
        def _():
            s["rim"][1] = jnp.zeros((8, LANES), F32)
            for j in range(parts):
                s["cross_in"][j] = jnp.zeros((16, LANES), BF16)

        identities(s["eye"])
        for load in loads[4:]:
            load.wait()
        norms(sparse_ref, alpha_ref, s["scale"], 0, sparse.shape[0] // 512)
        near.wait()

        @pl.when(place.exists)
        def _():
            far.wait()

        halo_place(s["rim"], s["table"], own, place.odd)
        pair_setup(s["table"], pos_ref, nb_ref, mask_ref, s["live"][0], s["off"], s["w"], s["sp"], s["r"])
        moments(s["off"], s["w"], s["r"], s["acc"], s["m"], s["mc"])
        descriptors(s["m"], s["mc"], s["d"], s["rinv"], s["desc"], s["eye"])
        kernel_sums(s["desc"], sparse_ref, s["scale"], factor_ref, s["grad"], s["vec"], s["energy"])
        s["vec_out"][...] = s["vec"][...].astype(BF16)
        vectors = [
            remote(
                s["vec_out"].at[pl.ds(pl.multiple_of(other * share, share), share)],
                s["vec_in"].at[j],
                s["vec_sems"],
                (j,),
                (place.brick, other),
            )
            for j, other in enumerate(place.others)
            if j
        ]
        for copy in vectors:
            copy.start()
        moment_grads(s["grad"], s["desc"], s["eye"], s["gd"], s["gt"], s["mc"], s["rinv"], s["g"])
        pair_terms(s["off"], s["sp"], s["r"], s["g"], s["t"], s["own"])
        scatter(nb_ref, s["t"], s["own"], s["energy"], s["tot"])
        s["relay_out"][...] = s["tot"][pl.ds(pl.multiple_of((halves + 1 - place.odd) * 16, 16), 16), :]
        relay = remote(s["relay_out"], s["relay_in"], s["relay_sems"], (0,), (place.mate, place.part))
        relay.start()
        s["cross_out"][...] = s["tot"][pl.ds(pl.multiple_of((halves + place.odd) * 16, 16), 16), :].astype(BF16)
        crossing = [
            remote(s["cross_out"], s["cross_in"].at[j], s["cross_sems"], (j,), (place.cross, other))
            for j, other in enumerate(place.others)
        ]

        @pl.when(place.exists)
        def _():
            for copy in crossing[::-1]:
                copy.start()

        odd = place.odd == 1
        near_send = jnp.where(odd, lo_ref[...], hi_ref[...])
        far_send = jnp.where(odd, hi_ref[...], lo_ref[...])
        near_slots = slots_of(near_send, 0, own)
        relay.wait()
        near_part = deliver(s["relay_in"][...], near_slots)
        for h in range(halves):
            s["tot_out"][h] = (
                s["tot"][h * 16 : (h + 1) * 16, :] + near_part[:, h * LANES : (h + 1) * LANES]
            ).astype(BF16)
        totals = [
            remote(
                s["tot_out"].at[other * share // LANES], s["tot_in"].at[j], s["tot_sems"], (j,), (place.brick, other)
            )
            for j, other in enumerate(place.others)
            if j
        ]
        for copy in totals:
            copy.start()
        vec = s["vec_out"][pl.ds(pl.multiple_of(place.part * share, share), share), :].astype(F32)
        for copy in vectors:
            copy.wait()
        for j in range(1, parts):
            vec = vec + s["vec_in"][j].astype(F32)
        variances = lax.dot_general(
            jnp.ones((16, rank), F32), vec * vec, NT, precision=lax.Precision.HIGHEST, preferred_element_type=F32
        )
        half = place.part * share // LANES
        far_slots = slots_of(far_send, half * LANES, LANES)
        mine = s["tot_out"][half].astype(F32)
        for copy in totals:
            copy.wait()
        for j in range(1, parts):
            mine = mine + s["tot_in"][j].astype(F32)

        @pl.when(place.exists)
        def _():
            for copy in crossing:
                copy.wait()

        ghosts = s["cross_in"][0].astype(F32)
        for j in range(1, parts):
            ghosts = ghosts + s["cross_in"][j].astype(F32)
        mine = mine + deliver(ghosts, far_slots)
        shift = lax.rem(LANES - lax.rem(place.part * share, LANES), LANES)
        out_ref[...] = pltpu.roll(mine, shift, 1)
        out_ref[10:11, :share] = variances[10:11]

    anywhere = pl.BlockSpec(memory_space=pltpu.HBM)
    return pl.pallas_call(
        kernel,
        out_shape=jax.ShapeDtypeStruct((16, LANES), F32),
        in_specs=[anywhere] * (len(inputs) + 1),
        out_specs=pl.BlockSpec(memory_space=pltpu.VMEM),
        scratch_shapes=local + list(names.values()),
        compiler_params=pltpu.CompilerParams(
            vmem_limit_bytes=60 * 1024 * 1024, collective_id=0, has_side_effects=True
        ),
        name="brick",
    )(*inputs, live)


def split(result, share):
    def kernel(result_ref, force_ref, energy_ref, variance_ref, virial_ref):
        force_ref[...] = result_ref[0:3, :share]
        virial_ref[...] = result_ref[3:9, :share]
        energy_ref[...] = result_ref[9:10, :share]
        variance_ref[...] = result_ref[10:11, :share]

    vmem = pl.BlockSpec(memory_space=pltpu.VMEM)
    return pl.pallas_call(
        kernel,
        out_shape=tuple(jax.ShapeDtypeStruct((n, share), F32) for n in (3, 1, 1, 6)),
        in_specs=[vmem],
        out_specs=(vmem,) * 4,
        name="split",
    )(result)


def shards(
    positions, species, live_count, neighbors, neighbor_mask, send_lo, send_hi, sparse_desc, alpha, var_factor
):
    parts = lax.axis_size("sparse")
    result = brick(
        positions,
        species[None],
        live_count,
        neighbors,
        neighbor_mask,
        send_lo[None],
        send_hi[None],
        sparse_desc,
        alpha.reshape(-1, LANES),
        var_factor,
        parts,
    )
    forces, energies, variances, virials = split(result, positions.shape[1] // parts)
    return forces, energies[0], variances[0], virials


def solution(mesh):
    return jax.shard_map(
        shards,
        mesh=mesh,
        in_specs=(
            P(None, "space"),
            P("space"),
            P("space"),
            P(None, "space"),
            P(None, "space"),
            P("space"),
            P("space"),
            P("sparse", None),
            P("sparse"),
            P("sparse", None),
        ),
        out_specs=(
            P(None, ("space", "sparse")),
            P(("space", "sparse")),
            P(("space", "sparse")),
            P(None, ("space", "sparse")),
        ),
        check_vma=False,
    )
```

```python
import jax
import jax.numpy as jnp
from jax import lax
from jax.experimental import pallas as pl
from jax.experimental.pallas import tpu as pltpu
from jax.sharding import PartitionSpec as P

EPS = 1e-6
F32, BF16 = jnp.float32, jnp.bfloat16
SPECIES, RADIAL = 4, 4
K = SPECIES * RADIAL
LANES = 128
LOW = 64
RATES = tuple(scale * 2.0**r for scale in (0.1, 0.15) for r in range(RADIAL))
ORDERS = ((0, 1), (1, 4), (4, 10))
FOLD = (1.0,) * 7 + (2.0,) * 3
PAIRS = ((0, 0), (1, 1), (2, 2), (0, 1), (0, 2), (1, 2))
NT = (((1,), (1,)), ((), ()))


def angular(radial, o):
    first = [radial * o[p] for p in range(3)]
    return [radial] + first + [first[a] * o[b] for a, b in PAIRS]


def along(start, size):
    return pl.ds(pl.multiple_of(start, size), size)


def norms(sparse_ref, alpha_ref, scale_ref, first, last, chunk=512):
    depth = sparse_ref.shape[1]
    ones = jnp.ones((8, LANES), BF16)
    row = lax.broadcasted_iota(jnp.int32, (8, chunk), 0)
    per = chunk // LANES
    for t in range(first, last):
        raw = sparse_ref[t * chunk : (t + 1) * chunk, :]
        parts = [raw[:, j * LANES : (j + 1) * LANES] for j in range(depth // LANES)]
        parts = [part * part for part in parts]
        while len(parts) > 1:
            parts = [x + y for x, y in zip(parts[::2], parts[1::2])] + parts[len(parts) // 2 * 2 :]
        squares = lax.dot_general(ones, parts[0], NT, preferred_element_type=F32)
        inverse = 1.0 / (squares + EPS)
        alpha = jnp.concatenate([alpha_ref[t * per + j : t * per + j + 1, :] for j in range(per)], axis=1)
        scale_ref[:, t * chunk : (t + 1) * chunk] = inverse * jnp.where(row == 0, 1.0, 2.0 * alpha)


def pick_from(table_ref, first, last, low, high, value, rows):
    picked = []
    for c in range(4):
        got = value[c]
        for t in range(first, last):
            source = jnp.broadcast_to(table_ref[c : c + 1, t * LANES : (t + 1) * LANES], (rows, LANES))
            part = jnp.take_along_axis(source, low, axis=1, mode="promise_in_bounds")
            got = part if got is None else jnp.where(high == t, part, got)
        picked.append(got)
    return picked


def own_setup(table_ref, nb_ref, pick_ref):
    halves, _, count, _ = pick_ref.shape
    blocks = count // 8

    def step(i, _):
        h, b = i // blocks, i % blocks
        rows = along(b * 8, 8)
        index = nb_ref[rows, along(h * LANES, LANES)]
        values = pick_from(table_ref, 0, halves, index & (LANES - 1), index // LANES, [None] * 4, 8)
        for c in range(4):
            pick_ref[h, c, rows, :] = values[c]
        return 0

    lax.fori_loop(0, halves * blocks, step, 0, unroll=8)


def pair_setup(table_ref, pos_ref, nb_ref, mask_ref, live, pick_ref, off_ref, w_ref, kind_ref, r_ref):
    own = pos_ref.shape[1]
    halves = own // LANES
    tables = table_ref.shape[1] // LANES
    blocks = nb_ref.shape[0] // 8
    lane = lax.broadcasted_iota(jnp.int32, (8, LANES), 1)

    def step(i, _):
        h, b = i // blocks, i % blocks
        rows, cols = along(b * 8, 8), along(h * LANES, LANES)
        index = nb_ref[rows, cols]
        held = [pick_ref[h, c, rows, :] for c in range(4)]
        picked = pick_from(table_ref, halves, tables, index & (LANES - 1), index // LANES, held, 8)
        o = [picked[p] - pos_ref[p : p + 1, cols] for p in range(3)]
        alive = ((index >= own) | (index < live)) & (h * LANES + lane < live)
        valid = jnp.where(alive, mask_ref[rows, cols].astype(F32), 0.0)
        for p in range(3):
            off_ref[h, p, rows, :] = o[p]
        for s in range(SPECIES - 1):
            w_ref[h, s, rows, :] = jnp.where(picked[3] == s, 1.0, 0.0)
        kind_ref[h, rows, :] = picked[3].astype(jnp.int32)
        square = o[0] * o[0] + o[1] * o[1] + o[2] * o[2]
        for e in range(2):
            radial = jnp.exp(square * (-RATES[e * RADIAL]))
            for r in range(RADIAL):
                if r:
                    radial = radial * radial
                r_ref[h, e * RADIAL + r, rows, :] = radial * valid
        return 0

    lax.fori_loop(0, halves * blocks, step, 0, unroll=8)


def moments(off_ref, w_ref, r_ref, acc_ref, m_ref, mc_ref):
    halves, _, count, _ = off_ref.shape
    rates = len(RATES)

    def step(i, _):
        h, er = i // rates, i % rates
        total = [[None] * 10 for _ in range(SPECIES)]
        for b in range(count // 8):
            rows = slice(b * 8, b * 8 + 8)
            v = angular(r_ref[h, er, rows, :], [off_ref[h, p, rows, :] for p in range(3)])
            for s in range(SPECIES):
                weight = w_ref[h, s, rows, :] if s < SPECIES - 1 else None
                for m in range(10):
                    term = v[m] if weight is None else weight * v[m]
                    total[s][m] = term if b == 0 else total[s][m] + term
        e, r = er // RADIAL, er % RADIAL
        for m in range(10):
            total[3][m] = total[3][m] - (total[0][m] + total[1][m] + total[2][m])
            for s in range(SPECIES):
                acc_ref[(h * 2 + e) * 10 + m, along((s * RADIAL + r) * 8, 8), :] = total[s][m]
        return 0

    lax.fori_loop(0, halves * rates, step, 0)

    def fold(i, _):
        value = acc_ref[i, pl.ds(0, K, stride=8), :]
        for j in range(1, 8):
            value = value + acc_ref[i, pl.ds(j, K, stride=8), :]
        m_ref[i] = value
        mc_ref[i] = value * jnp.where(i % 10 >= 7, 2.0, 1.0)
        return 0

    lax.fori_loop(0, halves * 20, fold, 0, unroll=8)


def descriptors(m_ref, mc_ref, d_ref, rinv_ref, desc_ref, plain_ref):
    halves = d_ref.shape[0]

    def step(k, squares):
        fresh = []
        for h in range(halves):
            base = h * 20
            total = squares[h]
            for l, (start, stop) in enumerate(ORDERS):
                value = None
                for m in range(start, stop):
                    term = m_ref[base + m, pl.ds(k, 1), :] * mc_ref[base + 10 + m]
                    value = term if value is None else value + term
                d_ref[h, along(l * K * K + k * K, K), :] = value
                total = total + value * value
            fresh.append(total)
        return tuple(fresh)

    squares = lax.fori_loop(0, K, step, (jnp.zeros((K, LANES), F32),) * halves, unroll=8)
    for h in range(halves):
        rinv = lax.rsqrt(jnp.sum(squares[h], axis=0, keepdims=True) + EPS)
        rinv_ref[h] = jnp.broadcast_to(rinv, (8, LANES))
        unit = (d_ref[h] * rinv).astype(BF16)
        desc_ref[h * LANES : (h + 1) * LANES, :] = lax.dot_general(
            plain_ref[...], unit, NT, preferred_element_type=F32
        ).astype(BF16)


def kernel_sums(desc_ref, sparse_ref, scale_ref, factor_ref, grad_ref, vec_ref, energy_ref):
    raw = sparse_ref[...]
    projection = lax.dot_general(desc_ref[...], raw, NT, preferred_element_type=F32)
    coefficient = projection * scale_ref[1:2, :]
    kernel = projection * projection * scale_ref[0:1, :]
    energy_terms = coefficient * projection
    energy = energy_terms[:, :LANES]
    for j in range(1, raw.shape[0] // LANES):
        energy = energy + energy_terms[:, j * LANES : (j + 1) * LANES]
    energy_ref[...] = energy
    grad_ref[...] = jnp.dot(coefficient.astype(BF16), raw, preferred_element_type=F32)
    vec_ref[...] = jnp.dot(kernel.astype(BF16), factor_ref[...], preferred_element_type=F32)


def moment_grads(grad_ref, desc_ref, eye_ref, gd_ref, gt_ref, mc_ref, rinv_ref, g_ref):
    halves = gt_ref.shape[0]
    unit = desc_ref[...].astype(F32)
    grad = grad_ref[...]
    along_unit = jnp.sum(grad * unit, axis=1, keepdims=True)
    gd_ref[...] = (grad - unit * along_unit).astype(BF16)
    for h in range(halves):
        for l in range(3):
            gt_ref[h, l] = lax.dot_general(
                eye_ref[...],
                gd_ref[h * LANES : (h + 1) * LANES, l * K * K : (l + 1) * K * K],
                NT,
                preferred_element_type=F32,
            )

    def step(i, _):
        h, e = i // 2, i % 2
        rinv = rinv_ref[h, 0:1, :]
        for l, (start, stop) in enumerate(ORDERS):
            total = [None] * 10
            for j in range(K):
                block = gt_ref[h, l, along((1 - e) * K * K + j * K, K), :]
                for m in range(start, stop):
                    term = block * mc_ref[h * 20 + (1 - e) * 10 + m, j : j + 1, :]
                    total[m] = term if j == 0 else total[m] + term
            for m in range(start, stop):
                g_ref[i * 10 + m] = total[m] * rinv
        return 0

    lax.fori_loop(0, halves * 2, step, 0)


def pair_terms(off_ref, kind_ref, r_ref, g_ref, t_ref, own_ref, group=2):
    halves, _, count, _ = off_ref.shape
    blocks = count // 8 // group
    own_ref[...] = jnp.zeros(own_ref.shape, F32)

    def step(i, _):
        h, b = i // blocks, i % blocks
        rows = [along((b * group + q) * 8, 8) for q in range(group)]
        o = [[off_ref[h, p, rows[q], :] for p in range(3)] for q in range(group)]
        ang = [[None] + o[q] + [o[q][x] * o[q][y] for x, y in PAIRS] for q in range(group)]
        kind = [kind_ref[h, rows[q], :] for q in range(group)]
        which = [[kind[q], kind[q] + SPECIES] for q in range(group)]
        top = [[None] * 10 for _ in range(group)]
        slope = [None] * group
        for er, rate in enumerate(RATES):
            e, r = er // RADIAL, er % RADIAL
            radial = [r_ref[h, er, rows[q], :] for q in range(group)]
            inner = [None] * group
            for m in range(10):
                g = g_ref[(h * 2 + e) * 10 + m, r // 2 * 8 : r // 2 * 8 + 8, :]
                for q in range(group):
                    pick = jnp.take_along_axis(g, which[q][r % 2], axis=0, mode="promise_in_bounds")
                    if m == 0:
                        inner[q] = pick
                    else:
                        inner[q] = inner[q] + pick * ang[q][m]
                        term = radial[q] * pick
                        top[q][m] = term if er == 0 else top[q][m] + term
            for q in range(group):
                term = (radial[q] * (-rate)) * inner[q]
                slope[q] = term if er == 0 else slope[q] + term
        sums = [None] * 9
        for q in range(group):
            x, y, z = o[q]
            t = top[q]
            gx = t[1] + 2.0 * x * (t[4] + slope[q]) + t[7] * y + t[8] * z
            gy = t[2] + 2.0 * y * (t[5] + slope[q]) + t[7] * x + t[9] * z
            gz = t[3] + 2.0 * z * (t[6] + slope[q]) + t[8] * x + t[9] * y
            g = [gx, gy, gz]
            terms = [-v for v in g] + [-0.5 * o[q][a] * g[c] for a, c in PAIRS]
            for c in range(9):
                t_ref[h, along(c * count + (b * group + q) * 8, 8), :] = terms[c]
                sums[c] = terms[c] if q == 0 else sums[c] + terms[c]
        for c in range(9):
            own_ref[h, c * 8 : c * 8 + 8, :] += -sums[c] if c < 3 else sums[c]
        return 0

    lax.fori_loop(0, halves * blocks, step, 0)


def scatter(nb_ref, t_ref, own_ref, energy_ref, tot_ref, unroll=16):
    count, own = nb_ref.shape
    halves = own // LANES
    tables = tot_ref.shape[0] // 16
    groups = tables * LANES // LOW
    per = LANES // LOW
    slot = lax.broadcasted_iota(jnp.int32, (LOW, own), 0).astype(F32).astype(BF16)
    row = lax.broadcasted_iota(jnp.int32, (16, own), 0)
    upper = jnp.where(row < 8, 0, 1).astype(F32).astype(BF16)
    every = row.astype(F32).astype(BF16)

    def step(i, total):
        left, right = [], []
        for u in range(unroll):
            n = i * unroll + u
            index = jnp.broadcast_to(nb_ref[pl.ds(n, 1), :], (16, own))
            low = (index & (LOW - 1)).astype(F32).astype(BF16)
            high = (index // LOW).astype(F32).astype(BF16)
            eight = jnp.concatenate([t_ref[h, pl.ds(n, 8, stride=count), :] for h in range(halves)], axis=1)
            eight = jnp.concatenate([eight, eight], axis=0).astype(BF16)
            ninth = jnp.concatenate([t_ref[h, pl.ds(8 * count + n, 1), :] for h in range(halves)], axis=1)
            ninth = jnp.broadcast_to(ninth, (16, own)).astype(BF16)
            zero, one = jnp.zeros_like(eight), jnp.ones_like(eight)
            shifted = high - upper
            left.append(
                jnp.concatenate(
                    [jnp.where(shifted == g, eight, zero) for g in range(0, groups, 2)]
                    + [jnp.where(high == every, ninth, zero)],
                    axis=0,
                )
            )
            right.append(
                jnp.concatenate([jnp.where(slot[j : j + 16] == low, one, zero) for j in range(0, LOW, 16)], axis=0)
            )
        return total + lax.dot_general(
            jnp.concatenate(left, axis=1), jnp.concatenate(right, axis=1), NT, preferred_element_type=F32
        )

    total = lax.fori_loop(0, count // unroll, step, jnp.zeros((groups * 8 + 16, LOW), F32))
    energies = 0.5 * lax.dot_general(
        jnp.ones((16, LANES), F32), energy_ref[...], NT, precision=lax.Precision.HIGHEST, preferred_element_type=F32
    )
    row = lax.broadcasted_iota(jnp.int32, (8, LANES), 0)
    for t in range(tables):
        main = jnp.concatenate([total[(t * per + g) * 8 : (t * per + g + 1) * 8] for g in range(per)], axis=1)
        last = jnp.concatenate(
            [total[groups * 8 + t * per + g : groups * 8 + t * per + g + 1] for g in range(per)], axis=1
        )
        rest = jnp.where(row == 0, last, 0.0)
        if t < halves:
            mine = own_ref[t, pl.ds(0, 16, stride=8), :]
            for j in range(1, 8):
                mine = mine + own_ref[t, pl.ds(j, 16, stride=8), :]
            main = main + mine[:8]
            rest = rest + jnp.where(row == 1, energies[:8, t * LANES : (t + 1) * LANES], mine[8:])
        tot_ref[t * 16 : t * 16 + 8, :] = main
        tot_ref[t * 16 + 8 : t * 16 + 16, :] = rest


def identities(plain_ref, eye_ref):
    size = K * K
    row = lax.broadcasted_iota(jnp.int32, (size, size), 0)
    col = lax.broadcasted_iota(jnp.int32, (size, size), 1)
    plain_ref[...] = jnp.where(row[:LANES, :LANES] == col[:LANES, :LANES], 1.0, 0.0).astype(BF16)
    outer = row // K
    inner = row % SPECIES * RADIAL + row % K // SPECIES
    eye_ref[:size, :] = jnp.where(outer * K + inner == col, 1.0, 0.0).astype(BF16)
    eye_ref[size:, :] = jnp.where(inner * K + outer == col, 1.0, 0.0).astype(BF16)


def scratch_shapes(own, count, width, sparse, depth, rank):
    halves = own // LANES
    return dict(
        off=pltpu.VMEM((halves, 3, count, LANES), F32),
        pick=pltpu.VMEM((halves, 4, count, LANES), F32),
        plain=pltpu.VMEM((LANES, LANES), BF16),
        w=pltpu.VMEM((halves, SPECIES - 1, count, LANES), F32),
        kind=pltpu.VMEM((halves, count, LANES), jnp.int32),
        r=pltpu.VMEM((halves, len(RATES), count, LANES), F32),
        acc=pltpu.VMEM((halves * 20, K * 8, LANES), F32),
        m=pltpu.VMEM((halves * 20, K, LANES), F32),
        mc=pltpu.VMEM((halves * 20, K, LANES), F32),
        d=pltpu.VMEM((halves, depth, LANES), F32),
        rinv=pltpu.VMEM((halves, 8, LANES), F32),
        desc=pltpu.VMEM((own, depth), BF16),
        eye=pltpu.VMEM((2 * K * K, K * K), BF16),
        scale=pltpu.VMEM((8, sparse), F32),
        grad=pltpu.VMEM((own, depth), F32),
        energy=pltpu.VMEM((own, LANES), F32),
        gd=pltpu.VMEM((own, depth), BF16),
        gt=pltpu.VMEM((halves, 3, 2 * K * K, LANES), F32),
        g=pltpu.VMEM((halves * 20, K, LANES), F32),
        t=pltpu.VMEM((halves, 9 * count, LANES), F32),
        own=pltpu.VMEM((halves, 16 * 8, LANES), F32),
    )


MESH = pl.DeviceIdType.MESH


def remote(source, target, sems, slot, device):
    return pltpu.make_async_remote_copy(
        src_ref=source,
        dst_ref=target,
        send_sem=sems.at[(0, *slot)],
        recv_sem=sems.at[(1, *slot)],
        device_id=device,
        device_id_type=MESH,
    )


class Place:
    def __init__(self):
        self.brick, self.part = lax.axis_index("space"), lax.axis_index("sparse")
        bricks, self.parts = lax.axis_size("space"), lax.axis_size("sparse")
        self.odd = lax.rem(self.brick, 2)
        self.mate = self.brick + 1 - 2 * self.odd
        self.exists = (self.brick > 0) & (self.brick < bricks - 1)
        self.cross = jnp.where(self.exists, self.brick - 1 + 2 * self.odd, self.mate)
        self.others = [lax.rem(self.part + j, self.parts) for j in range(self.parts)]

    def greet(self):
        barrier = pltpu.get_barrier_semaphore()

        def signal(device):
            pl.semaphore_signal(barrier, inc=1, device_id=device, device_id_type=MESH)

        signal((self.mate, self.part))

        @pl.when(self.exists)
        def _():
            for other in self.others:
                signal((self.cross, other))

        for other in self.others[1:]:
            signal((self.brick, other))

    def met(self):
        barrier = pltpu.get_barrier_semaphore()
        pl.semaphore_wait(barrier, jnp.where(self.exists, 2 * self.parts, self.parts))


def halo_pick(pos_ref, species_ref, send_refs, table_ref, face_ref):
    own = pos_ref.shape[1]
    table_ref[0:3, :own] = pos_ref[...]
    table_ref[3:4, :own] = species_ref[...].astype(F32)
    table_ref[4:8, :own] = jnp.zeros((4, own), F32)
    for f, send_ref in enumerate(send_refs):
        index = jnp.broadcast_to(send_ref[...], (8, LANES))
        low, high = index & (LANES - 1), index // LANES
        value = None
        for t in range(own // LANES):
            part = jnp.take_along_axis(
                table_ref[:, t * LANES : (t + 1) * LANES], low, axis=1, mode="promise_in_bounds"
            )
            value = part if value is None else jnp.where(high == t, part, value)
        face_ref[f] = value


def halo_place(rim_ref, table_ref, own, odd):
    mate, cross = rim_ref[0], rim_ref[1]
    table_ref[:, own : own + LANES] = jnp.where(odd == 1, mate, cross)
    table_ref[:, own + LANES : own + 2 * LANES] = jnp.where(odd == 1, cross, mate)


def deliver(ghosts, slots):
    high = ghosts.astype(BF16)
    low = (ghosts - high.astype(F32)).astype(BF16)
    both = lax.dot_general(jnp.concatenate([high, low], axis=0), slots, NT, preferred_element_type=F32)
    row = lax.broadcasted_iota(jnp.int32, (16, both.shape[1]), 0)
    return jnp.where(row < 9, both[:16] + both[16:], 0.0)


def slots_of(send, first, count):
    slot = first + lax.broadcasted_iota(jnp.int32, (count, LANES), 0)
    return jnp.where(slot == send, 1.0, 0.0).astype(BF16)


def brick(pos, species, live, nb, mask, send_lo, send_hi, sparse, alpha, factor, parts):
    own, count = pos.shape[1], nb.shape[0]
    depth, rank = sparse.shape[1], factor.shape[1]
    halves = own // LANES
    tables = halves + 2
    share = own // parts
    names = scratch_shapes(own, count, tables * LANES, sparse.shape[0], depth, rank)
    inputs = (pos, species, send_lo, send_hi, nb, mask, alpha, sparse, factor, live)
    names.update(
        table=pltpu.VMEM((8, tables * LANES), F32),
        face=pltpu.VMEM((2, 8, LANES), F32),
        rim=pltpu.VMEM((2, 8, LANES), F32),
        vec=pltpu.VMEM((own, rank), F32),
        tot=pltpu.VMEM((tables * 16, LANES), F32),
        vec_out=pltpu.VMEM((own, rank), BF16),
        vec_in=pltpu.VMEM((parts, share, rank), BF16),
        tot_out=pltpu.VMEM((halves, 16, LANES), BF16),
        tot_in=pltpu.VMEM((parts, 16, LANES), BF16),
        relay_out=pltpu.VMEM((16, LANES), F32),
        relay_in=pltpu.VMEM((16, LANES), F32),
        cross_out=pltpu.VMEM((16, LANES), BF16),
        cross_in=pltpu.VMEM((parts, 16, LANES), BF16),
        halo_sems=pltpu.SemaphoreType.DMA((2, 2)),
        relay_sems=pltpu.SemaphoreType.DMA((2, 1)),
        vec_sems=pltpu.SemaphoreType.DMA((2, parts)),
        tot_sems=pltpu.SemaphoreType.DMA((2, parts)),
        cross_sems=pltpu.SemaphoreType.DMA((2, parts)),
        load_sems=pltpu.SemaphoreType.DMA((len(inputs),)),
    )
    keys = list(names)
    local = [pltpu.VMEM(x.shape, x.dtype) for x in inputs]

    def kernel(*refs):
        sources, out_ref = refs[: len(inputs)], refs[len(inputs)]
        held = refs[len(inputs) + 1 : 2 * len(inputs) + 1]
        s = dict(zip(keys, refs[2 * len(inputs) + 1 :]))
        pos_ref, species_ref, lo_ref, hi_ref, nb_ref, mask_ref, alpha_ref, sparse_ref, factor_ref, live_ref = held
        place = Place()
        place.greet()
        loads = [
            pltpu.make_async_copy(x, y, s["load_sems"].at[k])
            for k, (x, y) in enumerate(zip(sources, held))
        ]
        for load in loads:
            load.start()
        for load in loads[:4]:
            load.wait()
        halo_pick(pos_ref, species_ref, (lo_ref, hi_ref), s["table"], s["face"])
        place.met()
        near = remote(s["face"].at[1 - place.odd], s["rim"].at[0], s["halo_sems"], (0,), (place.mate, place.part))
        far = remote(s["face"].at[place.odd], s["rim"].at[1], s["halo_sems"], (1,), (place.cross, place.part))
        near.start()

        @pl.when(place.exists)
        def _():
            far.start()

        @pl.when(jnp.logical_not(place.exists))
        def _():
            s["rim"][1] = jnp.zeros((8, LANES), F32)
            for j in range(parts):
                s["cross_in"][j] = jnp.zeros((16, LANES), BF16)

        identities(s["plain"], s["eye"])
        for load in loads[4:]:
            load.wait()
        norms(sparse_ref, alpha_ref, s["scale"], 0, sparse.shape[0] // 512)
        own_setup(s["table"], nb_ref, s["pick"])
        near.wait()

        @pl.when(place.exists)
        def _():
            far.wait()

        halo_place(s["rim"], s["table"], own, place.odd)
        live_row = jnp.broadcast_to(live_ref[...], (8, LANES))
        pair_setup(
            s["table"], pos_ref, nb_ref, mask_ref, live_row, s["pick"], s["off"], s["w"], s["kind"], s["r"]
        )
        moments(s["off"], s["w"], s["r"], s["acc"], s["m"], s["mc"])
        descriptors(s["m"], s["mc"], s["d"], s["rinv"], s["desc"], s["plain"])
        kernel_sums(s["desc"], sparse_ref, s["scale"], factor_ref, s["grad"], s["vec"], s["energy"])
        s["vec_out"][...] = s["vec"][...].astype(BF16)
        vectors = [
            remote(
                s["vec_out"].at[pl.ds(pl.multiple_of(other * share, share), share)],
                s["vec_in"].at[j],
                s["vec_sems"],
                (j,),
                (place.brick, other),
            )
            for j, other in enumerate(place.others)
            if j
        ]
        for copy in vectors:
            copy.start()
        moment_grads(s["grad"], s["desc"], s["eye"], s["gd"], s["gt"], s["mc"], s["rinv"], s["g"])
        pair_terms(s["off"], s["kind"], s["r"], s["g"], s["t"], s["own"])
        scatter(nb_ref, s["t"], s["own"], s["energy"], s["tot"])
        s["relay_out"][...] = s["tot"][pl.ds(pl.multiple_of((halves + 1 - place.odd) * 16, 16), 16), :]
        relay = remote(s["relay_out"], s["relay_in"], s["relay_sems"], (0,), (place.mate, place.part))
        relay.start()
        s["cross_out"][...] = s["tot"][pl.ds(pl.multiple_of((halves + place.odd) * 16, 16), 16), :].astype(BF16)
        crossing = [
            remote(s["cross_out"], s["cross_in"].at[j], s["cross_sems"], (j,), (place.cross, other))
            for j, other in enumerate(place.others)
        ]

        @pl.when(place.exists)
        def _():
            for copy in crossing[::-1]:
                copy.start()

        odd = place.odd == 1
        near_send = jnp.where(odd, lo_ref[...], hi_ref[...])
        far_send = jnp.where(odd, hi_ref[...], lo_ref[...])
        near_slots = slots_of(near_send, 0, own)
        relay.wait()
        near_part = deliver(s["relay_in"][...], near_slots)
        for h in range(halves):
            s["tot_out"][h] = (
                s["tot"][h * 16 : (h + 1) * 16, :] + near_part[:, h * LANES : (h + 1) * LANES]
            ).astype(BF16)
        totals = [
            remote(
                s["tot_out"].at[other * share // LANES], s["tot_in"].at[j], s["tot_sems"], (j,), (place.brick, other)
            )
            for j, other in enumerate(place.others)
            if j
        ]
        for copy in totals:
            copy.start()
        vec = s["vec_out"][pl.ds(pl.multiple_of(place.part * share, share), share), :].astype(F32)
        for copy in vectors:
            copy.wait()
        for j in range(1, parts):
            vec = vec + s["vec_in"][j].astype(F32)
        variances = lax.dot_general(
            jnp.ones((16, rank), F32), vec * vec, NT, precision=lax.Precision.HIGHEST, preferred_element_type=F32
        )
        half = place.part * share // LANES
        far_slots = slots_of(far_send, half * LANES, LANES)
        mine = s["tot_out"][half].astype(F32)
        for copy in totals:
            copy.wait()
        for j in range(1, parts):
            mine = mine + s["tot_in"][j].astype(F32)

        @pl.when(place.exists)
        def _():
            for copy in crossing:
                copy.wait()

        ghosts = s["cross_in"][0].astype(F32)
        for j in range(1, parts):
            ghosts = ghosts + s["cross_in"][j].astype(F32)
        mine = mine + deliver(ghosts, far_slots)
        shift = lax.rem(LANES - lax.rem(place.part * share, LANES), LANES)
        out_ref[...] = pltpu.roll(mine, shift, 1)
        out_ref[10:11, :share] = variances[10:11]

    anywhere = pl.BlockSpec(memory_space=pltpu.HBM)
    return pl.pallas_call(
        kernel,
        out_shape=jax.ShapeDtypeStruct((16, LANES), F32),
        in_specs=[anywhere] * len(inputs),
        out_specs=pl.BlockSpec(memory_space=pltpu.VMEM),
        scratch_shapes=local + list(names.values()),
        compiler_params=pltpu.CompilerParams(
            vmem_limit_bytes=60 * 1024 * 1024, collective_id=0, has_side_effects=True
        ),
        name="brick",
    )(*inputs)


def split(result, share):
    def kernel(result_ref, force_ref, energy_ref, variance_ref, virial_ref):
        force_ref[...] = result_ref[0:3, :share]
        virial_ref[...] = result_ref[3:9, :share]
        energy_ref[...] = result_ref[9:10, :share]
        variance_ref[...] = result_ref[10:11, :share]

    vmem = pl.BlockSpec(memory_space=pltpu.VMEM)
    return pl.pallas_call(
        kernel,
        out_shape=tuple(jax.ShapeDtypeStruct((n, share), F32) for n in (3, 1, 1, 6)),
        in_specs=[vmem],
        out_specs=(vmem,) * 4,
        name="split",
    )(result)


def shards(
    positions, species, live_count, neighbors, neighbor_mask, send_lo, send_hi, sparse_desc, alpha, var_factor
):
    parts = lax.axis_size("sparse")
    result = brick(
        positions,
        species[None],
        live_count[None],
        neighbors,
        neighbor_mask,
        send_lo[None],
        send_hi[None],
        sparse_desc,
        alpha.reshape(-1, LANES),
        var_factor,
        parts,
    )
    forces, energies, variances, virials = split(result, positions.shape[1] // parts)
    return forces, energies[0], variances[0], virials


def solution(mesh):
    return jax.shard_map(
        shards,
        mesh=mesh,
        in_specs=(
            P(None, "space"),
            P("space"),
            P("space"),
            P(None, "space"),
            P(None, "space"),
            P("space"),
            P("space"),
            P("sparse", None),
            P("sparse"),
            P("sparse", None),
        ),
        out_specs=(
            P(None, ("space", "sparse")),
            P(("space", "sparse")),
            P(("space", "sparse")),
            P(None, ("space", "sparse")),
        ),
        check_vma=False,
    )
```

```python
import jax
import jax.numpy as jnp
from jax import lax
from jax.experimental import pallas as pl
from jax.experimental.pallas import tpu as pltpu
from jax.sharding import PartitionSpec as P

EPS = 1e-6
F32, BF16 = jnp.float32, jnp.bfloat16
SPECIES, RADIAL = 4, 4
K = SPECIES * RADIAL
LANES = 128
LOW = 64
RATES = tuple(scale * 2.0**r for scale in (0.1, 0.15) for r in range(RADIAL))
ORDERS = ((0, 1), (1, 4), (4, 10))
FOLD = (1.0,) * 7 + (2.0,) * 3
PAIRS = ((0, 0), (1, 1), (2, 2), (0, 1), (0, 2), (1, 2))
NT = (((1,), (1,)), ((), ()))


def angular(radial, o):
    first = [radial * o[p] for p in range(3)]
    return [radial] + first + [first[a] * o[b] for a, b in PAIRS]


def along(start, size):
    return pl.ds(pl.multiple_of(start, size), size)


def norms(sparse_ref, alpha_ref, scale_ref, first, last, chunk=512):
    depth = sparse_ref.shape[1]
    ones = jnp.ones((8, LANES), BF16)
    row = lax.broadcasted_iota(jnp.int32, (8, chunk), 0)
    per = chunk // LANES
    for t in range(first, last):
        raw = sparse_ref[t * chunk : (t + 1) * chunk, :]
        parts = [raw[:, j * LANES : (j + 1) * LANES] for j in range(depth // LANES)]
        parts = [part * part for part in parts]
        while len(parts) > 1:
            parts = [x + y for x, y in zip(parts[::2], parts[1::2])] + parts[len(parts) // 2 * 2 :]
        squares = lax.dot_general(ones, parts[0], NT, preferred_element_type=F32)
        inverse = 1.0 / (squares + EPS)
        alpha = jnp.concatenate([alpha_ref[t * per + j : t * per + j + 1, :] for j in range(per)], axis=1)
        scale_ref[:, t * chunk : (t + 1) * chunk] = inverse * jnp.where(row == 0, 1.0, 2.0 * alpha)


def pick_from(table_ref, first, last, low, high, value, rows):
    picked = []
    for c in range(4):
        got = value[c]
        for t in range(first, last):
            source = jnp.broadcast_to(table_ref[c : c + 1, t * LANES : (t + 1) * LANES], (rows, LANES))
            part = jnp.take_along_axis(source, low, axis=1, mode="promise_in_bounds")
            got = part if got is None else jnp.where(high == t, part, got)
        picked.append(got)
    return picked


def own_setup(table_ref, nb_ref, pick_ref):
    halves, _, count, _ = pick_ref.shape
    blocks = count // 8

    def step(i, _):
        h, b = i // blocks, i % blocks
        rows = along(b * 8, 8)
        index = nb_ref[rows, along(h * LANES, LANES)]
        values = pick_from(table_ref, 0, halves, index & (LANES - 1), index // LANES, [None] * 4, 8)
        for c in range(4):
            pick_ref[h, c, rows, :] = values[c]
        return 0

    lax.fori_loop(0, halves * blocks, step, 0, unroll=8)


def pair_setup(table_ref, pos_ref, nb_ref, mask_ref, live, pick_ref, off_ref, w_ref, kind_ref, r_ref):
    own = pos_ref.shape[1]
    halves = own // LANES
    tables = table_ref.shape[1] // LANES
    blocks = nb_ref.shape[0] // 8
    lane = lax.broadcasted_iota(jnp.int32, (8, LANES), 1)

    def step(i, _):
        h, b = i // blocks, i % blocks
        rows, cols = along(b * 8, 8), along(h * LANES, LANES)
        index = nb_ref[rows, cols]
        held = [pick_ref[h, c, rows, :] for c in range(4)]
        picked = pick_from(table_ref, halves, tables, index & (LANES - 1), index // LANES, held, 8)
        o = [picked[p] - pos_ref[p : p + 1, cols] for p in range(3)]
        alive = ((index >= own) | (index < live)) & (h * LANES + lane < live)
        valid = jnp.where(alive, mask_ref[rows, cols].astype(F32), 0.0)
        for p in range(3):
            off_ref[h, p, rows, :] = o[p]
        for s in range(SPECIES - 1):
            w_ref[h, s, rows, :] = jnp.where(picked[3] == s, 1.0, 0.0)
        kind_ref[h, rows, :] = picked[3].astype(jnp.int32)
        square = o[0] * o[0] + o[1] * o[1] + o[2] * o[2]
        for e in range(2):
            radial = jnp.exp(square * (-RATES[e * RADIAL]))
            for r in range(RADIAL):
                if r:
                    radial = radial * radial
                r_ref[h, e * RADIAL + r, rows, :] = radial * valid
        return 0

    lax.fori_loop(0, halves * blocks, step, 0, unroll=8)


def moments(off_ref, w_ref, r_ref, acc_ref, m_ref, mc_ref):
    halves, _, count, _ = off_ref.shape

    def fold(i, ms):
        for m in ms:
            value = acc_ref[i * 10 + m, pl.ds(0, K, stride=8), :]
            for j in range(1, 8):
                value = value + acc_ref[i * 10 + m, pl.ds(j, K, stride=8), :]
            m_ref[i * 10 + m] = value
            mc_ref[i * 10 + m] = value * FOLD[m]

    def step(i, before):
        h, e = i // 2, i % 2
        for r in range(RADIAL):
            total = [[None] * 10 for _ in range(SPECIES)]
            for b in range(count // 8):
                rows = slice(b * 8, b * 8 + 8)
                v = angular(r_ref[h, e * RADIAL + r, rows, :], [off_ref[h, p, rows, :] for p in range(3)])
                for s in range(SPECIES):
                    weight = w_ref[h, s, rows, :] if s < SPECIES - 1 else None
                    for m in range(10):
                        term = v[m] if weight is None else weight * v[m]
                        total[s][m] = term if b == 0 else total[s][m] + term
            if before is not None:
                fold(before, range(r * 10 // RADIAL, (r + 1) * 10 // RADIAL))
            for m in range(10):
                total[3][m] = total[3][m] - (total[0][m] + total[1][m] + total[2][m])
                for s in range(SPECIES):
                    acc_ref[i * 10 + m, (s * RADIAL + r) * 8 : (s * RADIAL + r) * 8 + 8, :] = total[s][m]

    for i in range(halves * 2):
        step(i, i - 1 if i else None)
    fold(halves * 2 - 1, range(10))


def descriptors(m_ref, mc_ref, d_ref, rinv_ref, desc_ref, plain_ref):
    halves = d_ref.shape[0]

    def step(k, squares):
        fresh = []
        for h in range(halves):
            base = h * 20
            total = squares[h]
            for l, (start, stop) in enumerate(ORDERS):
                value = None
                for m in range(start, stop):
                    term = m_ref[base + m, pl.ds(k, 1), :] * mc_ref[base + 10 + m]
                    value = term if value is None else value + term
                d_ref[h, along(l * K * K + k * K, K), :] = value
                total = total + value * value
            fresh.append(total)
        return tuple(fresh)

    squares = lax.fori_loop(0, K, step, (jnp.zeros((K, LANES), F32),) * halves, unroll=8)
    for h in range(halves):
        rinv = lax.rsqrt(jnp.sum(squares[h], axis=0, keepdims=True) + EPS)
        rinv_ref[h] = jnp.broadcast_to(rinv, (8, LANES))
        unit = (d_ref[h] * rinv).astype(BF16)
        desc_ref[h * LANES : (h + 1) * LANES, :] = lax.dot_general(
            plain_ref[...], unit, NT, preferred_element_type=F32
        ).astype(BF16)


def kernel_sums(desc_ref, sparse_ref, scale_ref, factor_ref, grad_ref, vec_ref, energy_ref):
    raw = sparse_ref[...]
    projection = lax.dot_general(desc_ref[...], raw, NT, preferred_element_type=F32)
    coefficient = projection * scale_ref[1:2, :]
    kernel = projection * projection * scale_ref[0:1, :]
    energy_terms = coefficient * projection
    energy = energy_terms[:, :LANES]
    for j in range(1, raw.shape[0] // LANES):
        energy = energy + energy_terms[:, j * LANES : (j + 1) * LANES]
    energy_ref[...] = energy
    grad_ref[...] = jnp.dot(coefficient.astype(BF16), raw, preferred_element_type=F32)
    vec_ref[...] = jnp.dot(kernel.astype(BF16), factor_ref[...], preferred_element_type=F32)


def moment_grads(grad_ref, desc_ref, eye_ref, gd_ref, gt_ref, mc_ref, rinv_ref, g_ref):
    halves = gt_ref.shape[0]
    unit = desc_ref[...].astype(F32)
    grad = grad_ref[...]
    along_unit = jnp.sum(grad * unit, axis=1, keepdims=True)
    gd_ref[...] = (grad - unit * along_unit).astype(BF16)
    for l in range(3):
        turned = lax.dot_general(
            eye_ref[...], gd_ref[:, l * K * K : (l + 1) * K * K], NT, preferred_element_type=F32
        )
        for h in range(halves):
            gt_ref[h, l] = turned[:, h * LANES : (h + 1) * LANES]

    def step(i, _):
        h, e = i // 2, i % 2
        rinv = rinv_ref[h, 0:1, :]
        for l, (start, stop) in enumerate(ORDERS):
            total = [None] * 10
            for j in range(K):
                block = gt_ref[h, l, along((1 - e) * K * K + j * K, K), :]
                for m in range(start, stop):
                    term = block * mc_ref[h * 20 + (1 - e) * 10 + m, j : j + 1, :]
                    total[m] = term if j == 0 else total[m] + term
            for m in range(start, stop):
                g_ref[i * 10 + m] = total[m] * rinv
        return 0

    lax.fori_loop(0, halves * 2, step, 0)


def pair_terms(off_ref, kind_ref, r_ref, g_ref, t_ref, own_ref, group=2):
    halves, _, count, _ = off_ref.shape
    blocks = count // 8 // group
    own_ref[...] = jnp.zeros(own_ref.shape, F32)

    def step(i, _):
        h, b = i // blocks, i % blocks
        rows = [along((b * group + q) * 8, 8) for q in range(group)]
        o = [[off_ref[h, p, rows[q], :] for p in range(3)] for q in range(group)]
        ang = [[None] + o[q] + [o[q][x] * o[q][y] for x, y in PAIRS] for q in range(group)]
        kind = [kind_ref[h, rows[q], :] for q in range(group)]
        which = [[kind[q], kind[q] + SPECIES] for q in range(group)]
        top = [[None] * 10 for _ in range(group)]
        slope = [None] * group
        for er, rate in enumerate(RATES):
            e, r = er // RADIAL, er % RADIAL
            radial = [r_ref[h, er, rows[q], :] for q in range(group)]
            inner = [None] * group
            for m in range(10):
                g = g_ref[(h * 2 + e) * 10 + m, r // 2 * 8 : r // 2 * 8 + 8, :]
                for q in range(group):
                    pick = jnp.take_along_axis(g, which[q][r % 2], axis=0, mode="promise_in_bounds")
                    if m == 0:
                        inner[q] = pick
                    else:
                        inner[q] = inner[q] + pick * ang[q][m]
                        term = radial[q] * pick
                        top[q][m] = term if er == 0 else top[q][m] + term
            for q in range(group):
                term = (radial[q] * (-rate)) * inner[q]
                slope[q] = term if er == 0 else slope[q] + term
        sums = [None] * 9
        for q in range(group):
            x, y, z = o[q]
            t = top[q]
            gx = t[1] + 2.0 * x * (t[4] + slope[q]) + t[7] * y + t[8] * z
            gy = t[2] + 2.0 * y * (t[5] + slope[q]) + t[7] * x + t[9] * z
            gz = t[3] + 2.0 * z * (t[6] + slope[q]) + t[8] * x + t[9] * y
            g = [gx, gy, gz]
            terms = [-v for v in g] + [-0.5 * o[q][a] * g[c] for a, c in PAIRS]
            for c in range(9):
                t_ref[h, along(c * count + (b * group + q) * 8, 8), :] = terms[c]
                sums[c] = terms[c] if q == 0 else sums[c] + terms[c]
        for c in range(9):
            own_ref[h, c * 8 : c * 8 + 8, :] += -sums[c] if c < 3 else sums[c]
        return 0

    lax.fori_loop(0, halves * blocks, step, 0)


def scatter(nb_ref, hot_ref, t_ref, own_ref, energy_ref, tot_ref, unroll=32):
    count, own = nb_ref.shape
    halves = own // LANES
    tables = tot_ref.shape[0] // 16
    groups = tables * LANES // LOW
    per = LANES // LOW
    row = lax.broadcasted_iota(jnp.int32, (8, own), 0)

    def step(i, total):
        left, right = [], []
        for u in range(unroll):
            n = i * unroll + u
            index = nb_ref[pl.ds(n, 1), :]
            high = jnp.broadcast_to(index // LOW, (8, own))
            eight = jnp.concatenate([t_ref[h, pl.ds(n, 8, stride=count), :] for h in range(halves)], axis=1)
            ninth = jnp.concatenate([t_ref[h, pl.ds(8 * count + n, 1), :] for h in range(halves)], axis=1)
            masked = [jnp.where(high == g, eight, 0.0) for g in range(groups)]
            masked += [jnp.where(high == row, ninth, 0.0), jnp.zeros((8, own), F32)]
            left.append(jnp.concatenate(masked, axis=0).astype(BF16))
            right.append(hot_ref[n])
        return total + lax.dot_general(
            jnp.concatenate(left, axis=1), jnp.concatenate(right, axis=1), NT, preferred_element_type=F32
        )

    total = lax.fori_loop(0, count // unroll, step, jnp.zeros((groups * 8 + 16, LOW), F32))
    energies = 0.5 * lax.dot_general(
        jnp.ones((16, LANES), F32), energy_ref[...], NT, precision=lax.Precision.HIGHEST, preferred_element_type=F32
    )
    row = lax.broadcasted_iota(jnp.int32, (8, LANES), 0)
    for t in range(tables):
        main = jnp.concatenate([total[(t * per + g) * 8 : (t * per + g + 1) * 8] for g in range(per)], axis=1)
        last = jnp.concatenate(
            [total[groups * 8 + t * per + g : groups * 8 + t * per + g + 1] for g in range(per)], axis=1
        )
        rest = jnp.where(row == 0, last, 0.0)
        if t < halves:
            mine = own_ref[t, pl.ds(0, 16, stride=8), :]
            for j in range(1, 8):
                mine = mine + own_ref[t, pl.ds(j, 16, stride=8), :]
            main = main + mine[:8]
            rest = rest + jnp.where(row == 1, energies[:8, t * LANES : (t + 1) * LANES], mine[8:])
        tot_ref[t * 16 : t * 16 + 8, :] = main
        tot_ref[t * 16 + 8 : t * 16 + 16, :] = rest


def one_hots(nb_ref, hot_ref):
    count, own = nb_ref.shape
    slot = lax.broadcasted_iota(jnp.int32, (LOW, own), 0)

    def step(n, _):
        low = nb_ref[pl.ds(n, 1), :] & (LOW - 1)
        hot_ref[n] = jnp.where(slot == low, 1.0, 0.0).astype(BF16)
        return 0

    lax.fori_loop(0, count, step, 0, unroll=4)


def identities(plain_ref, eye_ref):
    size = K * K
    row = lax.broadcasted_iota(jnp.int32, (size, size), 0)
    col = lax.broadcasted_iota(jnp.int32, (size, size), 1)
    plain_ref[...] = jnp.where(row[:LANES, :LANES] == col[:LANES, :LANES], 1.0, 0.0).astype(BF16)
    outer = row // K
    inner = row % SPECIES * RADIAL + row % K // SPECIES
    eye_ref[:size, :] = jnp.where(outer * K + inner == col, 1.0, 0.0).astype(BF16)
    eye_ref[size:, :] = jnp.where(inner * K + outer == col, 1.0, 0.0).astype(BF16)


def scratch_shapes(own, count, width, sparse, depth, rank):
    halves = own // LANES
    return dict(
        off=pltpu.VMEM((halves, 3, count, LANES), F32),
        pick=pltpu.VMEM((halves, 4, count, LANES), F32),
        plain=pltpu.VMEM((LANES, LANES), BF16),
        w=pltpu.VMEM((halves, SPECIES - 1, count, LANES), F32),
        kind=pltpu.VMEM((halves, count, LANES), jnp.int32),
        r=pltpu.VMEM((halves, len(RATES), count, LANES), F32),
        acc=pltpu.VMEM((halves * 20, K * 8, LANES), F32),
        m=pltpu.VMEM((halves * 20, K, LANES), F32),
        mc=pltpu.VMEM((halves * 20, K, LANES), F32),
        d=pltpu.VMEM((halves, depth, LANES), F32),
        rinv=pltpu.VMEM((halves, 8, LANES), F32),
        desc=pltpu.VMEM((own, depth), BF16),
        eye=pltpu.VMEM((2 * K * K, K * K), BF16),
        scale=pltpu.VMEM((8, sparse), F32),
        grad=pltpu.VMEM((own, depth), F32),
        energy=pltpu.VMEM((own, LANES), F32),
        gd=pltpu.VMEM((own, depth), BF16),
        gt=pltpu.VMEM((halves, 3, 2 * K * K, LANES), F32),
        g=pltpu.VMEM((halves * 20, K, LANES), F32),
        t=pltpu.VMEM((halves, 9 * count, LANES), F32),
        own=pltpu.VMEM((halves, 16 * 8, LANES), F32),
        hot=pltpu.VMEM((count, LOW, own), BF16),
    )


MESH = pl.DeviceIdType.MESH


def remote(source, target, sems, slot, device):
    return pltpu.make_async_remote_copy(
        src_ref=source,
        dst_ref=target,
        send_sem=sems.at[(0, *slot)],
        recv_sem=sems.at[(1, *slot)],
        device_id=device,
        device_id_type=MESH,
    )


class Place:
    def __init__(self):
        self.brick, self.part = lax.axis_index("space"), lax.axis_index("sparse")
        bricks, self.parts = lax.axis_size("space"), lax.axis_size("sparse")
        self.odd = lax.rem(self.brick, 2)
        self.mate = self.brick + 1 - 2 * self.odd
        self.exists = (self.brick > 0) & (self.brick < bricks - 1)
        self.cross = jnp.where(self.exists, self.brick - 1 + 2 * self.odd, self.mate)
        self.others = [lax.rem(self.part + j, self.parts) for j in range(self.parts)]

    def greet(self):
        barrier = pltpu.get_barrier_semaphore()

        def signal(device):
            pl.semaphore_signal(barrier, inc=1, device_id=device, device_id_type=MESH)

        signal((self.mate, self.part))

        @pl.when(self.exists)
        def _():
            for other in self.others:
                signal((self.cross, other))

        for other in self.others[1:]:
            signal((self.brick, other))

    def met(self):
        barrier = pltpu.get_barrier_semaphore()
        pl.semaphore_wait(barrier, jnp.where(self.exists, 2 * self.parts, self.parts))


def halo_pick(pos_ref, species_ref, send_refs, table_ref, face_ref):
    own = pos_ref.shape[1]
    table_ref[0:3, :own] = pos_ref[...]
    table_ref[3:4, :own] = species_ref[...].astype(F32)
    table_ref[4:8, :own] = jnp.zeros((4, own), F32)
    for f, send_ref in enumerate(send_refs):
        index = jnp.broadcast_to(send_ref[...], (8, LANES))
        low, high = index & (LANES - 1), index // LANES
        value = None
        for t in range(own // LANES):
            part = jnp.take_along_axis(
                table_ref[:, t * LANES : (t + 1) * LANES], low, axis=1, mode="promise_in_bounds"
            )
            value = part if value is None else jnp.where(high == t, part, value)
        face_ref[f] = value


def halo_place(rim_ref, table_ref, own, odd):
    mate, cross = rim_ref[0], rim_ref[1]
    table_ref[:, own : own + LANES] = jnp.where(odd == 1, mate, cross)
    table_ref[:, own + LANES : own + 2 * LANES] = jnp.where(odd == 1, cross, mate)


def deliver(ghosts, slots):
    high = ghosts.astype(BF16)
    low = (ghosts - high.astype(F32)).astype(BF16)
    both = lax.dot_general(jnp.concatenate([high, low], axis=0), slots, NT, preferred_element_type=F32)
    row = lax.broadcasted_iota(jnp.int32, (16, both.shape[1]), 0)
    return jnp.where(row < 9, both[:16] + both[16:], 0.0)


def slots_of(send, first, count):
    slot = first + lax.broadcasted_iota(jnp.int32, (count, LANES), 0)
    return jnp.where(slot == send, 1.0, 0.0).astype(BF16)


def brick(pos, species, nb, mask, send_lo, send_hi, sparse, alpha, factor, parts):
    own, count = pos.shape[1], nb.shape[0]
    depth, rank = sparse.shape[1], factor.shape[1]
    halves = own // LANES
    tables = halves + 2
    share = own // parts
    names = scratch_shapes(own, count, tables * LANES, sparse.shape[0], depth, rank)
    inputs = (pos, species, send_lo, send_hi, nb, mask, alpha, sparse, factor)
    names.update(
        table=pltpu.VMEM((8, tables * LANES), F32),
        face=pltpu.VMEM((2, 8, LANES), F32),
        rim=pltpu.VMEM((2, 8, LANES), F32),
        vec=pltpu.VMEM((own, rank), F32),
        tot=pltpu.VMEM((tables * 16, LANES), F32),
        vec_out=pltpu.VMEM((own, rank), BF16),
        vec_in=pltpu.VMEM((parts, share, rank), BF16),
        tot_out=pltpu.VMEM((halves, 16, LANES), BF16),
        tot_in=pltpu.VMEM((parts, 16, LANES), BF16),
        relay_out=pltpu.VMEM((16, LANES), F32),
        relay_in=pltpu.VMEM((16, LANES), F32),
        cross_out=pltpu.VMEM((16, LANES), BF16),
        cross_in=pltpu.VMEM((parts, 16, LANES), BF16),
        halo_sems=pltpu.SemaphoreType.DMA((2, 2)),
        relay_sems=pltpu.SemaphoreType.DMA((2, 1)),
        vec_sems=pltpu.SemaphoreType.DMA((2, parts)),
        tot_sems=pltpu.SemaphoreType.DMA((2, parts)),
        cross_sems=pltpu.SemaphoreType.DMA((2, parts)),
        load_sems=pltpu.SemaphoreType.DMA((len(inputs),)),
    )
    keys = list(names)
    local = [pltpu.VMEM(x.shape, x.dtype) for x in inputs]

    def kernel(*refs):
        sources, out_ref = refs[: len(inputs)], refs[len(inputs)]
        held = refs[len(inputs) + 1 : 2 * len(inputs) + 1]
        s = dict(zip(keys, refs[2 * len(inputs) + 1 :]))
        pos_ref, species_ref, lo_ref, hi_ref, nb_ref, mask_ref, alpha_ref, sparse_ref, factor_ref = held
        place = Place()
        place.greet()
        loads = [
            pltpu.make_async_copy(x, y, s["load_sems"].at[k])
            for k, (x, y) in enumerate(zip(sources, held))
        ]
        for load in loads:
            load.start()
        for load in loads[:4]:
            load.wait()
        halo_pick(pos_ref, species_ref, (lo_ref, hi_ref), s["table"], s["face"])
        place.met()
        near = remote(s["face"].at[1 - place.odd], s["rim"].at[0], s["halo_sems"], (0,), (place.mate, place.part))
        far = remote(s["face"].at[place.odd], s["rim"].at[1], s["halo_sems"], (1,), (place.cross, place.part))
        near.start()

        @pl.when(place.exists)
        def _():
            far.start()

        @pl.when(jnp.logical_not(place.exists))
        def _():
            s["rim"][1] = jnp.zeros((8, LANES), F32)
            for j in range(parts):
                s["cross_in"][j] = jnp.zeros((16, LANES), BF16)

        identities(s["plain"], s["eye"])
        for load in loads[4:]:
            load.wait()
        norms(sparse_ref, alpha_ref, s["scale"], 0, sparse.shape[0] // 512)
        own_setup(s["table"], nb_ref, s["pick"])
        one_hots(nb_ref, s["hot"])
        near.wait()

        @pl.when(place.exists)
        def _():
            far.wait()

        halo_place(s["rim"], s["table"], own, place.odd)
        live_row = jnp.broadcast_to(jnp.sum(mask_ref[0:1, :], axis=1, keepdims=True), (8, LANES))
        pair_setup(
            s["table"], pos_ref, nb_ref, mask_ref, live_row, s["pick"], s["off"], s["w"], s["kind"], s["r"]
        )
        moments(s["off"], s["w"], s["r"], s["acc"], s["m"], s["mc"])
        descriptors(s["m"], s["mc"], s["d"], s["rinv"], s["desc"], s["plain"])
        kernel_sums(s["desc"], sparse_ref, s["scale"], factor_ref, s["grad"], s["vec"], s["energy"])
        s["vec_out"][...] = s["vec"][...].astype(BF16)
        vectors = [
            remote(
                s["vec_out"].at[pl.ds(pl.multiple_of(other * share, share), share)],
                s["vec_in"].at[j],
                s["vec_sems"],
                (j,),
                (place.brick, other),
            )
            for j, other in enumerate(place.others)
            if j
        ]
        for copy in vectors:
            copy.start()
        moment_grads(s["grad"], s["desc"], s["eye"], s["gd"], s["gt"], s["mc"], s["rinv"], s["g"])
        pair_terms(s["off"], s["kind"], s["r"], s["g"], s["t"], s["own"])
        scatter(nb_ref, s["hot"], s["t"], s["own"], s["energy"], s["tot"])
        s["relay_out"][...] = s["tot"][pl.ds(pl.multiple_of((halves + 1 - place.odd) * 16, 16), 16), :]
        relay = remote(s["relay_out"], s["relay_in"], s["relay_sems"], (0,), (place.mate, place.part))
        relay.start()
        s["cross_out"][...] = s["tot"][pl.ds(pl.multiple_of((halves + place.odd) * 16, 16), 16), :].astype(BF16)
        crossing = [
            remote(s["cross_out"], s["cross_in"].at[j], s["cross_sems"], (j,), (place.cross, other))
            for j, other in enumerate(place.others)
        ]

        @pl.when(place.exists)
        def _():
            for copy in crossing[::-1]:
                copy.start()

        odd = place.odd == 1
        near_send = jnp.where(odd, lo_ref[...], hi_ref[...])
        far_send = jnp.where(odd, hi_ref[...], lo_ref[...])
        near_slots = slots_of(near_send, 0, own)
        relay.wait()
        near_part = deliver(s["relay_in"][...], near_slots)
        for h in range(halves):
            s["tot_out"][h] = (
                s["tot"][h * 16 : (h + 1) * 16, :] + near_part[:, h * LANES : (h + 1) * LANES]
            ).astype(BF16)
        totals = [
            remote(
                s["tot_out"].at[other * share // LANES], s["tot_in"].at[j], s["tot_sems"], (j,), (place.brick, other)
            )
            for j, other in enumerate(place.others)
            if j
        ]
        for copy in totals:
            copy.start()
        vec = s["vec_out"][pl.ds(pl.multiple_of(place.part * share, share), share), :].astype(F32)
        for copy in vectors:
            copy.wait()
        for j in range(1, parts):
            vec = vec + s["vec_in"][j].astype(F32)
        variances = lax.dot_general(
            jnp.ones((16, rank), F32), vec * vec, NT, precision=lax.Precision.HIGHEST, preferred_element_type=F32
        )
        half = place.part * share // LANES
        far_slots = slots_of(far_send, half * LANES, LANES)
        mine = s["tot_out"][half].astype(F32)
        for copy in totals:
            copy.wait()
        for j in range(1, parts):
            mine = mine + s["tot_in"][j].astype(F32)

        @pl.when(place.exists)
        def _():
            for copy in crossing:
                copy.wait()

        ghosts = s["cross_in"][0].astype(F32)
        for j in range(1, parts):
            ghosts = ghosts + s["cross_in"][j].astype(F32)
        mine = mine + deliver(ghosts, far_slots)
        shift = lax.rem(LANES - lax.rem(place.part * share, LANES), LANES)
        out_ref[...] = pltpu.roll(mine, shift, 1)
        out_ref[10:11, :share] = variances[10:11]

    anywhere = pl.BlockSpec(memory_space=pltpu.HBM)
    return pl.pallas_call(
        kernel,
        out_shape=jax.ShapeDtypeStruct((16, LANES), F32),
        in_specs=[anywhere] * len(inputs),
        out_specs=pl.BlockSpec(memory_space=pltpu.VMEM),
        scratch_shapes=local + list(names.values()),
        compiler_params=pltpu.CompilerParams(
            vmem_limit_bytes=60 * 1024 * 1024, collective_id=0, has_side_effects=True
        ),
        name="brick",
    )(*inputs)


def split(result, share):
    def kernel(result_ref, force_ref, energy_ref, variance_ref, virial_ref):
        force_ref[...] = result_ref[0:3, :share]
        virial_ref[...] = result_ref[3:9, :share]
        energy_ref[...] = result_ref[9:10, :share]
        variance_ref[...] = result_ref[10:11, :share]

    vmem = pl.BlockSpec(memory_space=pltpu.VMEM)
    return pl.pallas_call(
        kernel,
        out_shape=tuple(jax.ShapeDtypeStruct((n, share), F32) for n in (3, 1, 1, 6)),
        in_specs=[vmem],
        out_specs=(vmem,) * 4,
        name="split",
    )(result)


def shards(
    positions, species, live_count, neighbors, neighbor_mask, send_lo, send_hi, sparse_desc, alpha, var_factor
):
    parts = lax.axis_size("sparse")
    result = brick(
        positions,
        species[None],
        neighbors,
        neighbor_mask,
        send_lo[None],
        send_hi[None],
        sparse_desc,
        alpha.reshape(-1, LANES),
        var_factor,
        parts,
    )
    forces, energies, variances, virials = split(result, positions.shape[1] // parts)
    return forces, energies[0], variances[0], virials


def solution(mesh):
    return jax.shard_map(
        shards,
        mesh=mesh,
        in_specs=(
            P(None, "space"),
            P("space"),
            P("space"),
            P(None, "space"),
            P(None, "space"),
            P("space"),
            P("space"),
            P("sparse", None),
            P("sparse"),
            P("sparse", None),
        ),
        out_specs=(
            P(None, ("space", "sparse")),
            P(("space", "sparse")),
            P(("space", "sparse")),
            P(None, ("space", "sparse")),
        ),
        check_vma=False,
    )
```

```python
import jax
import jax.numpy as jnp
from jax import lax
from jax.experimental import pallas as pl
from jax.experimental.pallas import tpu as pltpu
from jax.sharding import PartitionSpec as P

EPS = 1e-6
F32, BF16 = jnp.float32, jnp.bfloat16
SPECIES, RADIAL = 4, 4
K = SPECIES * RADIAL
LANES = 128
LOW = 64
RATES = tuple(scale * 2.0**r for scale in (0.1, 0.15) for r in range(RADIAL))
ORDERS = ((0, 1), (1, 4), (4, 10))
FOLD = (1.0,) * 7 + (2.0,) * 3
PAIRS = ((0, 0), (1, 1), (2, 2), (0, 1), (0, 2), (1, 2))
NT = (((1,), (1,)), ((), ()))


def angular(radial, o):
    first = [radial * o[p] for p in range(3)]
    return [radial] + first + [first[a] * o[b] for a, b in PAIRS]


def along(start, size):
    return pl.ds(pl.multiple_of(start, size), size)


def norms(sparse_ref, alpha_ref, scale_ref, first, last, chunk=512):
    depth = sparse_ref.shape[1]
    ones = jnp.ones((8, LANES), BF16)
    row = lax.broadcasted_iota(jnp.int32, (8, chunk), 0)
    per = chunk // LANES
    for t in range(first, last):
        raw = sparse_ref[t * chunk : (t + 1) * chunk, :]
        parts = [raw[:, j * LANES : (j + 1) * LANES] for j in range(depth // LANES)]
        parts = [part * part for part in parts]
        while len(parts) > 1:
            parts = [x + y for x, y in zip(parts[::2], parts[1::2])] + parts[len(parts) // 2 * 2 :]
        squares = lax.dot_general(ones, parts[0], NT, preferred_element_type=F32)
        inverse = 1.0 / (squares + EPS)
        alpha = jnp.concatenate([alpha_ref[t * per + j : t * per + j + 1, :] for j in range(per)], axis=1)
        scale_ref[:, t * chunk : (t + 1) * chunk] = inverse * jnp.where(row == 0, 1.0, 2.0 * alpha)


def pick_from(table_ref, first, last, low, high, value, rows):
    picked = []
    for c in range(4):
        got = value[c]
        for t in range(first, last):
            source = jnp.broadcast_to(table_ref[c : c + 1, t * LANES : (t + 1) * LANES], (rows, LANES))
            part = jnp.take_along_axis(source, low, axis=1, mode="promise_in_bounds")
            got = part if got is None else jnp.where(high == t, part, got)
        picked.append(got)
    return picked


def own_setup(table_ref, nb_ref, pick_ref):
    halves, _, count, _ = pick_ref.shape
    blocks = count // 8

    def step(i, _):
        h, b = i // blocks, i % blocks
        rows = along(b * 8, 8)
        index = nb_ref[rows, along(h * LANES, LANES)]
        values = pick_from(table_ref, 0, halves, index & (LANES - 1), index // LANES, [None] * 4, 8)
        for c in range(4):
            pick_ref[h, c, rows, :] = values[c]
        return 0

    lax.fori_loop(0, halves * blocks, step, 0, unroll=8)


def pair_setup(table_ref, pos_ref, nb_ref, mask_ref, live, pick_ref, off_ref, w_ref, kind_ref, r_ref):
    own = pos_ref.shape[1]
    halves = own // LANES
    tables = table_ref.shape[1] // LANES
    blocks = nb_ref.shape[0] // 8
    lane = lax.broadcasted_iota(jnp.int32, (8, LANES), 1)

    def step(i, _):
        h, b = i // blocks, i % blocks
        rows, cols = along(b * 8, 8), along(h * LANES, LANES)
        index = nb_ref[rows, cols]
        held = [pick_ref[h, c, rows, :] for c in range(4)]
        picked = pick_from(table_ref, halves, tables, index & (LANES - 1), index // LANES, held, 8)
        o = [picked[p] - pos_ref[p : p + 1, cols] for p in range(3)]
        alive = ((index >= own) | (index < live)) & (h * LANES + lane < live)
        valid = jnp.where(alive, mask_ref[rows, cols].astype(F32), 0.0)
        for p in range(3):
            off_ref[h, p, rows, :] = o[p]
        for s in range(SPECIES - 1):
            w_ref[h, s, rows, :] = jnp.where(picked[3] == s, 1.0, 0.0)
        kind_ref[h, rows, :] = picked[3].astype(jnp.int32)
        square = o[0] * o[0] + o[1] * o[1] + o[2] * o[2]
        for e in range(2):
            radial = jnp.exp(square * (-RATES[e * RADIAL]))
            for r in range(RADIAL):
                if r:
                    radial = radial * radial
                r_ref[h, e * RADIAL + r, rows, :] = radial * valid
        return 0

    lax.fori_loop(0, halves * blocks, step, 0, unroll=8)


def moments(off_ref, w_ref, r_ref, acc_ref, m_ref, mc_ref):
    halves, _, count, _ = off_ref.shape

    def fold(i, ms):
        for m in ms:
            value = acc_ref[i * 10 + m, pl.ds(0, K, stride=8), :]
            for j in range(1, 8):
                value = value + acc_ref[i * 10 + m, pl.ds(j, K, stride=8), :]
            m_ref[i * 10 + m] = value
            mc_ref[i * 10 + m] = value * FOLD[m]

    def step(i, before):
        h, e = i // 2, i % 2
        for r in range(RADIAL):
            total = [[None] * 10 for _ in range(SPECIES)]
            for b in range(count // 8):
                rows = slice(b * 8, b * 8 + 8)
                v = angular(r_ref[h, e * RADIAL + r, rows, :], [off_ref[h, p, rows, :] for p in range(3)])
                for s in range(SPECIES):
                    weight = w_ref[h, s, rows, :] if s < SPECIES - 1 else None
                    for m in range(10):
                        term = v[m] if weight is None else weight * v[m]
                        total[s][m] = term if b == 0 else total[s][m] + term
            if before is not None:
                fold(before, range(r * 10 // RADIAL, (r + 1) * 10 // RADIAL))
            for m in range(10):
                total[3][m] = total[3][m] - (total[0][m] + total[1][m] + total[2][m])
                for s in range(SPECIES):
                    acc_ref[i * 10 + m, (s * RADIAL + r) * 8 : (s * RADIAL + r) * 8 + 8, :] = total[s][m]

    for i in range(halves * 2):
        step(i, i - 1 if i else None)
    fold(halves * 2 - 1, range(10))


def descriptors(m_ref, mc_ref, d_ref, rinv_ref, desc_ref, plain_ref):
    halves = d_ref.shape[0]

    def step(k, squares):
        fresh = []
        for h in range(halves):
            base = h * 20
            total = squares[h]
            for l, (start, stop) in enumerate(ORDERS):
                value = None
                for m in range(start, stop):
                    term = m_ref[base + m, pl.ds(k, 1), :] * mc_ref[base + 10 + m]
                    value = term if value is None else value + term
                d_ref[h, along(l * K * K + k * K, K), :] = value
                total = total + value * value
            fresh.append(total)
        return tuple(fresh)

    squares = lax.fori_loop(0, K, step, (jnp.zeros((K, LANES), F32),) * halves, unroll=8)
    for h in range(halves):
        rinv = lax.rsqrt(jnp.sum(squares[h], axis=0, keepdims=True) + EPS)
        rinv_ref[h] = jnp.broadcast_to(rinv, (8, LANES))
        unit = (d_ref[h] * rinv).astype(BF16)
        desc_ref[h * LANES : (h + 1) * LANES, :] = lax.dot_general(
            plain_ref[...], unit, NT, preferred_element_type=F32
        ).astype(BF16)


def kernel_sums(desc_ref, sparse_ref, scale_ref, factor_ref, grad_ref, vec_ref, energy_ref):
    raw = sparse_ref[...]
    projection = lax.dot_general(desc_ref[...], raw, NT, preferred_element_type=F32)
    coefficient = projection * scale_ref[1:2, :]
    kernel = projection * projection * scale_ref[0:1, :]
    energy_terms = coefficient * projection
    energy = energy_terms[:, :LANES]
    for j in range(1, raw.shape[0] // LANES):
        energy = energy + energy_terms[:, j * LANES : (j + 1) * LANES]
    energy_ref[...] = energy
    grad_ref[...] = jnp.dot(coefficient.astype(BF16), raw, preferred_element_type=F32)
    vec_ref[...] = jnp.dot(kernel.astype(BF16), factor_ref[...], preferred_element_type=F32)


def moment_grads(grad_ref, desc_ref, eye_ref, gd_ref, gt_ref, mc_ref, rinv_ref, g_ref):
    halves = gt_ref.shape[0]
    unit = desc_ref[...].astype(F32)
    grad = grad_ref[...]
    along_unit = jnp.sum(grad * unit, axis=1, keepdims=True)
    gd_ref[...] = (grad - unit * along_unit).astype(BF16)
    for l in range(3):
        turned = lax.dot_general(
            eye_ref[...], gd_ref[:, l * K * K : (l + 1) * K * K], NT, preferred_element_type=F32
        )
        for h in range(halves):
            gt_ref[h, l] = turned[:, h * LANES : (h + 1) * LANES]

    def step(i, _):
        h, e = i // 2, i % 2
        rinv = rinv_ref[h, 0:1, :]
        for l, (start, stop) in enumerate(ORDERS):
            total = [None] * 10
            for j in range(K):
                block = gt_ref[h, l, along((1 - e) * K * K + j * K, K), :]
                for m in range(start, stop):
                    term = block * mc_ref[h * 20 + (1 - e) * 10 + m, j : j + 1, :]
                    total[m] = term if j == 0 else total[m] + term
            for m in range(start, stop):
                g_ref[i * 10 + m] = total[m] * rinv
        return 0

    lax.fori_loop(0, halves * 2, step, 0)


def pair_terms(off_ref, kind_ref, r_ref, g_ref, t_ref, own_ref, group=2):
    halves, _, count, _ = off_ref.shape
    blocks = count // 8 // group
    own_ref[...] = jnp.zeros(own_ref.shape, F32)

    def step(i, _):
        h, b = i // blocks, i % blocks
        rows = [along((b * group + q) * 8, 8) for q in range(group)]
        o = [[off_ref[h, p, rows[q], :] for p in range(3)] for q in range(group)]
        ang = [[None] + o[q] + [o[q][x] * o[q][y] for x, y in PAIRS] for q in range(group)]
        kind = [kind_ref[h, rows[q], :] for q in range(group)]
        which = [[kind[q], kind[q] + SPECIES] for q in range(group)]
        top = [[None] * 10 for _ in range(group)]
        slope = [None] * group
        for er, rate in enumerate(RATES):
            e, r = er // RADIAL, er % RADIAL
            radial = [r_ref[h, er, rows[q], :] for q in range(group)]
            inner = [None] * group
            for m in range(10):
                g = g_ref[(h * 2 + e) * 10 + m, r // 2 * 8 : r // 2 * 8 + 8, :]
                for q in range(group):
                    pick = jnp.take_along_axis(g, which[q][r % 2], axis=0, mode="promise_in_bounds")
                    if m == 0:
                        inner[q] = pick
                    else:
                        inner[q] = inner[q] + pick * ang[q][m]
                        term = radial[q] * pick
                        top[q][m] = term if er == 0 else top[q][m] + term
            for q in range(group):
                term = (radial[q] * (-rate)) * inner[q]
                slope[q] = term if er == 0 else slope[q] + term
        sums = [None] * 9
        for q in range(group):
            x, y, z = o[q]
            t = top[q]
            gx = t[1] + 2.0 * x * (t[4] + slope[q]) + t[7] * y + t[8] * z
            gy = t[2] + 2.0 * y * (t[5] + slope[q]) + t[7] * x + t[9] * z
            gz = t[3] + 2.0 * z * (t[6] + slope[q]) + t[8] * x + t[9] * y
            g = [gx, gy, gz]
            terms = [-v for v in g] + [-0.5 * o[q][a] * g[c] for a, c in PAIRS]
            for c in range(9):
                t_ref[h, along(c * count + (b * group + q) * 8, 8), :] = terms[c]
                sums[c] = terms[c] if q == 0 else sums[c] + terms[c]
        for c in range(9):
            own_ref[h, c * 8 : c * 8 + 8, :] += -sums[c] if c < 3 else sums[c]
        return 0

    lax.fori_loop(0, halves * blocks, step, 0)


def scatter(nb_ref, hot_ref, t_ref, own_ref, energy_ref, tot_ref, unroll=32):
    count, own = nb_ref.shape
    halves = own // LANES
    tables = tot_ref.shape[0] // 16
    groups = tables * LANES // LOW
    per = LANES // LOW
    row = lax.broadcasted_iota(jnp.int32, (8, own), 0)

    def step(i, total):
        left, right = [], []
        for u in range(unroll):
            n = i * unroll + u
            index = nb_ref[pl.ds(n, 1), :]
            high = jnp.broadcast_to(index // LOW, (8, own))
            eight = jnp.concatenate([t_ref[h, pl.ds(n, 8, stride=count), :] for h in range(halves)], axis=1)
            ninth = jnp.concatenate([t_ref[h, pl.ds(8 * count + n, 1), :] for h in range(halves)], axis=1)
            masked = [jnp.where(high == g, eight, 0.0) for g in range(groups)]
            masked += [jnp.where(high == row, ninth, 0.0), jnp.zeros((8, own), F32)]
            left.append(jnp.concatenate(masked, axis=0).astype(BF16))
            right.append(hot_ref[n])
        return total + lax.dot_general(
            jnp.concatenate(left, axis=1), jnp.concatenate(right, axis=1), NT, preferred_element_type=F32
        )

    total = lax.fori_loop(0, count // unroll, step, jnp.zeros((groups * 8 + 16, LOW), F32))
    energies = 0.5 * lax.dot_general(
        jnp.ones((16, LANES), F32), energy_ref[...], NT, precision=lax.Precision.HIGHEST, preferred_element_type=F32
    )
    row = lax.broadcasted_iota(jnp.int32, (8, LANES), 0)
    for t in range(tables):
        main = jnp.concatenate([total[(t * per + g) * 8 : (t * per + g + 1) * 8] for g in range(per)], axis=1)
        last = jnp.concatenate(
            [total[groups * 8 + t * per + g : groups * 8 + t * per + g + 1] for g in range(per)], axis=1
        )
        rest = jnp.where(row == 0, last, 0.0)
        if t < halves:
            mine = own_ref[t, pl.ds(0, 16, stride=8), :]
            for j in range(1, 8):
                mine = mine + own_ref[t, pl.ds(j, 16, stride=8), :]
            main = main + mine[:8]
            rest = rest + jnp.where(row == 1, energies[:8, t * LANES : (t + 1) * LANES], mine[8:])
        tot_ref[t * 16 : t * 16 + 8, :] = main
        tot_ref[t * 16 + 8 : t * 16 + 16, :] = rest


def one_hots(nb_ref, hot_ref):
    count, own = nb_ref.shape
    slot = lax.broadcasted_iota(jnp.int32, (LOW, own), 0)

    def step(n, _):
        low = nb_ref[pl.ds(n, 1), :] & (LOW - 1)
        hot_ref[n] = jnp.where(slot == low, 1.0, 0.0).astype(BF16)
        return 0

    lax.fori_loop(0, count, step, 0, unroll=4)


def identities(plain_ref, eye_ref):
    size = K * K
    row = lax.broadcasted_iota(jnp.int32, (size, size), 0)
    col = lax.broadcasted_iota(jnp.int32, (size, size), 1)
    plain_ref[...] = jnp.where(row[:LANES, :LANES] == col[:LANES, :LANES], 1.0, 0.0).astype(BF16)
    outer = row // K
    inner = row % SPECIES * RADIAL + row % K // SPECIES
    eye_ref[:size, :] = jnp.where(outer * K + inner == col, 1.0, 0.0).astype(BF16)
    eye_ref[size:, :] = jnp.where(inner * K + outer == col, 1.0, 0.0).astype(BF16)


def scratch_shapes(own, count, width, sparse, depth, rank):
    halves = own // LANES
    return dict(
        off=pltpu.VMEM((halves, 3, count, LANES), F32),
        pick=pltpu.VMEM((halves, 4, count, LANES), F32),
        plain=pltpu.VMEM((LANES, LANES), BF16),
        w=pltpu.VMEM((halves, SPECIES - 1, count, LANES), F32),
        kind=pltpu.VMEM((halves, count, LANES), jnp.int32),
        r=pltpu.VMEM((halves, len(RATES), count, LANES), F32),
        acc=pltpu.VMEM((halves * 20, K * 8, LANES), F32),
        m=pltpu.VMEM((halves * 20, K, LANES), F32),
        mc=pltpu.VMEM((halves * 20, K, LANES), F32),
        d=pltpu.VMEM((halves, depth, LANES), F32),
        rinv=pltpu.VMEM((halves, 8, LANES), F32),
        desc=pltpu.VMEM((own, depth), BF16),
        eye=pltpu.VMEM((2 * K * K, K * K), BF16),
        scale=pltpu.VMEM((8, sparse), F32),
        grad=pltpu.VMEM((own, depth), F32),
        energy=pltpu.VMEM((own, LANES), F32),
        gd=pltpu.VMEM((own, depth), BF16),
        gt=pltpu.VMEM((halves, 3, 2 * K * K, LANES), F32),
        g=pltpu.VMEM((halves * 20, K, LANES), F32),
        t=pltpu.VMEM((halves, 9 * count, LANES), F32),
        own=pltpu.VMEM((halves, 16 * 8, LANES), F32),
        hot=pltpu.VMEM((count, LOW, own), BF16),
    )


MESH = pl.DeviceIdType.MESH


def remote(source, target, sems, slot, device):
    return pltpu.make_async_remote_copy(
        src_ref=source,
        dst_ref=target,
        send_sem=sems.at[(0, *slot)],
        recv_sem=sems.at[(1, *slot)],
        device_id=device,
        device_id_type=MESH,
    )


class Place:
    def __init__(self):
        self.brick, self.part = lax.axis_index("space"), lax.axis_index("sparse")
        bricks, self.parts = lax.axis_size("space"), lax.axis_size("sparse")
        self.odd = lax.rem(self.brick, 2)
        self.mate = self.brick + 1 - 2 * self.odd
        self.exists = (self.brick > 0) & (self.brick < bricks - 1)
        self.cross = jnp.where(self.exists, self.brick - 1 + 2 * self.odd, self.mate)
        self.others = [lax.rem(self.part + j, self.parts) for j in range(self.parts)]

    def greet(self):
        barrier = pltpu.get_barrier_semaphore()

        def signal(device):
            pl.semaphore_signal(barrier, inc=1, device_id=device, device_id_type=MESH)

        @pl.when(self.exists)
        def _():
            signal((self.cross, self.part))

        signal((self.mate, self.part))
        for other in self.others[1:]:
            signal((self.brick, other))

    def met(self):
        barrier = pltpu.get_barrier_semaphore()
        pl.semaphore_wait(barrier, jnp.where(self.exists, self.parts + 1, self.parts))

    def tell(self, semaphore):
        for other in self.others[1:]:
            pl.semaphore_signal(semaphore, inc=1, device_id=(self.brick, other), device_id_type=MESH)

    def told(self, semaphore):
        pl.semaphore_wait(semaphore, self.parts - 1)


def halo_pick(pos_ref, species_ref, send_refs, table_ref, face_ref):
    own = pos_ref.shape[1]
    table_ref[0:3, :own] = pos_ref[...]
    table_ref[3:4, :own] = species_ref[...].astype(F32)
    table_ref[4:8, :own] = jnp.zeros((4, own), F32)
    for f, send_ref in enumerate(send_refs):
        index = jnp.broadcast_to(send_ref[...], (8, LANES))
        low, high = index & (LANES - 1), index // LANES
        value = None
        for t in range(own // LANES):
            part = jnp.take_along_axis(
                table_ref[:, t * LANES : (t + 1) * LANES], low, axis=1, mode="promise_in_bounds"
            )
            value = part if value is None else jnp.where(high == t, part, value)
        face_ref[f] = value


def halo_place(rim_ref, table_ref, own, odd):
    mate, cross = rim_ref[0], rim_ref[1]
    table_ref[:, own : own + LANES] = jnp.where(odd == 1, mate, cross)
    table_ref[:, own + LANES : own + 2 * LANES] = jnp.where(odd == 1, cross, mate)


def deliver(ghosts, slots):
    high = ghosts.astype(BF16)
    low = (ghosts - high.astype(F32)).astype(BF16)
    both = lax.dot_general(jnp.concatenate([high, low], axis=0), slots, NT, preferred_element_type=F32)
    row = lax.broadcasted_iota(jnp.int32, (16, both.shape[1]), 0)
    return jnp.where(row < 9, both[:16] + both[16:], 0.0)


def slots_of(send, first, count):
    slot = first + lax.broadcasted_iota(jnp.int32, (count, LANES), 0)
    return jnp.where(slot == send, 1.0, 0.0).astype(BF16)


def brick(pos, species, nb, mask, send_lo, send_hi, sparse, alpha, factor, parts):
    own, count = pos.shape[1], nb.shape[0]
    depth, rank = sparse.shape[1], factor.shape[1]
    halves = own // LANES
    tables = halves + 2
    share = own // parts
    names = scratch_shapes(own, count, tables * LANES, sparse.shape[0], depth, rank)
    inputs = (pos, species, send_lo, send_hi, nb, mask, alpha, sparse, factor)
    names.update(
        table=pltpu.VMEM((8, tables * LANES), F32),
        face=pltpu.VMEM((2, 8, LANES), F32),
        rim=pltpu.VMEM((2, 8, LANES), F32),
        vec=pltpu.VMEM((own, rank), F32),
        tot=pltpu.VMEM((tables * 16, LANES), F32),
        vec_out=pltpu.VMEM((own, rank), BF16),
        vec_in=pltpu.VMEM((parts, share, rank), BF16),
        tot_out=pltpu.VMEM((halves, 16, LANES), BF16),
        tot_in=pltpu.VMEM((parts, 16, LANES), BF16),
        relay_out=pltpu.VMEM((16, LANES), F32),
        relay_in=pltpu.VMEM((16, LANES), F32),
        cross_out=pltpu.VMEM((16, LANES), BF16),
        cross_in=pltpu.VMEM((parts, 16, LANES), BF16),
        halo_sems=pltpu.SemaphoreType.DMA((2, 2)),
        relay_sems=pltpu.SemaphoreType.DMA((2, 1)),
        vec_sems=pltpu.SemaphoreType.DMA((2, parts)),
        tot_sems=pltpu.SemaphoreType.DMA((2, parts)),
        cross_sems=pltpu.SemaphoreType.DMA((2, parts)),
        ready=pltpu.SemaphoreType.REGULAR,
        load_sems=pltpu.SemaphoreType.DMA((len(inputs),)),
    )
    keys = list(names)
    local = [pltpu.VMEM(x.shape, x.dtype) for x in inputs]

    def kernel(*refs):
        sources, out_ref = refs[: len(inputs)], refs[len(inputs)]
        held = refs[len(inputs) + 1 : 2 * len(inputs) + 1]
        s = dict(zip(keys, refs[2 * len(inputs) + 1 :]))
        pos_ref, species_ref, lo_ref, hi_ref, nb_ref, mask_ref, alpha_ref, sparse_ref, factor_ref = held
        place = Place()
        place.greet()
        loads = [
            pltpu.make_async_copy(x, y, s["load_sems"].at[k])
            for k, (x, y) in enumerate(zip(sources, held))
        ]
        for load in loads:
            load.start()
        for load in loads[:4]:
            load.wait()
        halo_pick(pos_ref, species_ref, (lo_ref, hi_ref), s["table"], s["face"])
        place.met()
        near = remote(s["face"].at[1 - place.odd], s["rim"].at[0], s["halo_sems"], (0,), (place.mate, place.part))
        far = remote(s["face"].at[place.odd], s["rim"].at[1], s["halo_sems"], (1,), (place.cross, place.part))

        @pl.when(place.exists)
        def _():
            far.start()

        near.start()
        place.tell(s["ready"])

        @pl.when(jnp.logical_not(place.exists))
        def _():
            s["rim"][1] = jnp.zeros((8, LANES), F32)
            for j in range(parts):
                s["cross_in"][j] = jnp.zeros((16, LANES), BF16)

        identities(s["plain"], s["eye"])
        for load in loads[4:]:
            load.wait()
        norms(sparse_ref, alpha_ref, s["scale"], 0, sparse.shape[0] // 512)
        own_setup(s["table"], nb_ref, s["pick"])
        one_hots(nb_ref, s["hot"])
        near.wait()

        @pl.when(place.exists)
        def _():
            far.wait()

        halo_place(s["rim"], s["table"], own, place.odd)
        live_row = jnp.broadcast_to(jnp.sum(mask_ref[0:1, :], axis=1, keepdims=True), (8, LANES))
        pair_setup(
            s["table"], pos_ref, nb_ref, mask_ref, live_row, s["pick"], s["off"], s["w"], s["kind"], s["r"]
        )
        moments(s["off"], s["w"], s["r"], s["acc"], s["m"], s["mc"])
        descriptors(s["m"], s["mc"], s["d"], s["rinv"], s["desc"], s["plain"])
        kernel_sums(s["desc"], sparse_ref, s["scale"], factor_ref, s["grad"], s["vec"], s["energy"])
        s["vec_out"][...] = s["vec"][...].astype(BF16)
        vectors = [
            remote(
                s["vec_out"].at[pl.ds(pl.multiple_of(other * share, share), share)],
                s["vec_in"].at[j],
                s["vec_sems"],
                (j,),
                (place.brick, other),
            )
            for j, other in enumerate(place.others)
            if j
        ]
        for copy in vectors:
            copy.start()
        moment_grads(s["grad"], s["desc"], s["eye"], s["gd"], s["gt"], s["mc"], s["rinv"], s["g"])
        pair_terms(s["off"], s["kind"], s["r"], s["g"], s["t"], s["own"])
        scatter(nb_ref, s["hot"], s["t"], s["own"], s["energy"], s["tot"])
        s["relay_out"][...] = s["tot"][pl.ds(pl.multiple_of((halves + 1 - place.odd) * 16, 16), 16), :]
        relay = remote(s["relay_out"], s["relay_in"], s["relay_sems"], (0,), (place.mate, place.part))
        relay.start()
        s["cross_out"][...] = s["tot"][pl.ds(pl.multiple_of((halves + place.odd) * 16, 16), 16), :].astype(BF16)
        crossing = [
            remote(s["cross_out"], s["cross_in"].at[j], s["cross_sems"], (j,), (place.cross, other))
            for j, other in enumerate(place.others)
        ]

        place.told(s["ready"])

        @pl.when(place.exists)
        def _():
            for copy in crossing[::-1]:
                copy.start()

        odd = place.odd == 1
        near_send = jnp.where(odd, lo_ref[...], hi_ref[...])
        far_send = jnp.where(odd, hi_ref[...], lo_ref[...])
        near_slots = slots_of(near_send, 0, own)
        relay.wait()
        near_part = deliver(s["relay_in"][...], near_slots)
        for h in range(halves):
            s["tot_out"][h] = (
                s["tot"][h * 16 : (h + 1) * 16, :] + near_part[:, h * LANES : (h + 1) * LANES]
            ).astype(BF16)
        totals = [
            remote(
                s["tot_out"].at[other * share // LANES], s["tot_in"].at[j], s["tot_sems"], (j,), (place.brick, other)
            )
            for j, other in enumerate(place.others)
            if j
        ]
        for copy in totals:
            copy.start()
        vec = s["vec_out"][pl.ds(pl.multiple_of(place.part * share, share), share), :].astype(F32)
        for copy in vectors:
            copy.wait()
        for j in range(1, parts):
            vec = vec + s["vec_in"][j].astype(F32)
        variances = lax.dot_general(
            jnp.ones((16, rank), F32), vec * vec, NT, precision=lax.Precision.HIGHEST, preferred_element_type=F32
        )
        half = place.part * share // LANES
        far_slots = slots_of(far_send, half * LANES, LANES)
        mine = s["tot_out"][half].astype(F32)
        for copy in totals:
            copy.wait()
        for j in range(1, parts):
            mine = mine + s["tot_in"][j].astype(F32)

        @pl.when(place.exists)
        def _():
            for copy in crossing:
                copy.wait()

        ghosts = s["cross_in"][0].astype(F32)
        for j in range(1, parts):
            ghosts = ghosts + s["cross_in"][j].astype(F32)
        mine = mine + deliver(ghosts, far_slots)
        shift = lax.rem(LANES - lax.rem(place.part * share, LANES), LANES)
        out_ref[...] = pltpu.roll(mine, shift, 1)
        out_ref[10:11, :share] = variances[10:11]

    anywhere = pl.BlockSpec(memory_space=pltpu.HBM)
    return pl.pallas_call(
        kernel,
        out_shape=jax.ShapeDtypeStruct((16, LANES), F32),
        in_specs=[anywhere] * len(inputs),
        out_specs=pl.BlockSpec(memory_space=pltpu.VMEM),
        scratch_shapes=local + list(names.values()),
        compiler_params=pltpu.CompilerParams(
            vmem_limit_bytes=60 * 1024 * 1024, collective_id=0, has_side_effects=True
        ),
        name="brick",
    )(*inputs)


def split(result, share):
    def kernel(result_ref, force_ref, energy_ref, variance_ref, virial_ref):
        force_ref[...] = result_ref[0:3, :share]
        virial_ref[...] = result_ref[3:9, :share]
        energy_ref[...] = result_ref[9:10, :share]
        variance_ref[...] = result_ref[10:11, :share]

    vmem = pl.BlockSpec(memory_space=pltpu.VMEM)
    return pl.pallas_call(
        kernel,
        out_shape=tuple(jax.ShapeDtypeStruct((n, share), F32) for n in (3, 1, 1, 6)),
        in_specs=[vmem],
        out_specs=(vmem,) * 4,
        name="split",
    )(result)


def shards(
    positions, species, live_count, neighbors, neighbor_mask, send_lo, send_hi, sparse_desc, alpha, var_factor
):
    parts = lax.axis_size("sparse")
    result = brick(
        positions,
        species[None],
        neighbors,
        neighbor_mask,
        send_lo[None],
        send_hi[None],
        sparse_desc,
        alpha.reshape(-1, LANES),
        var_factor,
        parts,
    )
    forces, energies, variances, virials = split(result, positions.shape[1] // parts)
    return forces, energies[0], variances[0], virials


def solution(mesh):
    return jax.shard_map(
        shards,
        mesh=mesh,
        in_specs=(
            P(None, "space"),
            P("space"),
            P("space"),
            P(None, "space"),
            P(None, "space"),
            P("space"),
            P("space"),
            P("sparse", None),
            P("sparse"),
            P("sparse", None),
        ),
        out_specs=(
            P(None, ("space", "sparse")),
            P(("space", "sparse")),
            P(("space", "sparse")),
            P(None, ("space", "sparse")),
        ),
        check_vma=False,
    )
```

```python
import jax
import jax.numpy as jnp
from jax import lax
from jax.experimental import pallas as pl
from jax.experimental.pallas import tpu as pltpu
from jax.sharding import PartitionSpec as P

EPS = 1e-6
F32, BF16 = jnp.float32, jnp.bfloat16
SPECIES, RADIAL = 4, 4
K = SPECIES * RADIAL
LANES = 128
LOW = 64
RATES = tuple(scale * 2.0**r for scale in (0.1, 0.15) for r in range(RADIAL))
ORDERS = ((0, 1), (1, 4), (4, 10))
FOLD = (1.0,) * 7 + (2.0,) * 3
PAIRS = ((0, 0), (1, 1), (2, 2), (0, 1), (0, 2), (1, 2))
NT = (((1,), (1,)), ((), ()))


def angular(radial, o):
    first = [radial * o[p] for p in range(3)]
    return [radial] + first + [first[a] * o[b] for a, b in PAIRS]


def along(start, size):
    return pl.ds(pl.multiple_of(start, size), size)


def norms(sparse_ref, alpha_ref, scale_ref, first, last, chunk=512):
    depth = sparse_ref.shape[1]
    ones = jnp.ones((8, LANES), BF16)
    row = lax.broadcasted_iota(jnp.int32, (8, chunk), 0)
    per = chunk // LANES
    for t in range(first, last):
        raw = sparse_ref[t * chunk : (t + 1) * chunk, :]
        parts = [raw[:, j * LANES : (j + 1) * LANES] for j in range(depth // LANES)]
        parts = [part * part for part in parts]
        while len(parts) > 1:
            parts = [x + y for x, y in zip(parts[::2], parts[1::2])] + parts[len(parts) // 2 * 2 :]
        squares = lax.dot_general(ones, parts[0], NT, preferred_element_type=F32)
        inverse = 1.0 / (squares + EPS)
        alpha = jnp.concatenate([alpha_ref[t * per + j : t * per + j + 1, :] for j in range(per)], axis=1)
        scale_ref[:, t * chunk : (t + 1) * chunk] = inverse * jnp.where(row == 0, 1.0, 2.0 * alpha)


def pick_from(table_ref, first, last, low, high, value, rows):
    picked = []
    for c in range(4):
        got = value[c]
        for t in range(first, last):
            source = jnp.broadcast_to(table_ref[c : c + 1, t * LANES : (t + 1) * LANES], (rows, LANES))
            part = jnp.take_along_axis(source, low, axis=1, mode="promise_in_bounds")
            got = part if got is None else jnp.where(high == t, part, got)
        picked.append(got)
    return picked


def own_setup(table_ref, nb_ref, pick_ref):
    halves, _, count, _ = pick_ref.shape
    blocks = count // 8

    def step(i, _):
        h, b = i // blocks, i % blocks
        rows = along(b * 8, 8)
        index = nb_ref[rows, along(h * LANES, LANES)]
        values = pick_from(table_ref, 0, halves, index & (LANES - 1), index // LANES, [None] * 4, 8)
        for c in range(4):
            pick_ref[h, c, rows, :] = values[c]
        return 0

    lax.fori_loop(0, halves * blocks, step, 0, unroll=8)


def pair_setup(table_ref, pos_ref, nb_ref, mask_ref, live, pick_ref, off_ref, w_ref, kind_ref, r_ref):
    own = pos_ref.shape[1]
    halves = own // LANES
    tables = table_ref.shape[1] // LANES
    blocks = nb_ref.shape[0] // 8
    lane = lax.broadcasted_iota(jnp.int32, (8, LANES), 1)

    def step(i, _):
        h, b = i // blocks, i % blocks
        rows, cols = along(b * 8, 8), along(h * LANES, LANES)
        index = nb_ref[rows, cols]
        held = [pick_ref[h, c, rows, :] for c in range(4)]
        picked = pick_from(table_ref, halves, tables, index & (LANES - 1), index // LANES, held, 8)
        o = [picked[p] - pos_ref[p : p + 1, cols] for p in range(3)]
        alive = ((index >= own) | (index < live)) & (h * LANES + lane < live)
        valid = jnp.where(alive, mask_ref[rows, cols].astype(F32), 0.0)
        for p in range(3):
            off_ref[h, p, rows, :] = o[p]
        for s in range(SPECIES - 1):
            w_ref[h, s, rows, :] = jnp.where(picked[3] == s, 1.0, 0.0)
        kind_ref[h, rows, :] = picked[3].astype(jnp.int32)
        square = o[0] * o[0] + o[1] * o[1] + o[2] * o[2]
        for e in range(2):
            radial = jnp.exp(square * (-RATES[e * RADIAL]))
            for r in range(RADIAL):
                if r:
                    radial = radial * radial
                r_ref[h, e * RADIAL + r, rows, :] = radial * valid
        return 0

    lax.fori_loop(0, halves * blocks, step, 0, unroll=8)


def moments(off_ref, w_ref, r_ref, acc_ref, m_ref, mc_ref):
    halves, _, count, _ = off_ref.shape

    def fold(i, ms):
        for m in ms:
            value = acc_ref[i * 10 + m, pl.ds(0, K, stride=8), :]
            for j in range(1, 8):
                value = value + acc_ref[i * 10 + m, pl.ds(j, K, stride=8), :]
            m_ref[i * 10 + m] = value
            mc_ref[i * 10 + m] = value * FOLD[m]

    def step(i, before):
        h, e = i // 2, i % 2
        for r in range(RADIAL):
            total = [[None] * 10 for _ in range(SPECIES)]
            for b in range(count // 8):
                rows = slice(b * 8, b * 8 + 8)
                v = angular(r_ref[h, e * RADIAL + r, rows, :], [off_ref[h, p, rows, :] for p in range(3)])
                for s in range(SPECIES):
                    weight = w_ref[h, s, rows, :] if s < SPECIES - 1 else None
                    for m in range(10):
                        term = v[m] if weight is None else weight * v[m]
                        total[s][m] = term if b == 0 else total[s][m] + term
            if before is not None:
                fold(before, range(r * 10 // RADIAL, (r + 1) * 10 // RADIAL))
            for m in range(10):
                total[3][m] = total[3][m] - (total[0][m] + total[1][m] + total[2][m])
                for s in range(SPECIES):
                    acc_ref[i * 10 + m, (s * RADIAL + r) * 8 : (s * RADIAL + r) * 8 + 8, :] = total[s][m]

    for i in range(halves * 2):
        step(i, i - 1 if i else None)
    fold(halves * 2 - 1, range(10))


def descriptors(m_ref, mc_ref, d_ref, rinv_ref, desc_ref, plain_ref):
    halves = d_ref.shape[0]

    def step(k, squares):
        fresh = []
        for h in range(halves):
            base = h * 20
            total = squares[h]
            for l, (start, stop) in enumerate(ORDERS):
                value = None
                for m in range(start, stop):
                    term = m_ref[base + m, pl.ds(k, 1), :] * mc_ref[base + 10 + m]
                    value = term if value is None else value + term
                d_ref[h, along(l * K * K + k * K, K), :] = value
                total = total + value * value
            fresh.append(total)
        return tuple(fresh)

    squares = lax.fori_loop(0, K, step, (jnp.zeros((K, LANES), F32),) * halves, unroll=8)
    for h in range(halves):
        rinv = lax.rsqrt(jnp.sum(squares[h], axis=0, keepdims=True) + EPS)
        rinv_ref[h] = jnp.broadcast_to(rinv, (8, LANES))
        unit = (d_ref[h] * rinv).astype(BF16)
        desc_ref[h * LANES : (h + 1) * LANES, :] = lax.dot_general(
            plain_ref[...], unit, NT, preferred_element_type=F32
        ).astype(BF16)


def kernel_sums(desc_ref, sparse_ref, scale_ref, grad_ref, kernel_ref, row_ref):
    raw = sparse_ref[...]
    projection = lax.dot_general(desc_ref[...], raw, NT, preferred_element_type=F32)
    coefficient = projection * scale_ref[1:2, :]
    kernel = (projection * projection * scale_ref[0:1, :]).astype(BF16)
    energy_terms = coefficient * projection
    energy = energy_terms[:, :LANES]
    for j in range(1, raw.shape[0] // LANES):
        energy = energy + energy_terms[:, j * LANES : (j + 1) * LANES]
    grad_ref[...] = jnp.dot(coefficient.astype(BF16), raw, preferred_element_type=F32)
    kernel_ref[...] = kernel
    row_ref[...] = energy


def moment_grads(grad_ref, desc_ref, eye_ref, gd_ref, gt_ref, mc_ref, rinv_ref, g_ref):
    halves = gt_ref.shape[0]
    unit = desc_ref[...].astype(F32)
    grad = grad_ref[...]
    along_unit = jnp.sum(grad * unit, axis=1, keepdims=True)
    gd_ref[...] = (grad - unit * along_unit).astype(BF16)
    for l in range(3):
        turned = lax.dot_general(
            eye_ref[...], gd_ref[:, l * K * K : (l + 1) * K * K], NT, preferred_element_type=F32
        )
        for h in range(halves):
            gt_ref[h, l] = turned[:, h * LANES : (h + 1) * LANES]

    def step(i, _):
        h, e = i // 2, i % 2
        rinv = rinv_ref[h, 0:1, :]
        for l, (start, stop) in enumerate(ORDERS):
            total = [None] * 10
            for j in range(K):
                block = gt_ref[h, l, along((1 - e) * K * K + j * K, K), :]
                for m in range(start, stop):
                    term = block * mc_ref[h * 20 + (1 - e) * 10 + m, j : j + 1, :]
                    total[m] = term if j == 0 else total[m] + term
            for m in range(start, stop):
                g_ref[i * 10 + m] = total[m] * rinv
        return 0

    lax.fori_loop(0, halves * 2, step, 0)


def pair_terms(off_ref, kind_ref, r_ref, g_ref, t_ref, own_ref, group=2):
    halves, _, count, _ = off_ref.shape
    blocks = count // 8 // group
    own_ref[...] = jnp.zeros(own_ref.shape, F32)

    def step(i, _):
        h, b = i // blocks, i % blocks
        rows = [along((b * group + q) * 8, 8) for q in range(group)]
        o = [[off_ref[h, p, rows[q], :] for p in range(3)] for q in range(group)]
        ang = [[None] + o[q] + [o[q][x] * o[q][y] for x, y in PAIRS] for q in range(group)]
        kind = [kind_ref[h, rows[q], :] for q in range(group)]
        which = [[kind[q], kind[q] + SPECIES] for q in range(group)]
        top = [[None] * 10 for _ in range(group)]
        slope = [None] * group
        for er, rate in enumerate(RATES):
            e, r = er // RADIAL, er % RADIAL
            radial = [r_ref[h, er, rows[q], :] for q in range(group)]
            inner = [None] * group
            for m in range(10):
                g = g_ref[(h * 2 + e) * 10 + m, r // 2 * 8 : r // 2 * 8 + 8, :]
                for q in range(group):
                    pick = jnp.take_along_axis(g, which[q][r % 2], axis=0, mode="promise_in_bounds")
                    if m == 0:
                        inner[q] = pick
                    else:
                        inner[q] = inner[q] + pick * ang[q][m]
                        term = radial[q] * pick
                        top[q][m] = term if er == 0 else top[q][m] + term
            for q in range(group):
                term = (radial[q] * (-rate)) * inner[q]
                slope[q] = term if er == 0 else slope[q] + term
        sums = [None] * 9
        for q in range(group):
            x, y, z = o[q]
            t = top[q]
            gx = t[1] + 2.0 * x * (t[4] + slope[q]) + t[7] * y + t[8] * z
            gy = t[2] + 2.0 * y * (t[5] + slope[q]) + t[7] * x + t[9] * z
            gz = t[3] + 2.0 * z * (t[6] + slope[q]) + t[8] * x + t[9] * y
            g = [gx, gy, gz]
            terms = [-v for v in g] + [-0.5 * o[q][a] * g[c] for a, c in PAIRS]
            for c in range(9):
                t_ref[h, along(c * count + (b * group + q) * 8, 8), :] = terms[c]
                sums[c] = terms[c] if q == 0 else sums[c] + terms[c]
        for c in range(9):
            own_ref[h, c * 8 : c * 8 + 8, :] += -sums[c] if c < 3 else sums[c]
        return 0

    lax.fori_loop(0, halves * blocks, step, 0)


def scatter(nb_ref, hot_ref, t_ref, tot_ref, unroll=32):
    count, own = nb_ref.shape
    halves = own // LANES
    tables = tot_ref.shape[0] // 16
    groups = tables * LANES // LOW
    per = LANES // LOW
    row = lax.broadcasted_iota(jnp.int32, (8, own), 0)

    def step(i, total):
        left, right = [], []
        for u in range(unroll):
            n = i * unroll + u
            index = nb_ref[pl.ds(n, 1), :]
            high = jnp.broadcast_to(index // LOW, (8, own))
            eight = jnp.concatenate([t_ref[h, pl.ds(n, 8, stride=count), :] for h in range(halves)], axis=1)
            ninth = jnp.concatenate([t_ref[h, pl.ds(8 * count + n, 1), :] for h in range(halves)], axis=1)
            masked = [jnp.where(high == g, eight, 0.0) for g in range(groups)]
            masked += [jnp.where(high == row, ninth, 0.0), jnp.zeros((8, own), F32)]
            left.append(jnp.concatenate(masked, axis=0).astype(BF16))
            right.append(hot_ref[n])
        return total + lax.dot_general(
            jnp.concatenate(left, axis=1), jnp.concatenate(right, axis=1), NT, preferred_element_type=F32
        )

    total = lax.fori_loop(0, count // unroll, step, jnp.zeros((groups * 8 + 16, LOW), F32))
    row = lax.broadcasted_iota(jnp.int32, (8, LANES), 0)
    for t in reversed(range(tables)):
        tot_ref[t * 16 : t * 16 + 8, :] = jnp.concatenate(
            [total[(t * per + g) * 8 : (t * per + g + 1) * 8] for g in range(per)], axis=1
        )
        last = jnp.concatenate(
            [total[groups * 8 + t * per + g : groups * 8 + t * per + g + 1] for g in range(per)], axis=1
        )
        tot_ref[t * 16 + 8 : t * 16 + 16, :] = jnp.where(row == 0, last, 0.0)


def own_terms(own_ref, row_ref, h):
    mine = own_ref[h, pl.ds(0, 16, stride=8), :]
    for j in range(1, 8):
        mine = mine + own_ref[h, pl.ds(j, 16, stride=8), :]
    row = lax.broadcasted_iota(jnp.int32, (16, LANES), 0)
    energies = 0.5 * lax.dot_general(
        jnp.ones((8, LANES), F32),
        row_ref[h * LANES : (h + 1) * LANES, :],
        NT,
        precision=lax.Precision.HIGHEST,
        preferred_element_type=F32,
    )
    return jnp.where(row == 9, energies[0:1], mine)


def one_hots(nb_ref, hot_ref):
    count, own = nb_ref.shape
    slot = lax.broadcasted_iota(jnp.int32, (LOW, own), 0)

    def step(n, _):
        low = nb_ref[pl.ds(n, 1), :] & (LOW - 1)
        hot_ref[n] = jnp.where(slot == low, 1.0, 0.0).astype(BF16)
        return 0

    lax.fori_loop(0, count, step, 0, unroll=4)


def identities(plain_ref, eye_ref):
    size = K * K
    row = lax.broadcasted_iota(jnp.int32, (size, size), 0)
    col = lax.broadcasted_iota(jnp.int32, (size, size), 1)
    plain_ref[...] = jnp.where(row[:LANES, :LANES] == col[:LANES, :LANES], 1.0, 0.0).astype(BF16)
    outer = row // K
    inner = row % SPECIES * RADIAL + row % K // SPECIES
    eye_ref[:size, :] = jnp.where(outer * K + inner == col, 1.0, 0.0).astype(BF16)
    eye_ref[size:, :] = jnp.where(inner * K + outer == col, 1.0, 0.0).astype(BF16)


def scratch_shapes(own, count, width, sparse, depth, rank):
    halves = own // LANES
    return dict(
        off=pltpu.VMEM((halves, 3, count, LANES), F32),
        pick=pltpu.VMEM((halves, 4, count, LANES), F32),
        plain=pltpu.VMEM((LANES, LANES), BF16),
        w=pltpu.VMEM((halves, SPECIES - 1, count, LANES), F32),
        kind=pltpu.VMEM((halves, count, LANES), jnp.int32),
        r=pltpu.VMEM((halves, len(RATES), count, LANES), F32),
        acc=pltpu.VMEM((halves * 20, K * 8, LANES), F32),
        m=pltpu.VMEM((halves * 20, K, LANES), F32),
        mc=pltpu.VMEM((halves * 20, K, LANES), F32),
        d=pltpu.VMEM((halves, depth, LANES), F32),
        rinv=pltpu.VMEM((halves, 8, LANES), F32),
        desc=pltpu.VMEM((own, depth), BF16),
        eye=pltpu.VMEM((2 * K * K, K * K), BF16),
        scale=pltpu.VMEM((8, sparse), F32),
        grad=pltpu.VMEM((own, depth), F32),
        row=pltpu.VMEM((own, LANES), F32),
        kernel=pltpu.VMEM((own, sparse), BF16),
        gd=pltpu.VMEM((own, depth), BF16),
        gt=pltpu.VMEM((halves, 3, 2 * K * K, LANES), F32),
        g=pltpu.VMEM((halves * 20, K, LANES), F32),
        t=pltpu.VMEM((halves, 9 * count, LANES), F32),
        own=pltpu.VMEM((halves, 16 * 8, LANES), F32),
        hot=pltpu.VMEM((count, LOW, own), BF16),
    )


MESH = pl.DeviceIdType.MESH


def remote(source, target, sems, slot, device):
    return pltpu.make_async_remote_copy(
        src_ref=source,
        dst_ref=target,
        send_sem=sems.at[(0, *slot)],
        recv_sem=sems.at[(1, *slot)],
        device_id=device,
        device_id_type=MESH,
    )


class Place:
    def __init__(self):
        self.brick, self.part = lax.axis_index("space"), lax.axis_index("sparse")
        bricks, self.parts = lax.axis_size("space"), lax.axis_size("sparse")
        self.odd = lax.rem(self.brick, 2)
        self.mate = self.brick + 1 - 2 * self.odd
        self.exists = (self.brick > 0) & (self.brick < bricks - 1)
        self.cross = jnp.where(self.exists, self.brick - 1 + 2 * self.odd, self.mate)
        self.others = [lax.rem(self.part + j, self.parts) for j in range(self.parts)]

    def greet(self):
        barrier = pltpu.get_barrier_semaphore()

        def signal(device):
            pl.semaphore_signal(barrier, inc=1, device_id=device, device_id_type=MESH)

        @pl.when(self.exists)
        def _():
            signal((self.cross, self.part))

        signal((self.mate, self.part))
        for other in self.others[1:]:
            signal((self.brick, other))

    def met(self):
        barrier = pltpu.get_barrier_semaphore()
        pl.semaphore_wait(barrier, jnp.where(self.exists, self.parts + 1, self.parts))

    def tell(self, semaphore):
        for other in self.others[1:]:
            pl.semaphore_signal(semaphore, inc=1, device_id=(self.brick, other), device_id_type=MESH)

    def told(self, semaphore):
        pl.semaphore_wait(semaphore, self.parts - 1)


def halo_pick(pos_ref, species_ref, send_refs, table_ref, face_ref):
    own = pos_ref.shape[1]
    table_ref[0:3, :own] = pos_ref[...]
    table_ref[3:4, :own] = species_ref[...].astype(F32)
    table_ref[4:8, :own] = jnp.zeros((4, own), F32)
    for f, send_ref in enumerate(send_refs):
        index = jnp.broadcast_to(send_ref[...], (8, LANES))
        low, high = index & (LANES - 1), index // LANES
        value = None
        for t in range(own // LANES):
            part = jnp.take_along_axis(
                table_ref[:, t * LANES : (t + 1) * LANES], low, axis=1, mode="promise_in_bounds"
            )
            value = part if value is None else jnp.where(high == t, part, value)
        face_ref[f] = value


def halo_place(rim_ref, table_ref, own, odd):
    mate, cross = rim_ref[0], rim_ref[1]
    table_ref[:, own : own + LANES] = jnp.where(odd == 1, mate, cross)
    table_ref[:, own + LANES : own + 2 * LANES] = jnp.where(odd == 1, cross, mate)


def deliver(ghosts, slots):
    high = ghosts.astype(BF16)
    low = (ghosts - high.astype(F32)).astype(BF16)
    both = lax.dot_general(jnp.concatenate([high, low], axis=0), slots, NT, preferred_element_type=F32)
    return both[:16] + both[16:]


def slots_of(send, first, count):
    slot = first + lax.broadcasted_iota(jnp.int32, (count, LANES), 0)
    return jnp.where(slot == send, 1.0, 0.0).astype(BF16)


def brick(pos, species, nb, mask, send_lo, send_hi, sparse, alpha, factor, parts):
    own, count = pos.shape[1], nb.shape[0]
    depth, rank = sparse.shape[1], factor.shape[1]
    halves = own // LANES
    tables = halves + 2
    share = own // parts
    names = scratch_shapes(own, count, tables * LANES, sparse.shape[0], depth, rank)
    inputs = (pos, species, send_lo, send_hi, nb, mask, alpha, sparse, factor)
    names.update(
        table=pltpu.VMEM((8, tables * LANES), F32),
        face=pltpu.VMEM((2, 8, LANES), F32),
        rim=pltpu.VMEM((2, 8, LANES), F32),
        tot=pltpu.VMEM((tables * 16, LANES), F32),
        vec_out=pltpu.VMEM((own, rank), BF16),
        vec_in=pltpu.VMEM((parts, share, rank), BF16),
        tot_out=pltpu.VMEM((halves, 16, LANES), BF16),
        tot_in=pltpu.VMEM((parts, 16, LANES), BF16),
        relay_out=pltpu.VMEM((16, LANES), F32),
        relay_in=pltpu.VMEM((16, LANES), F32),
        cross_out=pltpu.VMEM((16, LANES), BF16),
        cross_in=pltpu.VMEM((parts, 16, LANES), BF16),
        halo_sems=pltpu.SemaphoreType.DMA((2, 2)),
        relay_sems=pltpu.SemaphoreType.DMA((2, 1)),
        vec_sems=pltpu.SemaphoreType.DMA((2, parts)),
        tot_sems=pltpu.SemaphoreType.DMA((2, parts)),
        cross_sems=pltpu.SemaphoreType.DMA((2, parts)),
        ready=pltpu.SemaphoreType.REGULAR,
        load_sems=pltpu.SemaphoreType.DMA((len(inputs),)),
    )
    keys = list(names)
    local = [pltpu.VMEM(x.shape, x.dtype) for x in inputs]

    def kernel(*refs):
        sources, out_ref = refs[: len(inputs)], refs[len(inputs)]
        held = refs[len(inputs) + 1 : 2 * len(inputs) + 1]
        s = dict(zip(keys, refs[2 * len(inputs) + 1 :]))
        pos_ref, species_ref, lo_ref, hi_ref, nb_ref, mask_ref, alpha_ref, sparse_ref, factor_ref = held
        place = Place()
        place.greet()
        loads = [
            pltpu.make_async_copy(x, y, s["load_sems"].at[k])
            for k, (x, y) in enumerate(zip(sources, held))
        ]
        for load in loads:
            load.start()
        for load in loads[:4]:
            load.wait()
        halo_pick(pos_ref, species_ref, (lo_ref, hi_ref), s["table"], s["face"])
        place.met()
        near = remote(s["face"].at[1 - place.odd], s["rim"].at[0], s["halo_sems"], (0,), (place.mate, place.part))
        far = remote(s["face"].at[place.odd], s["rim"].at[1], s["halo_sems"], (1,), (place.cross, place.part))

        @pl.when(place.exists)
        def _():
            far.start()

        near.start()
        place.tell(s["ready"])

        @pl.when(jnp.logical_not(place.exists))
        def _():
            s["rim"][1] = jnp.zeros((8, LANES), F32)
            for j in range(parts):
                s["cross_in"][j] = jnp.zeros((16, LANES), BF16)

        identities(s["plain"], s["eye"])
        for load in loads[4:]:
            load.wait()
        norms(sparse_ref, alpha_ref, s["scale"], 0, sparse.shape[0] // 512)
        own_setup(s["table"], nb_ref, s["pick"])
        one_hots(nb_ref, s["hot"])
        near.wait()

        @pl.when(place.exists)
        def _():
            far.wait()

        halo_place(s["rim"], s["table"], own, place.odd)
        live_row = jnp.broadcast_to(jnp.sum(mask_ref[0:1, :], axis=1, keepdims=True), (8, LANES))
        pair_setup(
            s["table"], pos_ref, nb_ref, mask_ref, live_row, s["pick"], s["off"], s["w"], s["kind"], s["r"]
        )
        moments(s["off"], s["w"], s["r"], s["acc"], s["m"], s["mc"])
        descriptors(s["m"], s["mc"], s["d"], s["rinv"], s["desc"], s["plain"])
        kernel_sums(s["desc"], sparse_ref, s["scale"], s["grad"], s["kernel"], s["row"])
        moment_grads(s["grad"], s["desc"], s["eye"], s["gd"], s["gt"], s["mc"], s["rinv"], s["g"])
        pair_terms(s["off"], s["kind"], s["r"], s["g"], s["t"], s["own"])
        scatter(nb_ref, s["hot"], s["t"], s["tot"])
        s["cross_out"][...] = s["tot"][pl.ds(pl.multiple_of((halves + place.odd) * 16, 16), 16), :].astype(BF16)
        crossing = [
            remote(s["cross_out"], s["cross_in"].at[j], s["cross_sems"], (j,), (place.cross, other))
            for j, other in enumerate(place.others)
        ]

        place.told(s["ready"])

        @pl.when(place.exists)
        def _():
            for copy in crossing[::-1]:
                copy.start()

        s["relay_out"][...] = s["tot"][pl.ds(pl.multiple_of((halves + 1 - place.odd) * 16, 16), 16), :]
        relay = remote(s["relay_out"], s["relay_in"], s["relay_sems"], (0,), (place.mate, place.part))
        relay.start()
        s["vec_out"][...] = jnp.dot(s["kernel"][...], factor_ref[...], preferred_element_type=F32).astype(BF16)
        vectors = [
            remote(
                s["vec_out"].at[pl.ds(pl.multiple_of(other * share, share), share)],
                s["vec_in"].at[j],
                s["vec_sems"],
                (j,),
                (place.brick, other),
            )
            for j, other in enumerate(place.others)
            if j
        ]
        for copy in vectors:
            copy.start()
        odd = place.odd == 1
        near_send = jnp.where(odd, lo_ref[...], hi_ref[...])
        far_send = jnp.where(odd, hi_ref[...], lo_ref[...])
        near_slots = slots_of(near_send, 0, own)
        mine = [s["tot"][h * 16 : (h + 1) * 16, :] + own_terms(s["own"], s["row"], h) for h in range(halves)]
        relay.wait()
        near_part = deliver(s["relay_in"][...], near_slots)
        for h in range(halves):
            s["tot_out"][h] = (
                mine[h] + near_part[:, h * LANES : (h + 1) * LANES]
            ).astype(BF16)
        totals = [
            remote(
                s["tot_out"].at[other * share // LANES], s["tot_in"].at[j], s["tot_sems"], (j,), (place.brick, other)
            )
            for j, other in enumerate(place.others)
            if j
        ]
        for copy in totals:
            copy.start()
        vec = s["vec_out"][pl.ds(pl.multiple_of(place.part * share, share), share), :].astype(F32)
        for copy in vectors:
            copy.wait()
        for j in range(1, parts):
            vec = vec + s["vec_in"][j].astype(F32)
        variances = lax.dot_general(
            jnp.ones((16, rank), F32), vec * vec, NT, precision=lax.Precision.HIGHEST, preferred_element_type=F32
        )
        half = place.part * share // LANES
        far_slots = slots_of(far_send, half * LANES, LANES)
        mine = s["tot_out"][half].astype(F32)
        for copy in totals:
            copy.wait()
        for j in range(1, parts):
            mine = mine + s["tot_in"][j].astype(F32)

        @pl.when(place.exists)
        def _():
            for copy in crossing:
                copy.wait()

        ghosts = s["cross_in"][0].astype(F32)
        for j in range(1, parts):
            ghosts = ghosts + s["cross_in"][j].astype(F32)
        mine = mine + deliver(ghosts, far_slots)
        shift = lax.rem(LANES - lax.rem(place.part * share, LANES), LANES)
        out_ref[...] = pltpu.roll(mine, shift, 1)
        out_ref[10:11, :share] = variances[10:11]

    anywhere = pl.BlockSpec(memory_space=pltpu.HBM)
    return pl.pallas_call(
        kernel,
        out_shape=jax.ShapeDtypeStruct((16, LANES), F32),
        in_specs=[anywhere] * len(inputs),
        out_specs=pl.BlockSpec(memory_space=pltpu.VMEM),
        scratch_shapes=local + list(names.values()),
        compiler_params=pltpu.CompilerParams(
            vmem_limit_bytes=60 * 1024 * 1024, collective_id=0, has_side_effects=True
        ),
        name="brick",
    )(*inputs)


def split(result, share):
    def kernel(result_ref, force_ref, energy_ref, variance_ref, virial_ref):
        force_ref[...] = result_ref[0:3, :share]
        virial_ref[...] = result_ref[3:9, :share]
        energy_ref[...] = result_ref[9:10, :share]
        variance_ref[...] = result_ref[10:11, :share]

    vmem = pl.BlockSpec(memory_space=pltpu.VMEM)
    return pl.pallas_call(
        kernel,
        out_shape=tuple(jax.ShapeDtypeStruct((n, share), F32) for n in (3, 1, 1, 6)),
        in_specs=[vmem],
        out_specs=(vmem,) * 4,
        name="split",
    )(result)


def shards(
    positions, species, live_count, neighbors, neighbor_mask, send_lo, send_hi, sparse_desc, alpha, var_factor
):
    parts = lax.axis_size("sparse")
    result = brick(
        positions,
        species[None],
        neighbors,
        neighbor_mask,
        send_lo[None],
        send_hi[None],
        sparse_desc,
        alpha.reshape(-1, LANES),
        var_factor,
        parts,
    )
    forces, energies, variances, virials = split(result, positions.shape[1] // parts)
    return forces, energies[0], variances[0], virials


def solution(mesh):
    return jax.shard_map(
        shards,
        mesh=mesh,
        in_specs=(
            P(None, "space"),
            P("space"),
            P("space"),
            P(None, "space"),
            P(None, "space"),
            P("space"),
            P("space"),
            P("sparse", None),
            P("sparse"),
            P("sparse", None),
        ),
        out_specs=(
            P(None, ("space", "sparse")),
            P(("space", "sparse")),
            P(("space", "sparse")),
            P(None, ("space", "sparse")),
        ),
        check_vma=False,
    )
```

```python
import jax
import jax.numpy as jnp
from jax import lax
from jax.experimental import pallas as pl
from jax.experimental.pallas import tpu as pltpu
from jax.sharding import PartitionSpec as P

EPS = 1e-6
F32, BF16 = jnp.float32, jnp.bfloat16
SPECIES, RADIAL = 4, 4
K = SPECIES * RADIAL
LANES = 128
LOW = 64
RATES = tuple(scale * 2.0**r for scale in (0.1, 0.15) for r in range(RADIAL))
ORDERS = ((0, 1), (1, 4), (4, 10))
FOLD = (1.0,) * 7 + (2.0,) * 3
PAIRS = ((0, 0), (1, 1), (2, 2), (0, 1), (0, 2), (1, 2))
NT = (((1,), (1,)), ((), ()))


def angular(radial, o):
    first = [radial * o[p] for p in range(3)]
    return [radial] + first + [first[a] * o[b] for a, b in PAIRS]


def along(start, size):
    return pl.ds(pl.multiple_of(start, size), size)


def norms(sparse_ref, alpha_ref, scale_ref, first, last, chunk=512):
    depth = sparse_ref.shape[1]
    ones = jnp.ones((8, LANES), BF16)
    row = lax.broadcasted_iota(jnp.int32, (8, chunk), 0)
    per = chunk // LANES
    for t in range(first, last):
        raw = sparse_ref[t * chunk : (t + 1) * chunk, :]
        parts = [raw[:, j * LANES : (j + 1) * LANES] for j in range(depth // LANES)]
        parts = [part * part for part in parts]
        while len(parts) > 1:
            parts = [x + y for x, y in zip(parts[::2], parts[1::2])] + parts[len(parts) // 2 * 2 :]
        squares = lax.dot_general(ones, parts[0], NT, preferred_element_type=F32)
        inverse = 1.0 / (squares + EPS)
        alpha = jnp.concatenate([alpha_ref[t * per + j : t * per + j + 1, :] for j in range(per)], axis=1)
        scale_ref[:, t * chunk : (t + 1) * chunk] = inverse * jnp.where(row == 0, 1.0, 2.0 * alpha)


def pick_from(table_ref, first, last, low, high, value, rows):
    picked = []
    for c in range(4):
        got = value[c]
        for t in range(first, last):
            source = jnp.broadcast_to(table_ref[c : c + 1, t * LANES : (t + 1) * LANES], (rows, LANES))
            part = jnp.take_along_axis(source, low, axis=1, mode="promise_in_bounds")
            got = part if got is None else jnp.where(high == t, part, got)
        picked.append(got)
    return picked


def own_setup(table_ref, nb_ref, pick_ref):
    halves, _, count, _ = pick_ref.shape
    blocks = count // 8

    def step(i, _):
        h, b = i // blocks, i % blocks
        rows = along(b * 8, 8)
        index = nb_ref[rows, along(h * LANES, LANES)]
        values = pick_from(table_ref, 0, halves, index & (LANES - 1), index // LANES, [None] * 4, 8)
        for c in range(4):
            pick_ref[h, c, rows, :] = values[c]
        return 0

    lax.fori_loop(0, halves * blocks, step, 0, unroll=8)


def pair_setup(table_ref, pos_ref, nb_ref, mask_ref, live, pick_ref, off_ref, w_ref, kind_ref, r_ref):
    own = pos_ref.shape[1]
    halves = own // LANES
    tables = table_ref.shape[1] // LANES
    blocks = nb_ref.shape[0] // 8
    lane = lax.broadcasted_iota(jnp.int32, (8, LANES), 1)

    def step(i, _):
        h, b = i // blocks, i % blocks
        rows, cols = along(b * 8, 8), along(h * LANES, LANES)
        index = nb_ref[rows, cols]
        held = [pick_ref[h, c, rows, :] for c in range(4)]
        picked = pick_from(table_ref, halves, tables, index & (LANES - 1), index // LANES, held, 8)
        o = [picked[p] - pos_ref[p : p + 1, cols] for p in range(3)]
        alive = ((index >= own) | (index < live)) & (h * LANES + lane < live)
        valid = jnp.where(alive, mask_ref[rows, cols].astype(F32), 0.0)
        for p in range(3):
            off_ref[h, p, rows, :] = o[p]
        for s in range(SPECIES - 1):
            w_ref[h, s, rows, :] = jnp.where(picked[3] == s, 1.0, 0.0)
        kind_ref[h, rows, :] = picked[3].astype(jnp.int32)
        square = o[0] * o[0] + o[1] * o[1] + o[2] * o[2]
        for e in range(2):
            radial = jnp.exp(square * (-RATES[e * RADIAL]))
            for r in range(RADIAL):
                if r:
                    radial = radial * radial
                r_ref[h, e * RADIAL + r, rows, :] = radial * valid
        return 0

    lax.fori_loop(0, halves * blocks, step, 0, unroll=8)


def moments(off_ref, w_ref, r_ref, acc_ref, m_ref, mc_ref):
    halves, _, count, _ = off_ref.shape

    def fold(i, ms):
        for m in ms:
            value = acc_ref[i * 10 + m, pl.ds(0, K, stride=8), :]
            for j in range(1, 8):
                value = value + acc_ref[i * 10 + m, pl.ds(j, K, stride=8), :]
            m_ref[i * 10 + m] = value
            mc_ref[i * 10 + m] = value * FOLD[m]

    def step(i, before):
        h, e = i // 2, i % 2
        for r in range(RADIAL):
            total = [[None] * 10 for _ in range(SPECIES)]
            for b in range(count // 8):
                rows = slice(b * 8, b * 8 + 8)
                v = angular(r_ref[h, e * RADIAL + r, rows, :], [off_ref[h, p, rows, :] for p in range(3)])
                for s in range(SPECIES):
                    weight = w_ref[h, s, rows, :] if s < SPECIES - 1 else None
                    for m in range(10):
                        term = v[m] if weight is None else weight * v[m]
                        total[s][m] = term if b == 0 else total[s][m] + term
            if before is not None:
                fold(before, range(r * 10 // RADIAL, (r + 1) * 10 // RADIAL))
            for m in range(10):
                total[3][m] = total[3][m] - (total[0][m] + total[1][m] + total[2][m])
                for s in range(SPECIES):
                    acc_ref[i * 10 + m, (s * RADIAL + r) * 8 : (s * RADIAL + r) * 8 + 8, :] = total[s][m]

    for i in range(halves * 2):
        step(i, i - 1 if i else None)
    fold(halves * 2 - 1, range(10))


def descriptors(m_ref, mc_ref, d_ref, rinv_ref, desc_ref, plain_ref):
    halves = d_ref.shape[0]

    def step(k, squares):
        fresh = []
        for h in range(halves):
            base = h * 20
            total = squares[h]
            for l, (start, stop) in enumerate(ORDERS):
                value = None
                for m in range(start, stop):
                    term = m_ref[base + m, pl.ds(k, 1), :] * mc_ref[base + 10 + m]
                    value = term if value is None else value + term
                d_ref[h, along(l * K * K + k * K, K), :] = value
                total = total + value * value
            fresh.append(total)
        return tuple(fresh)

    squares = lax.fori_loop(0, K, step, (jnp.zeros((K, LANES), F32),) * halves, unroll=16)
    for h in range(halves):
        rinv = lax.rsqrt(jnp.sum(squares[h], axis=0, keepdims=True) + EPS)
        rinv_ref[h] = jnp.broadcast_to(rinv, (8, LANES))
        unit = (d_ref[h] * rinv).astype(BF16)
        desc_ref[h * LANES : (h + 1) * LANES, :] = lax.dot_general(
            plain_ref[...], unit, NT, preferred_element_type=F32
        ).astype(BF16)


def kernel_sums(desc_ref, sparse_ref, scale_ref, grad_ref, kernel_ref, row_ref):
    raw = sparse_ref[...]
    projection = lax.dot_general(desc_ref[...], raw, NT, preferred_element_type=F32)
    coefficient = projection * scale_ref[1:2, :]
    kernel = (projection * projection * scale_ref[0:1, :]).astype(BF16)
    energy_terms = coefficient * projection
    energy = energy_terms[:, :LANES]
    for j in range(1, raw.shape[0] // LANES):
        energy = energy + energy_terms[:, j * LANES : (j + 1) * LANES]
    grad_ref[...] = jnp.dot(coefficient.astype(BF16), raw, preferred_element_type=F32)
    kernel_ref[...] = kernel
    row_ref[...] = energy


def moment_grads(grad_ref, desc_ref, eye_ref, gd_ref, gt_ref, mc_ref, rinv_ref, g_ref):
    halves = gt_ref.shape[0]
    unit = desc_ref[...].astype(F32)
    grad = grad_ref[...]
    along_unit = jnp.sum(grad * unit, axis=1, keepdims=True)
    gd_ref[...] = (grad - unit * along_unit).astype(BF16)
    for l in range(3):
        turned = lax.dot_general(
            eye_ref[...], gd_ref[:, l * K * K : (l + 1) * K * K], NT, preferred_element_type=F32
        )
        for h in range(halves):
            gt_ref[h, l] = turned[:, h * LANES : (h + 1) * LANES]

    def step(i, _):
        h, e = i // 2, i % 2
        rinv = rinv_ref[h, 0:1, :]
        for l, (start, stop) in enumerate(ORDERS):
            total = [None] * 10
            for j in range(K):
                block = gt_ref[h, l, along((1 - e) * K * K + j * K, K), :]
                for m in range(start, stop):
                    term = block * mc_ref[h * 20 + (1 - e) * 10 + m, j : j + 1, :]
                    total[m] = term if j == 0 else total[m] + term
            for m in range(start, stop):
                g_ref[i * 10 + m] = total[m] * rinv
        return 0

    lax.fori_loop(0, halves * 2, step, 0, unroll=2)


def pair_terms(off_ref, kind_ref, r_ref, g_ref, t_ref, own_ref, group=2):
    halves, _, count, _ = off_ref.shape
    blocks = count // 8 // group
    own_ref[...] = jnp.zeros(own_ref.shape, F32)

    def step(i, _):
        h, b = i // blocks, i % blocks
        rows = [along((b * group + q) * 8, 8) for q in range(group)]
        o = [[off_ref[h, p, rows[q], :] for p in range(3)] for q in range(group)]
        ang = [[None] + o[q] + [o[q][x] * o[q][y] for x, y in PAIRS] for q in range(group)]
        kind = [kind_ref[h, rows[q], :] for q in range(group)]
        which = [[kind[q], kind[q] + SPECIES] for q in range(group)]
        top = [[None] * 10 for _ in range(group)]
        slope = [None] * group
        for er, rate in enumerate(RATES):
            e, r = er // RADIAL, er % RADIAL
            radial = [r_ref[h, er, rows[q], :] for q in range(group)]
            inner = [None] * group
            for m in range(10):
                g = g_ref[(h * 2 + e) * 10 + m, r // 2 * 8 : r // 2 * 8 + 8, :]
                for q in range(group):
                    pick = jnp.take_along_axis(g, which[q][r % 2], axis=0, mode="promise_in_bounds")
                    if m == 0:
                        inner[q] = pick
                    else:
                        inner[q] = inner[q] + pick * ang[q][m]
                        term = radial[q] * pick
                        top[q][m] = term if er == 0 else top[q][m] + term
            for q in range(group):
                term = (radial[q] * (-rate)) * inner[q]
                slope[q] = term if er == 0 else slope[q] + term
        sums = [None] * 9
        for q in range(group):
            x, y, z = o[q]
            t = top[q]
            gx = t[1] + 2.0 * x * (t[4] + slope[q]) + t[7] * y + t[8] * z
            gy = t[2] + 2.0 * y * (t[5] + slope[q]) + t[7] * x + t[9] * z
            gz = t[3] + 2.0 * z * (t[6] + slope[q]) + t[8] * x + t[9] * y
            g = [gx, gy, gz]
            terms = [-v for v in g] + [-0.5 * o[q][a] * g[c] for a, c in PAIRS]
            for c in range(9):
                t_ref[h, along(c * count + (b * group + q) * 8, 8), :] = terms[c]
                sums[c] = terms[c] if q == 0 else sums[c] + terms[c]
        for c in range(9):
            own_ref[h, c * 8 : c * 8 + 8, :] += -sums[c] if c < 3 else sums[c]
        return 0

    lax.fori_loop(0, halves * blocks, step, 0)


def scatter(nb_ref, hot_ref, t_ref, tot_ref, picks, unroll=32):
    count, own = nb_ref.shape
    halves = own // LANES
    per = LANES // LOW
    groups = [table * per + g for table in picks.values() for g in range(per)]
    row = lax.broadcasted_iota(jnp.int32, (8, own), 0)
    listed = jnp.full((8, own), -1, jnp.int32)
    for k, group in enumerate(groups):
        listed = jnp.where(row == k, group, listed)

    def step(i, total):
        left, right = [], []
        for u in range(unroll):
            n = i * unroll + u
            index = nb_ref[pl.ds(n, 1), :]
            high = jnp.broadcast_to(index // LOW, (8, own))
            eight = jnp.concatenate([t_ref[h, pl.ds(n, 8, stride=count), :] for h in range(halves)], axis=1)
            ninth = jnp.concatenate([t_ref[h, pl.ds(8 * count + n, 1), :] for h in range(halves)], axis=1)
            masked = [jnp.where(high == group, eight, 0.0) for group in groups]
            masked += [jnp.where(high == listed, ninth, 0.0), jnp.zeros((8, own), F32)]
            left.append(jnp.concatenate(masked, axis=0).astype(BF16))
            right.append(hot_ref[n])
        return total + lax.dot_general(
            jnp.concatenate(left, axis=1), jnp.concatenate(right, axis=1), NT, preferred_element_type=F32
        )

    size = len(groups) * 8
    total = lax.fori_loop(0, count // unroll, step, jnp.zeros((size + 16, LOW), F32))
    row = lax.broadcasted_iota(jnp.int32, (8, LANES), 0)
    for k, t in enumerate(picks):
        tot_ref[t * 16 : t * 16 + 8, :] = jnp.concatenate(
            [total[(k * per + g) * 8 : (k * per + g + 1) * 8] for g in range(per)], axis=1
        )
        last = jnp.concatenate([total[size + k * per + g : size + k * per + g + 1] for g in range(per)], axis=1)
        tot_ref[t * 16 + 8 : t * 16 + 16, :] = jnp.where(row == 0, last, 0.0)


def own_terms(own_ref, row_ref, h):
    mine = own_ref[h, pl.ds(0, 16, stride=8), :]
    for j in range(1, 8):
        mine = mine + own_ref[h, pl.ds(j, 16, stride=8), :]
    row = lax.broadcasted_iota(jnp.int32, (16, LANES), 0)
    energies = 0.5 * lax.dot_general(
        jnp.ones((8, LANES), F32),
        row_ref[h * LANES : (h + 1) * LANES, :],
        NT,
        precision=lax.Precision.HIGHEST,
        preferred_element_type=F32,
    )
    return jnp.where(row == 9, energies[0:1], mine)


def one_hots(nb_ref, hot_ref):
    count, own = nb_ref.shape
    slot = lax.broadcasted_iota(jnp.int32, (LOW, own), 0)

    def step(n, _):
        low = nb_ref[pl.ds(n, 1), :] & (LOW - 1)
        hot_ref[n] = jnp.where(slot == low, 1.0, 0.0).astype(BF16)
        return 0

    lax.fori_loop(0, count, step, 0, unroll=4)


def identities(plain_ref, eye_ref):
    size = K * K
    row = lax.broadcasted_iota(jnp.int32, (size, size), 0)
    col = lax.broadcasted_iota(jnp.int32, (size, size), 1)
    plain_ref[...] = jnp.where(row[:LANES, :LANES] == col[:LANES, :LANES], 1.0, 0.0).astype(BF16)
    outer = row // K
    inner = row % SPECIES * RADIAL + row % K // SPECIES
    eye_ref[:size, :] = jnp.where(outer * K + inner == col, 1.0, 0.0).astype(BF16)
    eye_ref[size:, :] = jnp.where(inner * K + outer == col, 1.0, 0.0).astype(BF16)


def scratch_shapes(own, count, width, sparse, depth, rank):
    halves = own // LANES
    return dict(
        off=pltpu.VMEM((halves, 3, count, LANES), F32),
        pick=pltpu.VMEM((halves, 4, count, LANES), F32),
        plain=pltpu.VMEM((LANES, LANES), BF16),
        w=pltpu.VMEM((halves, SPECIES - 1, count, LANES), F32),
        kind=pltpu.VMEM((halves, count, LANES), jnp.int32),
        r=pltpu.VMEM((halves, len(RATES), count, LANES), F32),
        acc=pltpu.VMEM((halves * 20, K * 8, LANES), F32),
        m=pltpu.VMEM((halves * 20, K, LANES), F32),
        mc=pltpu.VMEM((halves * 20, K, LANES), F32),
        d=pltpu.VMEM((halves, depth, LANES), F32),
        rinv=pltpu.VMEM((halves, 8, LANES), F32),
        desc=pltpu.VMEM((own, depth), BF16),
        eye=pltpu.VMEM((2 * K * K, K * K), BF16),
        scale=pltpu.VMEM((8, sparse), F32),
        grad=pltpu.VMEM((own, depth), F32),
        row=pltpu.VMEM((own, LANES), F32),
        kernel=pltpu.VMEM((own, sparse), BF16),
        gd=pltpu.VMEM((own, depth), BF16),
        gt=pltpu.VMEM((halves, 3, 2 * K * K, LANES), F32),
        g=pltpu.VMEM((halves * 20, K, LANES), F32),
        t=pltpu.VMEM((halves, 9 * count, LANES), F32),
        own=pltpu.VMEM((halves, 16 * 8, LANES), F32),
        hot=pltpu.VMEM((count, LOW, own), BF16),
    )


MESH = pl.DeviceIdType.MESH


def remote(source, target, sems, slot, device):
    return pltpu.make_async_remote_copy(
        src_ref=source,
        dst_ref=target,
        send_sem=sems.at[(0, *slot)],
        recv_sem=sems.at[(1, *slot)],
        device_id=device,
        device_id_type=MESH,
    )


class Place:
    def __init__(self):
        self.brick, self.part = lax.axis_index("space"), lax.axis_index("sparse")
        bricks, self.parts = lax.axis_size("space"), lax.axis_size("sparse")
        self.odd = lax.rem(self.brick, 2)
        self.mate = self.brick + 1 - 2 * self.odd
        self.exists = (self.brick > 0) & (self.brick < bricks - 1)
        self.cross = jnp.where(self.exists, self.brick - 1 + 2 * self.odd, self.mate)
        self.others = [lax.rem(self.part + j, self.parts) for j in range(self.parts)]

    def greet(self):
        barrier = pltpu.get_barrier_semaphore()

        def signal(device):
            pl.semaphore_signal(barrier, inc=1, device_id=device, device_id_type=MESH)

        @pl.when(self.exists)
        def _():
            signal((self.cross, self.part))

        signal((self.mate, self.part))
        for other in self.others[1:]:
            signal((self.brick, other))

    def met(self):
        barrier = pltpu.get_barrier_semaphore()
        pl.semaphore_wait(barrier, jnp.where(self.exists, self.parts + 1, self.parts))

    def tell(self, semaphore):
        for other in self.others[1:]:
            pl.semaphore_signal(semaphore, inc=1, device_id=(self.brick, other), device_id_type=MESH)

    def told(self, semaphore):
        pl.semaphore_wait(semaphore, self.parts - 1)


def halo_pick(pos_ref, species_ref, send_refs, table_ref, face_ref):
    own = pos_ref.shape[1]
    table_ref[0:3, :own] = pos_ref[...]
    table_ref[3:4, :own] = species_ref[...].astype(F32)
    table_ref[4:8, :own] = jnp.zeros((4, own), F32)
    for f, send_ref in enumerate(send_refs):
        index = jnp.broadcast_to(send_ref[...], (8, LANES))
        low, high = index & (LANES - 1), index // LANES
        value = None
        for t in range(own // LANES):
            part = jnp.take_along_axis(
                table_ref[:, t * LANES : (t + 1) * LANES], low, axis=1, mode="promise_in_bounds"
            )
            value = part if value is None else jnp.where(high == t, part, value)
        face_ref[f] = value


def halo_place(rim_ref, table_ref, own, odd):
    mate, cross = rim_ref[0], rim_ref[1]
    table_ref[:, own : own + LANES] = jnp.where(odd == 1, mate, cross)
    table_ref[:, own + LANES : own + 2 * LANES] = jnp.where(odd == 1, cross, mate)


def deliver(ghosts, slots):
    high = ghosts.astype(BF16)
    low = (ghosts - high.astype(F32)).astype(BF16)
    both = lax.dot_general(jnp.concatenate([high, low], axis=0), slots, NT, preferred_element_type=F32)
    return both[:16] + both[16:]


def slots_of(send, first, count):
    slot = first + lax.broadcasted_iota(jnp.int32, (count, LANES), 0)
    return jnp.where(slot == send, 1.0, 0.0).astype(BF16)


def brick(pos, species, nb, mask, send_lo, send_hi, sparse, alpha, factor, parts):
    own, count = pos.shape[1], nb.shape[0]
    depth, rank = sparse.shape[1], factor.shape[1]
    halves = own // LANES
    tables = halves + 2
    share = own // parts
    names = scratch_shapes(own, count, tables * LANES, sparse.shape[0], depth, rank)
    inputs = (pos, species, send_lo, send_hi, nb, mask, alpha, sparse, factor)
    names.update(
        table=pltpu.VMEM((8, tables * LANES), F32),
        face=pltpu.VMEM((2, 8, LANES), F32),
        rim=pltpu.VMEM((2, 8, LANES), F32),
        tot=pltpu.VMEM((tables * 16, LANES), F32),
        vec_out=pltpu.VMEM((own, rank), BF16),
        vec_in=pltpu.VMEM((parts, share, rank), BF16),
        tot_out=pltpu.VMEM((halves, 16, LANES), BF16),
        tot_in=pltpu.VMEM((parts, 16, LANES), BF16),
        relay_out=pltpu.VMEM((16, LANES), F32),
        relay_in=pltpu.VMEM((16, LANES), F32),
        cross_out=pltpu.VMEM((16, LANES), BF16),
        cross_in=pltpu.VMEM((parts, 16, LANES), BF16),
        halo_sems=pltpu.SemaphoreType.DMA((2, 2)),
        relay_sems=pltpu.SemaphoreType.DMA((2, 1)),
        vec_sems=pltpu.SemaphoreType.DMA((2, parts)),
        tot_sems=pltpu.SemaphoreType.DMA((2, parts)),
        cross_sems=pltpu.SemaphoreType.DMA((2, parts)),
        ready=pltpu.SemaphoreType.REGULAR,
        load_sems=pltpu.SemaphoreType.DMA((len(inputs),)),
    )
    keys = list(names)
    local = [pltpu.VMEM(x.shape, x.dtype) for x in inputs]

    def kernel(*refs):
        sources, out_ref = refs[: len(inputs)], refs[len(inputs)]
        held = refs[len(inputs) + 1 : 2 * len(inputs) + 1]
        s = dict(zip(keys, refs[2 * len(inputs) + 1 :]))
        pos_ref, species_ref, lo_ref, hi_ref, nb_ref, mask_ref, alpha_ref, sparse_ref, factor_ref = held
        place = Place()
        place.greet()
        loads = [
            pltpu.make_async_copy(x, y, s["load_sems"].at[k])
            for k, (x, y) in enumerate(zip(sources, held))
        ]
        for load in loads:
            load.start()
        for load in loads[:4]:
            load.wait()
        halo_pick(pos_ref, species_ref, (lo_ref, hi_ref), s["table"], s["face"])
        place.met()
        near = remote(s["face"].at[1 - place.odd], s["rim"].at[0], s["halo_sems"], (0,), (place.mate, place.part))
        far = remote(s["face"].at[place.odd], s["rim"].at[1], s["halo_sems"], (1,), (place.cross, place.part))

        @pl.when(place.exists)
        def _():
            far.start()

        near.start()
        place.tell(s["ready"])

        @pl.when(jnp.logical_not(place.exists))
        def _():
            s["rim"][1] = jnp.zeros((8, LANES), F32)
            for j in range(parts):
                s["cross_in"][j] = jnp.zeros((16, LANES), BF16)

        identities(s["plain"], s["eye"])
        for load in loads[4:]:
            load.wait()
        norms(sparse_ref, alpha_ref, s["scale"], 0, sparse.shape[0] // 512)
        own_setup(s["table"], nb_ref, s["pick"])
        one_hots(nb_ref, s["hot"])
        near.wait()

        @pl.when(place.exists)
        def _():
            far.wait()

        halo_place(s["rim"], s["table"], own, place.odd)
        live_row = jnp.broadcast_to(jnp.sum(mask_ref[0:1, :], axis=1, keepdims=True), (8, LANES))
        pair_setup(
            s["table"], pos_ref, nb_ref, mask_ref, live_row, s["pick"], s["off"], s["w"], s["kind"], s["r"]
        )
        moments(s["off"], s["w"], s["r"], s["acc"], s["m"], s["mc"])
        descriptors(s["m"], s["mc"], s["d"], s["rinv"], s["desc"], s["plain"])
        kernel_sums(s["desc"], sparse_ref, s["scale"], s["grad"], s["kernel"], s["row"])
        moment_grads(s["grad"], s["desc"], s["eye"], s["gd"], s["gt"], s["mc"], s["rinv"], s["g"])
        pair_terms(s["off"], s["kind"], s["r"], s["g"], s["t"], s["own"])
        scatter(nb_ref, s["hot"], s["t"], s["tot"], {halves + 1: halves + place.odd, halves: halves + 1 - place.odd})
        s["cross_out"][...] = s["tot"][(halves + 1) * 16 :, :].astype(BF16)
        crossing = [
            remote(s["cross_out"], s["cross_in"].at[j], s["cross_sems"], (j,), (place.cross, other))
            for j, other in enumerate(place.others)
        ]

        place.told(s["ready"])

        @pl.when(place.exists)
        def _():
            for j in sorted(range(parts), key=lambda j: -min(j, parts - j)):
                crossing[j].start()

        s["relay_out"][...] = s["tot"][halves * 16 : (halves + 1) * 16, :]
        relay = remote(s["relay_out"], s["relay_in"], s["relay_sems"], (0,), (place.mate, place.part))
        relay.start()
        scatter(nb_ref, s["hot"], s["t"], s["tot"], {h: h for h in range(halves)})
        s["vec_out"][...] = jnp.dot(s["kernel"][...], factor_ref[...], preferred_element_type=F32).astype(BF16)
        vectors = [
            remote(
                s["vec_out"].at[pl.ds(pl.multiple_of(other * share, share), share)],
                s["vec_in"].at[j],
                s["vec_sems"],
                (j,),
                (place.brick, other),
            )
            for j, other in enumerate(place.others)
            if j
        ]
        for copy in vectors:
            copy.start()
        odd = place.odd == 1
        near_send = jnp.where(odd, lo_ref[...], hi_ref[...])
        far_send = jnp.where(odd, hi_ref[...], lo_ref[...])
        near_slots = slots_of(near_send, 0, own)
        mine = [s["tot"][h * 16 : (h + 1) * 16, :] + own_terms(s["own"], s["row"], h) for h in range(halves)]
        relay.wait()
        near_part = deliver(s["relay_in"][...], near_slots)
        for h in range(halves):
            s["tot_out"][h] = (
                mine[h] + near_part[:, h * LANES : (h + 1) * LANES]
            ).astype(BF16)
        totals = [
            remote(
                s["tot_out"].at[other * share // LANES], s["tot_in"].at[j], s["tot_sems"], (j,), (place.brick, other)
            )
            for j, other in enumerate(place.others)
            if j
        ]
        for copy in totals:
            copy.start()
        vec = s["vec_out"][pl.ds(pl.multiple_of(place.part * share, share), share), :].astype(F32)
        for copy in vectors:
            copy.wait()
        for j in range(1, parts):
            vec = vec + s["vec_in"][j].astype(F32)
        variances = lax.dot_general(
            jnp.ones((16, rank), F32), vec * vec, NT, precision=lax.Precision.HIGHEST, preferred_element_type=F32
        )
        half = place.part * share // LANES
        far_slots = slots_of(far_send, half * LANES, LANES)
        mine = s["tot_out"][half].astype(F32)
        for copy in totals:
            copy.wait()
        for j in range(1, parts):
            mine = mine + s["tot_in"][j].astype(F32)

        @pl.when(place.exists)
        def _():
            for copy in crossing:
                copy.wait()

        ghosts = s["cross_in"][0].astype(F32)
        for j in range(1, parts):
            ghosts = ghosts + s["cross_in"][j].astype(F32)
        mine = mine + deliver(ghosts, far_slots)
        shift = lax.rem(LANES - lax.rem(place.part * share, LANES), LANES)
        out_ref[...] = pltpu.roll(mine, shift, 1)
        out_ref[10:11, :share] = variances[10:11]

    anywhere = pl.BlockSpec(memory_space=pltpu.HBM)
    return pl.pallas_call(
        kernel,
        out_shape=jax.ShapeDtypeStruct((16, LANES), F32),
        in_specs=[anywhere] * len(inputs),
        out_specs=pl.BlockSpec(memory_space=pltpu.VMEM),
        scratch_shapes=local + list(names.values()),
        compiler_params=pltpu.CompilerParams(
            vmem_limit_bytes=60 * 1024 * 1024, collective_id=0, has_side_effects=True
        ),
        name="brick",
    )(*inputs)


def split(result, share):
    def kernel(result_ref, force_ref, energy_ref, variance_ref, virial_ref):
        force_ref[...] = result_ref[0:3, :share]
        virial_ref[...] = result_ref[3:9, :share]
        energy_ref[...] = result_ref[9:10, :share]
        variance_ref[...] = result_ref[10:11, :share]

    vmem = pl.BlockSpec(memory_space=pltpu.VMEM)
    return pl.pallas_call(
        kernel,
        out_shape=tuple(jax.ShapeDtypeStruct((n, share), F32) for n in (3, 1, 1, 6)),
        in_specs=[vmem],
        out_specs=(vmem,) * 4,
        name="split",
    )(result)


def shards(
    positions, species, live_count, neighbors, neighbor_mask, send_lo, send_hi, sparse_desc, alpha, var_factor
):
    parts = lax.axis_size("sparse")
    result = brick(
        positions,
        species[None],
        neighbors,
        neighbor_mask,
        send_lo[None],
        send_hi[None],
        sparse_desc,
        alpha.reshape(-1, LANES),
        var_factor,
        parts,
    )
    forces, energies, variances, virials = split(result, positions.shape[1] // parts)
    return forces, energies[0], variances[0], virials


def solution(mesh):
    return jax.shard_map(
        shards,
        mesh=mesh,
        in_specs=(
            P(None, "space"),
            P("space"),
            P("space"),
            P(None, "space"),
            P(None, "space"),
            P("space"),
            P("space"),
            P("sparse", None),
            P("sparse"),
            P("sparse", None),
        ),
        out_specs=(
            P(None, ("space", "sparse")),
            P(("space", "sparse")),
            P(("space", "sparse")),
            P(None, ("space", "sparse")),
        ),
        check_vma=False,
    )
```

```python
import jax
import jax.numpy as jnp
from jax import lax
from jax.experimental import pallas as pl
from jax.experimental.pallas import tpu as pltpu
from jax.sharding import PartitionSpec as P

EPS = 1e-6
F32, BF16 = jnp.float32, jnp.bfloat16
SPECIES, RADIAL = 4, 4
K = SPECIES * RADIAL
LANES = 128
LOW = 64
RATES = tuple(scale * 2.0**r for scale in (0.1, 0.15) for r in range(RADIAL))
ORDERS = ((0, 1), (1, 4), (4, 10))
FOLD = (1.0,) * 7 + (2.0,) * 3
PAIRS = ((0, 0), (1, 1), (2, 2), (0, 1), (0, 2), (1, 2))
NT = (((1,), (1,)), ((), ()))


def angular(radial, o):
    first = [radial * o[p] for p in range(3)]
    return [radial] + first + [first[a] * o[b] for a, b in PAIRS]


def along(start, size):
    return pl.ds(pl.multiple_of(start, size), size)


def norms(sparse_ref, alpha_ref, scale_ref, first, last, chunk=512):
    depth = sparse_ref.shape[1]
    ones = jnp.ones((8, LANES), BF16)
    row = lax.broadcasted_iota(jnp.int32, (8, chunk), 0)
    per = chunk // LANES
    for t in range(first, last):
        raw = sparse_ref[t * chunk : (t + 1) * chunk, :]
        parts = [raw[:, j * LANES : (j + 1) * LANES] for j in range(depth // LANES)]
        parts = [part * part for part in parts]
        while len(parts) > 1:
            parts = [x + y for x, y in zip(parts[::2], parts[1::2])] + parts[len(parts) // 2 * 2 :]
        squares = lax.dot_general(ones, parts[0], NT, preferred_element_type=F32)
        inverse = 1.0 / (squares + EPS)
        alpha = jnp.concatenate([alpha_ref[t * per + j : t * per + j + 1, :] for j in range(per)], axis=1)
        scale_ref[:, t * chunk : (t + 1) * chunk] = inverse * jnp.where(row == 0, 1.0, 2.0 * alpha)


def pick_from(table_ref, first, last, low, high, value, rows):
    picked = []
    for c in range(4):
        got = value[c]
        for t in range(first, last):
            source = jnp.broadcast_to(table_ref[c : c + 1, t * LANES : (t + 1) * LANES], (rows, LANES))
            part = jnp.take_along_axis(source, low, axis=1, mode="promise_in_bounds")
            got = part if got is None else jnp.where(high == t, part, got)
        picked.append(got)
    return picked


def own_setup(table_ref, nb_ref, pick_ref):
    halves, _, count, _ = pick_ref.shape
    blocks = count // 8

    def step(i, _):
        h, b = i // blocks, i % blocks
        rows = along(b * 8, 8)
        index = nb_ref[rows, along(h * LANES, LANES)]
        values = pick_from(table_ref, 0, halves, index & (LANES - 1), index // LANES, [None] * 4, 8)
        for c in range(4):
            pick_ref[h, c, rows, :] = values[c]
        return 0

    lax.fori_loop(0, halves * blocks, step, 0, unroll=8)


def pair_setup(table_ref, pos_ref, nb_ref, mask_ref, live, pick_ref, off_ref, w_ref, kind_ref, r_ref):
    own = pos_ref.shape[1]
    halves = own // LANES
    tables = table_ref.shape[1] // LANES
    blocks = nb_ref.shape[0] // 8
    lane = lax.broadcasted_iota(jnp.int32, (8, LANES), 1)

    def step(i, _):
        h, b = i // blocks, i % blocks
        rows, cols = along(b * 8, 8), along(h * LANES, LANES)
        index = nb_ref[rows, cols]
        held = [pick_ref[h, c, rows, :] for c in range(4)]
        picked = pick_from(table_ref, halves, tables, index & (LANES - 1), index // LANES, held, 8)
        o = [picked[p] - pos_ref[p : p + 1, cols] for p in range(3)]
        alive = ((index >= own) | (index < live)) & (h * LANES + lane < live)
        valid = jnp.where(alive, mask_ref[rows, cols].astype(F32), 0.0)
        for p in range(3):
            off_ref[h, p, rows, :] = o[p]
        for s in range(SPECIES - 1):
            w_ref[h, s, rows, :] = jnp.where(picked[3] == s, 1.0, 0.0)
        kind_ref[h, rows, :] = picked[3].astype(jnp.int32)
        square = o[0] * o[0] + o[1] * o[1] + o[2] * o[2]
        for e in range(2):
            radial = jnp.exp(square * (-RATES[e * RADIAL]))
            for r in range(RADIAL):
                if r:
                    radial = radial * radial
                r_ref[h, e * RADIAL + r, rows, :] = radial * valid
        return 0

    lax.fori_loop(0, halves * blocks, step, 0, unroll=8)


def moments(off_ref, w_ref, r_ref, acc_ref, m_ref, mc_ref):
    halves, _, count, _ = off_ref.shape

    def fold(i, ms):
        for m in ms:
            value = acc_ref[i * 10 + m, pl.ds(0, K, stride=8), :]
            for j in range(1, 8):
                value = value + acc_ref[i * 10 + m, pl.ds(j, K, stride=8), :]
            m_ref[i * 10 + m] = value
            mc_ref[i * 10 + m] = value * FOLD[m]

    def step(i, before):
        h, e = i // 2, i % 2
        for r in range(RADIAL):
            total = [[None] * 10 for _ in range(SPECIES)]
            for b in range(count // 8):
                rows = slice(b * 8, b * 8 + 8)
                v = angular(r_ref[h, e * RADIAL + r, rows, :], [off_ref[h, p, rows, :] for p in range(3)])
                for s in range(SPECIES):
                    weight = w_ref[h, s, rows, :] if s < SPECIES - 1 else None
                    for m in range(10):
                        term = v[m] if weight is None else weight * v[m]
                        total[s][m] = term if b == 0 else total[s][m] + term
            if before is not None:
                fold(before, range(r * 10 // RADIAL, (r + 1) * 10 // RADIAL))
            for m in range(10):
                total[3][m] = total[3][m] - (total[0][m] + total[1][m] + total[2][m])
                for s in range(SPECIES):
                    acc_ref[i * 10 + m, (s * RADIAL + r) * 8 : (s * RADIAL + r) * 8 + 8, :] = total[s][m]

    for i in range(halves * 2):
        step(i, i - 1 if i else None)
    fold(halves * 2 - 1, range(10))


def descriptors(m_ref, mc_ref, d_ref, rinv_ref, desc_ref, plain_ref):
    halves = d_ref.shape[0]

    def step(k, squares):
        fresh = []
        for h in range(halves):
            base = h * 20
            total = squares[h]
            for l, (start, stop) in enumerate(ORDERS):
                value = None
                for m in range(start, stop):
                    term = m_ref[base + m, pl.ds(k, 1), :] * mc_ref[base + 10 + m]
                    value = term if value is None else value + term
                d_ref[h, along(l * K * K + k * K, K), :] = value
                total = total + value * value
            fresh.append(total)
        return tuple(fresh)

    squares = lax.fori_loop(0, K, step, (jnp.zeros((K, LANES), F32),) * halves, unroll=16)
    for h in range(halves):
        rinv = lax.rsqrt(jnp.sum(squares[h], axis=0, keepdims=True) + EPS)
        rinv_ref[h] = jnp.broadcast_to(rinv, (8, LANES))
        unit = (d_ref[h] * rinv).astype(BF16)
        desc_ref[h * LANES : (h + 1) * LANES, :] = lax.dot_general(
            plain_ref[...], unit, NT, preferred_element_type=F32
        ).astype(BF16)


def kernel_sums(desc_ref, sparse_ref, scale_ref, grad_ref, kernel_ref, row_ref):
    raw = sparse_ref[...]
    projection = lax.dot_general(desc_ref[...], raw, NT, preferred_element_type=F32)
    coefficient = projection * scale_ref[1:2, :]
    kernel = (projection * projection * scale_ref[0:1, :]).astype(BF16)
    energy_terms = coefficient * projection
    energy = energy_terms[:, :LANES]
    for j in range(1, raw.shape[0] // LANES):
        energy = energy + energy_terms[:, j * LANES : (j + 1) * LANES]
    grad_ref[...] = jnp.dot(coefficient.astype(BF16), raw, preferred_element_type=F32)
    kernel_ref[...] = kernel
    row_ref[...] = energy


def moment_grads(grad_ref, desc_ref, eye_ref, gd_ref, gt_ref, mc_ref, rinv_ref, g_ref):
    halves = gt_ref.shape[0]
    unit = desc_ref[...].astype(F32)
    grad = grad_ref[...]
    along_unit = jnp.sum(grad * unit, axis=1, keepdims=True)
    gd_ref[...] = (grad - unit * along_unit).astype(BF16)
    for l in range(3):
        turned = lax.dot_general(
            eye_ref[...], gd_ref[:, l * K * K : (l + 1) * K * K], NT, preferred_element_type=F32
        )
        for h in range(halves):
            gt_ref[h, l] = turned[:, h * LANES : (h + 1) * LANES]

    def step(i, _):
        h, e = i // 2, i % 2
        rinv = rinv_ref[h, 0:1, :]
        for l, (start, stop) in enumerate(ORDERS):
            total = [None] * 10
            for j in range(K):
                block = gt_ref[h, l, along((1 - e) * K * K + j * K, K), :]
                for m in range(start, stop):
                    term = block * mc_ref[h * 20 + (1 - e) * 10 + m, j : j + 1, :]
                    total[m] = term if j == 0 else total[m] + term
            for m in range(start, stop):
                g_ref[i * 10 + m] = total[m] * rinv
        return 0

    lax.fori_loop(0, halves * 2, step, 0, unroll=2)


def pair_terms(off_ref, kind_ref, r_ref, g_ref, t_ref, own_ref, group=2):
    halves, _, count, _ = off_ref.shape
    blocks = count // 8 // group
    own_ref[...] = jnp.zeros(own_ref.shape, F32)

    def step(i, _):
        h, b = i // blocks, i % blocks
        rows = [along((b * group + q) * 8, 8) for q in range(group)]
        o = [[off_ref[h, p, rows[q], :] for p in range(3)] for q in range(group)]
        ang = [[None] + o[q] + [o[q][x] * o[q][y] for x, y in PAIRS] for q in range(group)]
        kind = [kind_ref[h, rows[q], :] for q in range(group)]
        which = [[kind[q], kind[q] + SPECIES] for q in range(group)]
        top = [[None] * 10 for _ in range(group)]
        slope = [None] * group
        for er, rate in enumerate(RATES):
            e, r = er // RADIAL, er % RADIAL
            radial = [r_ref[h, er, rows[q], :] for q in range(group)]
            inner = [None] * group
            for m in range(10):
                g = g_ref[(h * 2 + e) * 10 + m, r // 2 * 8 : r // 2 * 8 + 8, :]
                for q in range(group):
                    pick = jnp.take_along_axis(g, which[q][r % 2], axis=0, mode="promise_in_bounds")
                    if m == 0:
                        inner[q] = pick
                    else:
                        inner[q] = inner[q] + pick * ang[q][m]
                        term = radial[q] * pick
                        top[q][m] = term if er == 0 else top[q][m] + term
            for q in range(group):
                term = (radial[q] * (-rate)) * inner[q]
                slope[q] = term if er == 0 else slope[q] + term
        sums = [None] * 9
        for q in range(group):
            x, y, z = o[q]
            t = top[q]
            gx = t[1] + 2.0 * x * (t[4] + slope[q]) + t[7] * y + t[8] * z
            gy = t[2] + 2.0 * y * (t[5] + slope[q]) + t[7] * x + t[9] * z
            gz = t[3] + 2.0 * z * (t[6] + slope[q]) + t[8] * x + t[9] * y
            g = [gx, gy, gz]
            terms = [-v for v in g] + [-0.5 * o[q][a] * g[c] for a, c in PAIRS]
            for c in range(9):
                t_ref[h, along(c * count + (b * group + q) * 8, 8), :] = terms[c]
                sums[c] = terms[c] if q == 0 else sums[c] + terms[c]
        for c in range(9):
            own_ref[h, c * 8 : c * 8 + 8, :] += -sums[c] if c < 3 else sums[c]
        return 0

    lax.fori_loop(0, halves * blocks, step, 0)


def scatter(nb_ref, hot_ref, t_ref, tot_ref, picks, unroll=32):
    count, own = nb_ref.shape
    halves = own // LANES
    per = LANES // LOW
    groups = [table * per + g for table in picks.values() for g in range(per)]
    row = lax.broadcasted_iota(jnp.int32, (8, own), 0)
    listed = jnp.full((8, own), -1, jnp.int32)
    for k, group in enumerate(groups):
        listed = jnp.where(row == k, group, listed)

    def step(i, total):
        left, right = [], []
        for u in range(unroll):
            n = i * unroll + u
            index = nb_ref[pl.ds(n, 1), :]
            high = jnp.broadcast_to(index // LOW, (8, own))
            eight = jnp.concatenate([t_ref[h, pl.ds(n, 8, stride=count), :] for h in range(halves)], axis=1)
            ninth = jnp.concatenate([t_ref[h, pl.ds(8 * count + n, 1), :] for h in range(halves)], axis=1)
            masked = [jnp.where(high == group, eight, 0.0) for group in groups]
            masked += [jnp.where(high == listed, ninth, 0.0), jnp.zeros((8, own), F32)]
            left.append(jnp.concatenate(masked, axis=0).astype(BF16))
            right.append(hot_ref[n])
        return total + lax.dot_general(
            jnp.concatenate(left, axis=1), jnp.concatenate(right, axis=1), NT, preferred_element_type=F32
        )

    size = len(groups) * 8
    total = lax.fori_loop(0, count // unroll, step, jnp.zeros((size + 16, LOW), F32))
    row = lax.broadcasted_iota(jnp.int32, (8, LANES), 0)
    for k, t in enumerate(picks):
        tot_ref[t * 16 : t * 16 + 8, :] = jnp.concatenate(
            [total[(k * per + g) * 8 : (k * per + g + 1) * 8] for g in range(per)], axis=1
        )
        last = jnp.concatenate([total[size + k * per + g : size + k * per + g + 1] for g in range(per)], axis=1)
        tot_ref[t * 16 + 8 : t * 16 + 16, :] = jnp.where(row == 0, last, 0.0)


def own_terms(own_ref, row_ref, h):
    mine = own_ref[h, pl.ds(0, 16, stride=8), :]
    for j in range(1, 8):
        mine = mine + own_ref[h, pl.ds(j, 16, stride=8), :]
    row = lax.broadcasted_iota(jnp.int32, (16, LANES), 0)
    energies = 0.5 * lax.dot_general(
        jnp.ones((8, LANES), F32),
        row_ref[h * LANES : (h + 1) * LANES, :],
        NT,
        precision=lax.Precision.HIGHEST,
        preferred_element_type=F32,
    )
    return jnp.where(row == 9, energies[0:1], mine)


def one_hots(nb_ref, hot_ref):
    count, own = nb_ref.shape
    slot = lax.broadcasted_iota(jnp.int32, (LOW, own), 0)

    def step(n, _):
        low = nb_ref[pl.ds(n, 1), :] & (LOW - 1)
        hot_ref[n] = jnp.where(slot == low, 1.0, 0.0).astype(BF16)
        return 0

    lax.fori_loop(0, count, step, 0, unroll=4)


def identities(plain_ref, eye_ref):
    size = K * K
    row = lax.broadcasted_iota(jnp.int32, (size, size), 0)
    col = lax.broadcasted_iota(jnp.int32, (size, size), 1)
    plain_ref[...] = jnp.where(row[:LANES, :LANES] == col[:LANES, :LANES], 1.0, 0.0).astype(BF16)
    outer = row // K
    inner = row % SPECIES * RADIAL + row % K // SPECIES
    eye_ref[:size, :] = jnp.where(outer * K + inner == col, 1.0, 0.0).astype(BF16)
    eye_ref[size:, :] = jnp.where(inner * K + outer == col, 1.0, 0.0).astype(BF16)


def scratch_shapes(own, count, width, sparse, depth, rank):
    halves = own // LANES
    return dict(
        off=pltpu.VMEM((halves, 3, count, LANES), F32),
        pick=pltpu.VMEM((halves, 4, count, LANES), F32),
        plain=pltpu.VMEM((LANES, LANES), BF16),
        w=pltpu.VMEM((halves, SPECIES - 1, count, LANES), F32),
        kind=pltpu.VMEM((halves, count, LANES), jnp.int32),
        r=pltpu.VMEM((halves, len(RATES), count, LANES), F32),
        acc=pltpu.VMEM((halves * 20, K * 8 + 8, LANES), F32),
        m=pltpu.VMEM((halves * 20, K, LANES), F32),
        mc=pltpu.VMEM((halves * 20, K, LANES), F32),
        d=pltpu.VMEM((halves, depth, LANES), F32),
        rinv=pltpu.VMEM((halves, 8, LANES), F32),
        desc=pltpu.VMEM((own, depth), BF16),
        eye=pltpu.VMEM((2 * K * K, K * K), BF16),
        scale=pltpu.VMEM((8, sparse), F32),
        grad=pltpu.VMEM((own, depth), F32),
        row=pltpu.VMEM((own, LANES), F32),
        kernel=pltpu.VMEM((own, sparse), BF16),
        gd=pltpu.VMEM((own, depth), BF16),
        gt=pltpu.VMEM((halves, 3, 2 * K * K, LANES), F32),
        g=pltpu.VMEM((halves * 20, K, LANES), F32),
        t=pltpu.VMEM((halves, 9 * count, LANES), F32),
        own=pltpu.VMEM((halves, 16 * 8 + 8, LANES), F32),
        hot=pltpu.VMEM((count, LOW, own), BF16),
    )


MESH = pl.DeviceIdType.MESH


def remote(source, target, sems, slot, device):
    return pltpu.make_async_remote_copy(
        src_ref=source,
        dst_ref=target,
        send_sem=sems.at[(0, *slot)],
        recv_sem=sems.at[(1, *slot)],
        device_id=device,
        device_id_type=MESH,
    )


class Place:
    def __init__(self):
        self.brick, self.part = lax.axis_index("space"), lax.axis_index("sparse")
        bricks, self.parts = lax.axis_size("space"), lax.axis_size("sparse")
        self.odd = lax.rem(self.brick, 2)
        self.mate = self.brick + 1 - 2 * self.odd
        self.exists = (self.brick > 0) & (self.brick < bricks - 1)
        self.cross = jnp.where(self.exists, self.brick - 1 + 2 * self.odd, self.mate)
        self.others = [lax.rem(self.part + j, self.parts) for j in range(self.parts)]

    def greet(self):
        barrier = pltpu.get_barrier_semaphore()

        def signal(device):
            pl.semaphore_signal(barrier, inc=1, device_id=device, device_id_type=MESH)

        @pl.when(self.exists)
        def _():
            signal((self.cross, self.part))

        signal((self.mate, self.part))
        for other in self.others[1:]:
            signal((self.brick, other))

    def met(self):
        barrier = pltpu.get_barrier_semaphore()
        pl.semaphore_wait(barrier, jnp.where(self.exists, self.parts + 1, self.parts))

    def tell(self, semaphore):
        for other in self.others[1:]:
            pl.semaphore_signal(semaphore, inc=1, device_id=(self.brick, other), device_id_type=MESH)

    def told(self, semaphore):
        pl.semaphore_wait(semaphore, self.parts - 1)


def halo_pick(pos_ref, species_ref, send_refs, table_ref, face_ref):
    own = pos_ref.shape[1]
    table_ref[0:3, :own] = pos_ref[...]
    table_ref[3:4, :own] = species_ref[...].astype(F32)
    table_ref[4:8, :own] = jnp.zeros((4, own), F32)
    for f, send_ref in enumerate(send_refs):
        index = jnp.broadcast_to(send_ref[...], (8, LANES))
        low, high = index & (LANES - 1), index // LANES
        value = None
        for t in range(own // LANES):
            part = jnp.take_along_axis(
                table_ref[:, t * LANES : (t + 1) * LANES], low, axis=1, mode="promise_in_bounds"
            )
            value = part if value is None else jnp.where(high == t, part, value)
        face_ref[f] = value


def halo_place(rim_ref, table_ref, own, odd):
    mate, cross = rim_ref[0], rim_ref[1]
    table_ref[:, own : own + LANES] = jnp.where(odd == 1, mate, cross)
    table_ref[:, own + LANES : own + 2 * LANES] = jnp.where(odd == 1, cross, mate)


def deliver(ghosts, slots):
    high = ghosts.astype(BF16)
    low = (ghosts - high.astype(F32)).astype(BF16)
    both = lax.dot_general(jnp.concatenate([high, low], axis=0), slots, NT, preferred_element_type=F32)
    return both[:16] + both[16:]


def slots_of(send, first, count):
    slot = first + lax.broadcasted_iota(jnp.int32, (count, LANES), 0)
    return jnp.where(slot == send, 1.0, 0.0).astype(BF16)


def brick(pos, species, nb, mask, send_lo, send_hi, sparse, alpha, factor, parts):
    own, count = pos.shape[1], nb.shape[0]
    depth, rank = sparse.shape[1], factor.shape[1]
    halves = own // LANES
    tables = halves + 2
    share = own // parts
    names = scratch_shapes(own, count, tables * LANES, sparse.shape[0], depth, rank)
    inputs = (pos, species, send_lo, send_hi, nb, mask, alpha, sparse, factor)
    names.update(
        table=pltpu.VMEM((8, tables * LANES), F32),
        face=pltpu.VMEM((2, 8, LANES), F32),
        rim=pltpu.VMEM((2, 8, LANES), F32),
        tot=pltpu.VMEM((tables * 16, LANES), F32),
        vec_out=pltpu.VMEM((own, rank), BF16),
        vec_in=pltpu.VMEM((parts, share, rank), BF16),
        tot_out=pltpu.VMEM((halves, 16, LANES), BF16),
        tot_in=pltpu.VMEM((parts, 16, LANES), BF16),
        relay_out=pltpu.VMEM((16, LANES), F32),
        relay_in=pltpu.VMEM((16, LANES), F32),
        cross_out=pltpu.VMEM((16, LANES), BF16),
        cross_in=pltpu.VMEM((parts, 16, LANES), BF16),
        halo_sems=pltpu.SemaphoreType.DMA((2, 2)),
        relay_sems=pltpu.SemaphoreType.DMA((2, 1)),
        vec_sems=pltpu.SemaphoreType.DMA((2, parts)),
        tot_sems=pltpu.SemaphoreType.DMA((2, parts)),
        cross_sems=pltpu.SemaphoreType.DMA((2, parts)),
        ready=pltpu.SemaphoreType.REGULAR,
        load_sems=pltpu.SemaphoreType.DMA((len(inputs),)),
    )
    keys = list(names)
    local = [pltpu.VMEM(x.shape, x.dtype) for x in inputs]

    def kernel(*refs):
        sources, out_ref = refs[: len(inputs)], refs[len(inputs)]
        held = refs[len(inputs) + 1 : 2 * len(inputs) + 1]
        s = dict(zip(keys, refs[2 * len(inputs) + 1 :]))
        pos_ref, species_ref, lo_ref, hi_ref, nb_ref, mask_ref, alpha_ref, sparse_ref, factor_ref = held
        place = Place()
        place.greet()
        loads = [
            pltpu.make_async_copy(x, y, s["load_sems"].at[k])
            for k, (x, y) in enumerate(zip(sources, held))
        ]
        for load in loads:
            load.start()
        for load in loads[:4]:
            load.wait()
        halo_pick(pos_ref, species_ref, (lo_ref, hi_ref), s["table"], s["face"])
        place.met()
        near = remote(s["face"].at[1 - place.odd], s["rim"].at[0], s["halo_sems"], (0,), (place.mate, place.part))
        far = remote(s["face"].at[place.odd], s["rim"].at[1], s["halo_sems"], (1,), (place.cross, place.part))

        @pl.when(place.exists)
        def _():
            far.start()

        near.start()
        place.tell(s["ready"])

        @pl.when(jnp.logical_not(place.exists))
        def _():
            s["rim"][1] = jnp.zeros((8, LANES), F32)
            for j in range(parts):
                s["cross_in"][j] = jnp.zeros((16, LANES), BF16)

        identities(s["plain"], s["eye"])
        for load in loads[4:]:
            load.wait()
        norms(sparse_ref, alpha_ref, s["scale"], 0, sparse.shape[0] // 512)
        own_setup(s["table"], nb_ref, s["pick"])
        one_hots(nb_ref, s["hot"])
        near.wait()

        @pl.when(place.exists)
        def _():
            far.wait()

        halo_place(s["rim"], s["table"], own, place.odd)
        live_row = jnp.broadcast_to(jnp.sum(mask_ref[0:1, :], axis=1, keepdims=True), (8, LANES))
        pair_setup(
            s["table"], pos_ref, nb_ref, mask_ref, live_row, s["pick"], s["off"], s["w"], s["kind"], s["r"]
        )
        moments(s["off"], s["w"], s["r"], s["acc"], s["m"], s["mc"])
        descriptors(s["m"], s["mc"], s["d"], s["rinv"], s["desc"], s["plain"])
        kernel_sums(s["desc"], sparse_ref, s["scale"], s["grad"], s["kernel"], s["row"])
        moment_grads(s["grad"], s["desc"], s["eye"], s["gd"], s["gt"], s["mc"], s["rinv"], s["g"])
        pair_terms(s["off"], s["kind"], s["r"], s["g"], s["t"], s["own"])
        scatter(nb_ref, s["hot"], s["t"], s["tot"], {halves + 1: halves + place.odd, halves: halves + 1 - place.odd})
        s["cross_out"][...] = s["tot"][(halves + 1) * 16 :, :].astype(BF16)
        crossing = [
            remote(s["cross_out"], s["cross_in"].at[j], s["cross_sems"], (j,), (place.cross, other))
            for j, other in enumerate(place.others)
        ]

        place.told(s["ready"])

        @pl.when(place.exists)
        def _():
            for j in sorted(range(parts), key=lambda j: -min(j, parts - j)):
                crossing[j].start()

        s["relay_out"][...] = s["tot"][halves * 16 : (halves + 1) * 16, :]
        relay = remote(s["relay_out"], s["relay_in"], s["relay_sems"], (0,), (place.mate, place.part))
        relay.start()
        scatter(nb_ref, s["hot"], s["t"], s["tot"], {h: h for h in range(halves)})
        s["vec_out"][...] = jnp.dot(s["kernel"][...], factor_ref[...], preferred_element_type=F32).astype(BF16)
        vectors = [
            remote(
                s["vec_out"].at[pl.ds(pl.multiple_of(other * share, share), share)],
                s["vec_in"].at[j],
                s["vec_sems"],
                (j,),
                (place.brick, other),
            )
            for j, other in enumerate(place.others)
            if j
        ]
        for copy in vectors:
            copy.start()
        odd = place.odd == 1
        near_send = jnp.where(odd, lo_ref[...], hi_ref[...])
        far_send = jnp.where(odd, hi_ref[...], lo_ref[...])
        near_slots = slots_of(near_send, 0, own)
        mine = [s["tot"][h * 16 : (h + 1) * 16, :] + own_terms(s["own"], s["row"], h) for h in range(halves)]
        relay.wait()
        near_part = deliver(s["relay_in"][...], near_slots)
        for h in range(halves):
            s["tot_out"][h] = (
                mine[h] + near_part[:, h * LANES : (h + 1) * LANES]
            ).astype(BF16)
        totals = [
            remote(
                s["tot_out"].at[other * share // LANES], s["tot_in"].at[j], s["tot_sems"], (j,), (place.brick, other)
            )
            for j, other in enumerate(place.others)
            if j
        ]
        for copy in totals:
            copy.start()
        vec = s["vec_out"][pl.ds(pl.multiple_of(place.part * share, share), share), :].astype(F32)
        for copy in vectors:
            copy.wait()
        for j in range(1, parts):
            vec = vec + s["vec_in"][j].astype(F32)
        variances = lax.dot_general(
            jnp.ones((16, rank), F32), vec * vec, NT, precision=lax.Precision.HIGHEST, preferred_element_type=F32
        )
        half = place.part * share // LANES
        far_slots = slots_of(far_send, half * LANES, LANES)
        mine = s["tot_out"][half].astype(F32)
        for copy in totals:
            copy.wait()
        for j in range(1, parts):
            mine = mine + s["tot_in"][j].astype(F32)

        @pl.when(place.exists)
        def _():
            for copy in crossing:
                copy.wait()

        ghosts = s["cross_in"][0].astype(F32)
        for j in range(1, parts):
            ghosts = ghosts + s["cross_in"][j].astype(F32)
        mine = mine + deliver(ghosts, far_slots)
        shift = lax.rem(LANES - lax.rem(place.part * share, LANES), LANES)
        out_ref[...] = pltpu.roll(mine, shift, 1)
        out_ref[10:11, :share] = variances[10:11]

    anywhere = pl.BlockSpec(memory_space=pltpu.HBM)
    return pl.pallas_call(
        kernel,
        out_shape=jax.ShapeDtypeStruct((16, LANES), F32),
        in_specs=[anywhere] * len(inputs),
        out_specs=pl.BlockSpec(memory_space=pltpu.VMEM),
        scratch_shapes=local + list(names.values()),
        compiler_params=pltpu.CompilerParams(
            vmem_limit_bytes=60 * 1024 * 1024, collective_id=0, has_side_effects=True
        ),
        name="brick",
    )(*inputs)


def split(result, share):
    def kernel(result_ref, force_ref, energy_ref, variance_ref, virial_ref):
        force_ref[...] = result_ref[0:3, :share]
        virial_ref[...] = result_ref[3:9, :share]
        energy_ref[...] = result_ref[9:10, :share]
        variance_ref[...] = result_ref[10:11, :share]

    vmem = pl.BlockSpec(memory_space=pltpu.VMEM)
    return pl.pallas_call(
        kernel,
        out_shape=tuple(jax.ShapeDtypeStruct((n, share), F32) for n in (3, 1, 1, 6)),
        in_specs=[vmem],
        out_specs=(vmem,) * 4,
        name="split",
    )(result)


def shards(
    positions, species, live_count, neighbors, neighbor_mask, send_lo, send_hi, sparse_desc, alpha, var_factor
):
    parts = lax.axis_size("sparse")
    result = brick(
        positions,
        species[None],
        neighbors,
        neighbor_mask,
        send_lo[None],
        send_hi[None],
        sparse_desc,
        alpha.reshape(-1, LANES),
        var_factor,
        parts,
    )
    forces, energies, variances, virials = split(result, positions.shape[1] // parts)
    return forces, energies[0], variances[0], virials


def solution(mesh):
    return jax.shard_map(
        shards,
        mesh=mesh,
        in_specs=(
            P(None, "space"),
            P("space"),
            P("space"),
            P(None, "space"),
            P(None, "space"),
            P("space"),
            P("space"),
            P("sparse", None),
            P("sparse"),
            P("sparse", None),
        ),
        out_specs=(
            P(None, ("space", "sparse")),
            P(("space", "sparse")),
            P(("space", "sparse")),
            P(None, ("space", "sparse")),
        ),
        check_vma=False,
    )
```
